128 devices in a mesh: row: 4 (over z), kv: 32 (over x, y, core).
Axes of the slice: x: 4, y: 4, z: 4, core: 2. Of those that a mesh axis runs over, the one named last changes fastest.
Arguments:
- hidden: bfloat16 [256, 5120], P(None, 'kv'), may hold values from -6 to 6
- query_weight: bfloat16 [5120, 8192], P('kv', 'row'), may hold values from -0.078125 to 0.078125
- adapter_down_weight: bfloat16 [32, 5120, 16], P(None, 'kv'), may hold values from -0.078125 to 0.078125
- adapter_up_weight: float32 [32, 16, 8192], P(None, None, 'row'), may hold values from -1.5 to 1.5
- query_norm_gain: float32 [128], replicated, may hold values from 0.1 to 1.9
- paged_key_cache: bfloat16 [4096, 128, 8, 128], P('kv', None, 'row'), may hold values from -400 to 400
- paged_value_cache: bfloat16 [4096, 128, 8, 128], P('kv', None, 'row'), may hold values from -6 to 6
- output_weight: bfloat16 [8192, 5120], P('row', 'kv'), may hold values from -0.0625 to 0.0625
- holder: int32 [256, 32], P('kv'), may hold values from 0 to 31, as said below
- holder_block_index: int32 [256, 32], P('kv'), may hold values from 0 to 127
- block_used_length: int32 [256, 32], P('kv'), may hold values from 1 to 128
- tenant: int32 [256], replicated, may hold values from 0 to 63
- tenant_adapter: int32 [64], replicated, may hold values from 0 to 31
Outputs:
- projected: bfloat16 [256, 5120], P('row', 'kv')
The draws below stay inside these ranges and needn't reach their ends.
Inputs may be any that keep to these rules, and one draw needn't show every extreme that they name: At most 16 of the 8 x 32 slots of the rows of one index of kv name one holder; in every draw one holder is named exactly 16 times by the slots of every index.
All inputs are finite; a program needn't handle non-finite values.
Results may differ from the reference program's by a relative error of at most 0.0159.
The reference program's roundings to bfloat16 on the way count: a program that leaves them out, or rounds other values in their place, can miss the bound.
Values may be sent and summed in bfloat16 or wider, within the bound.
A program may use at most 256 MiB of HBM per device.

```python
import math
import jax
import jax.numpy as jnp
from jax import lax

MODEL_WIDTH = 5120
QUERY_HEADS = 64
KVH = 8
HEAD_WIDTH = 128
ADAPTER_RANK = 16
ADAPTER_COUNT = 32
TENANTS = 64
BLOCK = 128
BPR = 32
ROWS_DEV = 8
BLK_DEV = 128
CAP = 16
ROWS = 256
BLOCKS = 4096
N_KV = 32


def draw_paged_key_cache(key, part):
    key = jax.random.fold_in(key, 5)
    noise_key = jax.random.fold_in(key, 0)
    values = jax.random.truncated_normal(noise_key, -6.0, 6.0, (BLOCKS, BLOCK, KVH, HEAD_WIDTH), jnp.float32)
    return values.astype(jnp.bfloat16)


def draw_holder(key, part):
    key = jax.random.fold_in(key, 7)
    hot_key, device_key = jax.random.split(key)
    hot_holder = jax.random.randint(hot_key, (), 0, N_KV)
    seat_owner = (jnp.arange(N_KV * CAP, dtype=jnp.int32) // CAP + hot_holder) % N_KV

    def one_device(device_seed):
        order_key, place_key = jax.random.split(device_seed)
        remaining = jax.random.permutation(order_key, N_KV * CAP - CAP) + CAP
        seats = jnp.concatenate([jnp.arange(CAP, dtype=jnp.int32), remaining.astype(jnp.int32)])[:ROWS_DEV * BPR]
        chosen = seat_owner[seats]
        return jax.random.permutation(place_key, chosen).reshape(ROWS_DEV, BPR)
    drawn = jax.vmap(one_device)(jax.random.split(device_key, N_KV))
    return drawn.reshape(ROWS, BPR).astype(jnp.int32)


def plant(entries, key, least, top_value):
    spot = [jax.random.randint(jax.random.fold_in(key, axis), (), 0, length) for axis, length in enumerate(entries.shape)]
    widest = entries.shape.index(max(entries.shape))
    neighbour = spot[:widest] + [(spot[widest] + 1) % entries.shape[widest]] + spot[widest + 1:]
    return entries.at[tuple(spot)].set(least).at[tuple(neighbour)].set(top_value)


def levels(rng, dims, cuts, low, largest):
    def one(dim, parts):
        steps = jax.random.uniform(jax.random.fold_in(jax.random.fold_in(rng, 6), dim), (parts,), jnp.float32, low / len(cuts), largest / len(cuts))
        return jnp.repeat(jnp.exp(steps), dims[dim] // parts).reshape((-1,) + (1,) * (len(dims) - dim - 1))

    loudness = one(*cuts[0])
    for cut in cuts[1:]:
        loudness = loudness * one(*cut)
    return loudness


def gaussian(stream_key, extent, width, reach, cuts=(), kind=jnp.bfloat16):
    gain = levels(stream_key, extent, cuts, -0.22, 0.18) if cuts else 1.0
    array = jax.random.normal(stream_key, extent, jnp.float32) * width * gain
    return jnp.minimum(jnp.maximum(array, -reach), reach).astype(kind)


def setup_inputs(seed: int = 0) -> dict:
    key_of = jax.random.split(jax.random.key(seed), 14)
    return {
        "hidden": gaussian(key_of[0], (ROWS, MODEL_WIDTH), 1.0, 6.0, ((1, 32),)),
        "query_weight": gaussian(key_of[1], (MODEL_WIDTH, QUERY_HEADS * HEAD_WIDTH), MODEL_WIDTH ** -0.5, 0.078125, ((0, 32), (1, 4))),
        "adapter_down_weight": gaussian(key_of[2], (ADAPTER_COUNT, MODEL_WIDTH, ADAPTER_RANK), MODEL_WIDTH ** -0.5, 0.078125, ((1, 32),)),
        "adapter_up_weight": gaussian(key_of[3], (ADAPTER_COUNT, ADAPTER_RANK, QUERY_HEADS * HEAD_WIDTH), ADAPTER_RANK ** -0.5, 1.5, ((2, 4),), jnp.float32),
        "query_norm_gain": jnp.clip(1.0 + 0.18 * jax.random.normal(key_of[4], (HEAD_WIDTH,), jnp.float32), 0.1, 1.9),
        "paged_key_cache": draw_paged_key_cache(jax.random.fold_in(key_of[13], 71), 0),
        "paged_value_cache": gaussian(key_of[6], (BLOCKS, BLOCK, KVH, HEAD_WIDTH), 1.0, 6.0, ((0, 32), (2, 4))),
        "output_weight": gaussian(key_of[7], (QUERY_HEADS * HEAD_WIDTH, MODEL_WIDTH), (QUERY_HEADS * HEAD_WIDTH) ** -0.5, 0.0625, ((0, 4), (1, 32))),
        "holder": draw_holder(jax.random.fold_in(key_of[13], 71), 0),
        "holder_block_index": plant(jax.random.randint(key_of[9], (ROWS, BPR), 0, BLK_DEV), jax.random.fold_in(key_of[9], 1), 0, BLK_DEV - 1).astype(jnp.int32),
        "block_used_length": plant(jax.random.randint(key_of[10], (ROWS, BPR), 1, BLOCK + 1), jax.random.fold_in(key_of[10], 1), 1, BLOCK).astype(jnp.int32),
        "tenant": plant(jax.random.randint(key_of[11], (ROWS,), 0, TENANTS), jax.random.fold_in(key_of[11], 1), 0, TENANTS - 1).astype(jnp.int32),
        "tenant_adapter": plant(jax.random.randint(key_of[12], (TENANTS,), 0, ADAPTER_COUNT), jax.random.fold_in(key_of[12], 1), 0, ADAPTER_COUNT - 1).astype(jnp.int32),
    }


ADAPTER_SCALE = 0.5
ROPE_BASE = 1000000.0
EPSILON = 1e-06
NEG_FILL = -1e+30

def rotate_half(query, position):
    half_width = query.shape[-1] // 2
    frequency = ROPE_BASE ** (-(jnp.arange(half_width, dtype=jnp.float32) * 2.0) / query.shape[-1])
    angles = position[:, None] * frequency[None, :]
    cosine = jnp.concatenate([jnp.cos(angles), jnp.cos(angles)], axis=-1)[:, None, :]
    sine_part = jnp.concatenate([jnp.sin(angles), jnp.sin(angles)], axis=-1)[:, None, :]
    first_half = query[..., :half_width]
    second_half = query[..., half_width:]
    turned = jnp.concatenate([-second_half, first_half], axis=-1)
    return query * cosine + turned * sine_part

def prepare_queries(query_linear, query_norm_gain, block_used_length):
    row_count = query_linear.shape[0]
    head_size = query_norm_gain.shape[0]
    query = query_linear.reshape(row_count, query_linear.shape[1] // head_size, head_size)
    squares = lax.optimization_barrier(jnp.mean(query * query, axis=-1, keepdims=True))
    query = query * lax.rsqrt(squares + EPSILON) * query_norm_gain
    position = (lax.optimization_barrier(jnp.sum(block_used_length, axis=1)) - 1).astype(jnp.float32)
    return rotate_half(query, position).astype(jnp.bfloat16)

def merge_blocks(block_out, block_top, block_total, axis):
    overall = lax.optimization_barrier(jnp.max(block_top, axis=axis, keepdims=True))
    factors = jnp.exp(block_top - overall)
    numerator = lax.optimization_barrier(jnp.sum(factors[..., None] * block_out, axis=axis))
    denominator = lax.optimization_barrier(jnp.sum(factors * block_total, axis=axis))
    return numerator / denominator[..., None]

def reference(hidden, query_weight, adapter_down_weight, adapter_up_weight, query_norm_gain, paged_key_cache, paged_value_cache, output_weight, holder, holder_block_index, block_used_length, tenant, tenant_adapter):
    adapter_per_row = tenant_adapter[tenant]
    base_product = jnp.dot(hidden, query_weight, preferred_element_type=jnp.float32)
    down_projected_rows = adapter_down_weight[adapter_per_row]
    reduced_rank_rows = jnp.einsum('rd,rdk->rk', hidden.astype(jnp.float32), down_projected_rows.astype(jnp.float32))
    up_projected_rows = adapter_up_weight[adapter_per_row]
    adapter_product = jnp.einsum('wi,wio->wo', reduced_rank_rows, up_projected_rows, precision=lax.Precision.HIGHEST)
    query_linear = base_product + ADAPTER_SCALE * adapter_product
    queries = lax.optimization_barrier(prepare_queries(query_linear, query_norm_gain, block_used_length))
    global_blocks = (holder * BLK_DEV + holder_block_index).astype(jnp.int32)

    def attend_row(operands):
        query, blocks, lengths = operands
        keys = paged_key_cache[blocks].astype(jnp.float32)
        values = paged_value_cache[blocks].astype(jnp.float32)
        grouped = query.astype(jnp.float32).reshape(KVH, QUERY_HEADS // KVH, HEAD_WIDTH)
        scores = jnp.einsum('agd,btad->bagt', grouped, keys) * (1.0 / math.sqrt(HEAD_WIDTH))
        token_mask = (jnp.arange(BLOCK, dtype=jnp.int32)[None, :] < lengths[:, None])[:, None, None, :]
        block_top = lax.optimization_barrier(jnp.max(jnp.where(token_mask, scores, NEG_FILL), axis=-1))
        weights = jnp.where(token_mask, jnp.exp(scores - block_top[..., None]), 0.0)
        block_total = lax.optimization_barrier(jnp.sum(weights, axis=-1))
        rounded = lax.optimization_barrier(weights.astype(jnp.bfloat16))
        block_out = jnp.einsum('bagt,btad->bagd', rounded.astype(jnp.float32), values)
        return merge_blocks(block_out, block_top, block_total, 0).reshape(QUERY_HEADS * HEAD_WIDTH)
    attention = lax.map(attend_row, (queries, global_blocks, block_used_length)).astype(jnp.bfloat16)
    return jnp.dot(attention, output_weight, preferred_element_type=jnp.float32).astype(jnp.bfloat16)
```

```python
import functools
import math

import jax
import jax.numpy as jnp
from jax import lax
from jax.experimental import pallas as pl
from jax.experimental.pallas import tpu as pltpu
from jax.sharding import PartitionSpec as P

NEG = -1e30
F32, BF16, I32 = jnp.float32, jnp.bfloat16, jnp.int32
NT = (((1,), (1,)), ((), ()))
TN = (((0,), (0,)), ((), ()))
TT = (((0,), (1,)), ((), ()))
MESH = pl.DeviceIdType.MESH
PIECES = 8
ADAPTER_SCALE = 0.5
ROPE_BASE = 1000000.0
EPSILON = 1e-06


def iota(shape, dim):
    return lax.broadcasted_iota(I32, shape, dim)


def flat_row(x):
    rows, n = x.shape
    wide = jnp.concatenate([x.astype(F32)] * rows, axis=1)
    keep = lax.div(iota(wide.shape, 1), n) == iota(wide.shape, 0)
    return jnp.sum(jnp.where(keep, wide, 0.0), axis=0, keepdims=True)


def remote(src, dst, send, recv, device):
    return pltpu.make_async_remote_copy(
        src_ref=src, dst_ref=dst, send_sem=send, recv_sem=recv, device_id=device, device_id_type=MESH)


def project_kernel(ht_ref, w_ref, dt_ref, up_hbm, gain_ref, freq_ref, holder_ref, index_ref, used_ref,
                   tenant_ref, held_ref, tenant_s, held_s, q_ref, ent_ref,
                   part, pair, mine, landed, total, low_t, turned, up, ent_send,
                   up_sem, pair_send, pair_recv, rs_send, rs_recv, ag_send, ag_recv, fw_send, fw_recv,
                   en_send, en_recv):
    row, me = lax.axis_index("row"), lax.axis_index("kv")
    peers = lax.axis_size("kv")
    chips = peers // 2
    chip, core = me // 2, me % 2
    partner = (row, 2 * chip + 1 - core)
    wide = w_ref.shape[1]
    heads, width = q_ref.shape[1], q_ref.shape[2]
    own = q_ref.shape[0] // peers
    cap = ent_ref.shape[0] // peers
    barrier = pltpu.get_barrier_semaphore()

    def greet(i, c):
        pl.semaphore_signal(barrier, inc=1, device_id=(row, (me + i) % peers), device_id_type=MESH)
        return c

    lax.fori_loop(1, peers, greet, 0)
    up_copy = pltpu.make_async_copy(up_hbm, up, up_sem)
    up_copy.start()

    ht = ht_ref[...]
    part[:, :wide] = lax.dot_general(ht, w_ref[...], TN, preferred_element_type=F32)
    low = lax.dot_general(ht, dt_ref[...], TT, preferred_element_type=F32)
    rows, ranks = low.shape
    rank = ranks // 32
    is_tenant = jnp.where(tenant_ref[...] == iota((held_ref.shape[1], rows), 0), 1.0, 0.0).astype(BF16)
    held = jnp.broadcast_to(held_ref[...].astype(F32), (16, held_ref.shape[1])).astype(BF16)
    adapter = jnp.dot(held, is_tenant, preferred_element_type=F32)[0:8]
    adapter = jnp.transpose(adapter)[:, 0:1].astype(I32)
    low = jnp.where(lax.div(iota(low.shape, 1), rank) == adapter, low, 0.0)
    part[:, wide:] = sum(low[:, 128 * i: 128 * (i + 1)] for i in range(ranks // 128))

    dest, index, used = flat_row(holder_ref[...]), flat_row(index_ref[...]), flat_row(used_ref[...])
    count = dest.shape[1]
    to = dest == iota((peers, count), 0).astype(F32)
    earlier = jnp.where(iota((count, count), 0) < iota((count, count), 1), 1.0, 0.0).astype(BF16)
    before = jnp.dot(jnp.where(to, 1.0, 0.0).astype(BF16), earlier, preferred_element_type=F32)
    place = dest * cap + jnp.sum(jnp.where(to, before, 0.0), axis=0, keepdims=True)
    chosen = jnp.where(place == iota((peers * cap, count), 0).astype(F32), 1.0, 0.0).astype(BF16)
    sub = iota((128, count), 0)
    from_row = (me * own + lax.div(iota((1, count), 1), count // own)).astype(F32)
    fields = jnp.where(sub == 0, index, jnp.where(sub == 1, used, jnp.where(sub == 2, from_row, 0.0)))
    ent = lax.dot_general(chosen, fields.astype(BF16), NT, preferred_element_type=F32).astype(BF16)
    ent_send[...] = ent

    pl.semaphore_wait(barrier, peers - 1)

    def pair_copy(d):
        return remote(part.at[pl.ds((2 * d + 1 - core) * own, own)], pair.at[d],
                      pair_send.at[d], pair_recv.at[d], partner)

    def rs_copy(d, slot):
        return remote(mine.at[d], landed.at[slot], rs_send.at[d], rs_recv.at[slot], (row, 2 * d + core))

    def ent_copy(t, slot):
        return remote(ent_send.at[pl.ds(t * cap, cap)], ent_ref.at[pl.ds(slot * cap, cap)],
                      en_send.at[t], en_recv.at[slot], (row, t))

    def pair_start(i, c):
        pair_copy((chip + 1 + i) % chips).start()
        return c

    lax.fori_loop(0, chips, pair_start, 0)

    def forward(i, c):
        d = (chip + 1 + i) % chips
        pair_copy(d).wait_recv()
        mine[d] = part[pl.ds((2 * d + core) * own, own), :] + pair[d]
        rs_copy(d, chip).start()
        return c

    lax.fori_loop(0, chips - 1, forward, 0)
    pair_copy(chip).wait_recv()
    total[...] = part[pl.ds(me * own, own), :] + pair[chip]

    def ent_start(i, c):
        ent_copy((me + i) % peers, me).start()
        return c

    lax.fori_loop(1, peers, ent_start, 0)
    at = pl.ds(me * cap, cap)
    ent_ref[at, :] = ent_send[at, :]

    angles = (jnp.sum(used_ref[...], axis=1, keepdims=True) - 1).astype(F32) * freq_ref[...]
    cosine, sine = jnp.cos(angles), jnp.sin(angles)
    sine = jnp.where(iota(sine.shape, 1) < width // 2, -sine, sine)
    up_copy.wait()

    def gather(i, c):
        s = (chip + chips - 1 - i) % chips
        rs_copy(s, s).wait_recv()
        total[...] += landed[s]
        return c

    lax.fori_loop(0, chips - 1, gather, 0)

    low_t[...] = jnp.transpose(jnp.concatenate([total[:, wide:], jnp.zeros((128 - own, 128), F32)], axis=0)).reshape(low_t.shape)
    for r in range(own):
        adapter = held_s[tenant_s[me * own + r]]
        column = low_t[lax.rem(adapter, 128 // rank)][:, r:r + 1]
        more = jnp.sum(column * up[adapter], axis=0, keepdims=True)
        total[r:r + 1, :wide] += ADAPTER_SCALE * more
    gain = gain_ref[...]
    for h in range(heads):
        x = total[:, h * width:(h + 1) * width]
        x = x * lax.rsqrt(jnp.mean(x * x, axis=1, keepdims=True) + EPSILON) * gain
        turned[:, h, :] = x * cosine + pltpu.roll(x, width // 2, 1) * sine
    q_ref[pl.ds(me * own, own)] = turned[...].astype(BF16)

    def q_copy(d, owner, send, recv, device):
        at = pl.ds(owner * own, own)
        return remote(q_ref.at[at], q_ref.at[at], send, recv, device)

    def ag_copy(d, owner, slot):
        return q_copy(d, owner, ag_send.at[d], ag_recv.at[slot], (row, 2 * d + core))

    def fw_copy(d, owner):
        return q_copy(d, owner, fw_send.at[d], fw_recv.at[d], partner)

    def ag_start(i, c):
        ag_copy((chip + 1 + i) % chips, me, chip).start()
        return c

    lax.fori_loop(0, chips - 1, ag_start, 0)
    fw_copy(chip, me).start()

    def ag_forward(i, c):
        s = (chip + chips - 1 - i) % chips
        ag_copy(s, 2 * s + core, s).wait_recv()
        fw_copy(s, 2 * s + core).start()
        return c

    lax.fori_loop(0, chips - 1, ag_forward, 0)

    def finish(d, c):
        pair_copy(d).wait_send()
        fw_copy(d, 2 * d + 1 - core).wait_recv()
        fw_copy(d, 2 * d + core).wait_send()
        return c

    lax.fori_loop(0, chips, finish, 0)

    def finish_others(i, c):
        d = (chip + 1 + i) % chips
        rs_copy(d, chip).wait_send()
        ag_copy(d, me, chip).wait_send()
        return c

    lax.fori_loop(0, chips - 1, finish_others, 0)

    def finish_ent(i, c):
        t = (me + i) % peers
        ent_copy(t, t).wait_recv()
        ent_copy(t, me).wait_send()
        return c

    lax.fori_loop(1, peers, finish_ent, 0)


def project(ht, w, dt, up, gain, freq, holder, index, used, tenant, held, peers):
    rows, wide, width = ht.shape[1], w.shape[1], gain.shape[1]
    own = rows // peers
    cap = 2 * own * holder.shape[1] // peers
    chips = peers // 2
    heads = wide // width
    span = wide + 128
    vm = pl.BlockSpec(memory_space=pltpu.VMEM)
    sm = pl.BlockSpec(memory_space=pltpu.SMEM)
    dma = pltpu.SemaphoreType.DMA
    return pl.pallas_call(
        project_kernel,
        out_shape=[jax.ShapeDtypeStruct((rows, heads, width), BF16),
                   jax.ShapeDtypeStruct((peers * cap, 128), BF16)],
        in_specs=[vm, vm, vm, pl.BlockSpec(memory_space=pl.ANY), vm, vm, vm, vm, vm, vm, vm, sm, sm],
        out_specs=[vm, vm],
        scratch_shapes=[
            pltpu.VMEM((rows, span), F32), pltpu.VMEM((chips, own, span), F32),
            pltpu.VMEM((chips, own, span), F32), pltpu.VMEM((chips, own, span), F32),
            pltpu.VMEM((own, span), F32), pltpu.VMEM((128 // up.shape[1], up.shape[1], 128), F32),
            pltpu.VMEM((own, heads, width), F32),
            pltpu.VMEM(up.shape, F32), pltpu.VMEM((peers * cap, 128), BF16),
            dma, dma((chips,)), dma((chips,)), dma((chips,)), dma((chips,)), dma((chips,)), dma((chips,)),
            dma((chips,)), dma((chips,)), dma((peers,)), dma((peers,)),
        ],
        compiler_params=pltpu.CompilerParams(
            vmem_limit_bytes=40 * 2**20, collective_id=0, has_side_effects=True),
        name="project",
    )(ht, w, dt, up, gain, freq, holder, index, used, tenant.reshape(1, -1), held.reshape(1, -1), tenant, held)


def combine_kernel(p_ref, ml_ref, wo_ref, out_ref, parts, tops, flat, attended, terms, summed,
                   p_send, p_recv, m_send, m_recv, ag_send, ag_recv, fw_send, fw_recv, z_send, z_recv):
    row, me = lax.axis_index("row"), lax.axis_index("kv")
    peers, planes = lax.axis_size("kv"), lax.axis_size("row")
    chips = peers // 2
    chip, core = me // 2, me % 2
    partner = (row, 2 * chip + 1 - core)
    pair_rows = 16
    heads, width = p_ref.shape[2] // pair_rows, p_ref.shape[3]
    out_rows = out_ref.shape[0]
    barrier = pltpu.get_barrier_semaphore()

    def greet(i, c):
        pl.semaphore_signal(barrier, inc=1, device_id=(row, (me + i) % peers), device_id_type=MESH)
        return c

    def greet_plane(i, c):
        pl.semaphore_signal(barrier, inc=1, device_id=((row + i) % planes, me), device_id_type=MESH)
        return c

    lax.fori_loop(1, peers, greet, 0)
    lax.fori_loop(1, planes, greet_plane, 0)
    pl.semaphore_wait(barrier, peers + planes - 2)

    def part_copies(t, slot):
        return (remote(p_ref.at[t % 2, t // 2], parts.at[slot], p_send.at[t], p_recv.at[slot], (row, t)),
                remote(ml_ref.at[t % 2, t // 2], tops.at[slot], m_send.at[t], m_recv.at[slot], (row, t)))

    def part_start(i, c):
        for copy in part_copies((me + i) % peers, me):
            copy.start()
        return c

    lax.fori_loop(1, peers, part_start, 0)
    parts[me] = p_ref[core, chip]
    tops[me] = ml_ref[core, chip]

    def part_wait(i, c):
        t = (me + peers - i) % peers
        for copy in part_copies(t, t):
            copy.wait_recv()
        return c

    lax.fori_loop(1, peers, part_wait, 0)
    top, weight = tops[:, 0, :], tops[:, 1, :]
    factor = jnp.exp2(top - jnp.max(top, axis=0, keepdims=True))
    factor = factor / jnp.sum(factor * weight, axis=0, keepdims=True)
    factor = jnp.transpose(jnp.concatenate([factor, jnp.zeros((128 - peers, 128), F32)], axis=0))
    total = jnp.zeros((128, width), F32)
    for s in range(peers):
        total += factor[:, s:s + 1] * parts[s].astype(F32)
    flat[...] = total
    here = pl.ds(chip * pair_rows, pair_rows)
    for h in range(heads):
        attended[core, here, h * width:(h + 1) * width] = flat[pl.ds(h, pair_rows, stride=heads), :].astype(BF16)

    def at_copy(c, d, send, recv, device):
        at = pl.ds(d * pair_rows, pair_rows)
        return remote(attended.at[c, at], attended.at[c, at], send, recv, device)

    def ag_copy(d, source):
        return at_copy(core, source, ag_send.at[d], ag_recv.at[source], (row, 2 * d + core))

    def fw_copy(c, d):
        return at_copy(c, d, fw_send.at[d], fw_recv.at[d], partner)

    def ag_start(i, c):
        ag_copy((chip + 1 + i) % chips, chip).start()
        return c

    lax.fori_loop(0, chips - 1, ag_start, 0)
    fw_copy(core, chip).start()

    def ag_forward(i, c):
        s = (chip + chips - 1 - i) % chips
        ag_copy(s, s).wait_recv()
        fw_copy(core, s).start()
        return c

    lax.fori_loop(0, chips - 1, ag_forward, 0)

    def fw_wait(d, c):
        fw_copy(1 - core, d).wait_recv()
        return c

    lax.fori_loop(0, chips, fw_wait, 0)
    half = heads * width
    terms[...] = (lax.dot_general(attended[0], wo_ref[:, :half], NT, preferred_element_type=F32)
                  + lax.dot_general(attended[1], wo_ref[:, half:], NT, preferred_element_type=F32))

    def z_copy(z, slot):
        return remote(terms.at[pl.ds(z * out_rows, out_rows)], summed.at[slot], z_send.at[z], z_recv.at[slot], (z, me))

    for i in range(1, planes):
        z_copy((row + i) % planes, row).start()
    total = terms[pl.ds(row * out_rows, out_rows), :]
    for i in range(1, planes):
        z = (row + i) % planes
        z_copy(z, z).wait_recv()
        total += summed[z]
    out_ref[...] = total.astype(BF16)

    def finish(i, c):
        for copy in part_copies((me + i) % peers, me):
            copy.wait_send()
        return c

    lax.fori_loop(1, peers, finish, 0)

    def finish_ag(i, c):
        ag_copy((chip + 1 + i) % chips, chip).wait_send()
        return c

    lax.fori_loop(0, chips - 1, finish_ag, 0)

    def finish_fw(d, c):
        fw_copy(core, d).wait_send()
        return c

    lax.fori_loop(0, chips, finish_fw, 0)
    for i in range(1, planes):
        z_copy((row + i) % planes, row).wait_send()


def combine(p, ml, wo, peers, planes):
    chips = peers // 2
    rows = chips * 16
    wide = wo.shape[1]
    cols = wo.shape[0]
    vm = pl.BlockSpec(memory_space=pltpu.VMEM)
    dma = pltpu.SemaphoreType.DMA
    return pl.pallas_call(
        combine_kernel,
        out_shape=jax.ShapeDtypeStruct((rows // planes, cols), BF16),
        in_specs=[vm, vm, vm],
        out_specs=vm,
        scratch_shapes=[
            pltpu.VMEM((peers, 128, 128), BF16), pltpu.VMEM((peers, 8, 128), F32), pltpu.VMEM((128, 128), F32),
            pltpu.VMEM((2, rows, wide // 2), BF16), pltpu.VMEM((rows, cols), F32),
            pltpu.VMEM((planes, rows // planes, cols), F32),
            dma((peers,)), dma((peers,)), dma((peers,)), dma((peers,)),
            dma((chips,)), dma((chips,)), dma((chips,)), dma((chips,)), dma((planes,)), dma((planes,)),
        ],
        compiler_params=pltpu.CompilerParams(
            vmem_limit_bytes=40 * 2**20, collective_id=1, has_side_effects=True),
        name="combine",
    )(p, ml, wo)


def attend_kernel(group, unroll, q_ref, ent_ref, k_hbm, v_hbm, p_ref, ml_ref,
                  kbuf, vbuf, o_st, m_st, l_st, acc, mx, tot, tab_v, ent_v, tab, ent_s,
                  k_sem, v_sem, t_sem):
    blocks, toks, width = kbuf.shape
    rows, heads = q_ref.shape[0], q_ref.shape[1]
    slots = ent_ref.shape[0]
    owners = rows // 8
    per_owner = slots // owners
    positions = tab.shape[1]
    step = blocks // PIECES
    coef = math.log2(math.e) / math.sqrt(width)

    def piece(i):
        at = pl.ds(i * step, step)
        return (pltpu.make_async_copy(k_hbm.at[at], kbuf.at[at], k_sem.at[i]),
                pltpu.make_async_copy(v_hbm.at[at], vbuf.at[at], v_sem.at[i]))

    for i in range(PIECES):
        for copy in piece(i):
            copy.start()

    ent = ent_ref[...]
    entf = ent.astype(F32)
    pick = (lax.broadcasted_iota(I32, (16, 128), 0) == lax.broadcasted_iota(I32, (16, 128), 1)).astype(F32).astype(BF16)
    ent_t = lax.dot_general(pick, ent, NT, preferred_element_type=F32)
    blk_r, len_r, row_r = ent_t[0:1], ent_t[1:2], ent_t[2:3]
    key_c = jnp.where(entf[:, 1:2] > 0, entf[:, 0:1], 999.0)
    key_r = jnp.where(len_r > 0, blk_r, 999.0)
    earlier = lax.broadcasted_iota(I32, (slots, slots), 1) < lax.broadcasted_iota(I32, (slots, slots), 0)
    within = jnp.sum(jnp.where((key_c == key_r) & earlier, 1.0, 0.0), axis=1, keepdims=True)
    block_of = lax.broadcasted_iota(I32, (blocks, slots), 0).astype(F32) == key_r
    count = jnp.sum(jnp.where(block_of, 1.0, 0.0), axis=1, keepdims=True)
    chunks = jnp.floor((count + (group - 1)) * (1.0 / group))
    below = (lax.broadcasted_iota(I32, (blocks, blocks), 1) < lax.broadcasted_iota(I32, (blocks, blocks), 0))
    first = jnp.dot(jnp.where(below, 1.0, 0.0).astype(BF16),
                    jnp.broadcast_to(chunks, (blocks, 128)).astype(BF16), preferred_element_type=F32)
    total = jnp.sum(chunks, axis=0, keepdims=True)
    own_block = (key_c == lax.broadcasted_iota(I32, (slots, blocks), 1).astype(F32))
    first_c = jnp.dot(jnp.where(own_block, 1.0, 0.0).astype(BF16), first.astype(BF16),
                      preferred_element_type=F32)[:, 0:1]
    major = jnp.floor(within * (1.0 / group))
    place = (first_c + major) * group + (within - major * group)
    place = jnp.where(entf[:, 1:2] > 0, place, -1.0)
    slot_r = lax.broadcasted_iota(I32, (1, slots), 1) + 1
    half = lax.div(slot_r, 2)
    odd = slot_r - 2 * half
    sub = lax.broadcasted_iota(I32, (16, slots), 0)
    fields = jnp.where(sub == 0, blk_r, jnp.where(sub == 1, len_r, jnp.where(sub == 2, row_r, jnp.where(
        sub == 3, half.astype(F32), jnp.where(sub == 4, odd.astype(F32), 0.0))))).astype(BF16)
    chosen = jnp.where(place == lax.broadcasted_iota(I32, (slots, positions), 1).astype(F32), 1.0, 0.0).astype(BF16)
    table = jnp.dot(fields, chosen, preferred_element_type=F32)
    sub = lax.broadcasted_iota(I32, (8, positions), 0)
    t8 = table[0:8]
    tab_v[...] = jnp.where(sub == 1, 2.0 * t8, jnp.where(
        sub == 3, 2.0 * t8 + table[4:5], jnp.where(sub == 4, total, t8))).astype(I32)
    sub = lax.broadcasted_iota(I32, (8, slots), 0)
    last_row = (lax.div(lax.broadcasted_iota(I32, (1, slots), 1), per_owner) * 8 + 7).astype(F32)
    ent_v[...] = jnp.where(sub == 2, jnp.where(len_r > 0, row_r, last_row), ent_t[0:8]).astype(I32)
    copies = (pltpu.make_async_copy(tab_v, tab, t_sem.at[0]), pltpu.make_async_copy(ent_v, ent_s, t_sem.at[1]))
    for copy in copies:
        copy.start()
    acc[...] = jnp.zeros_like(acc)
    mx[...] = jnp.full_like(mx, NEG)
    tot[...] = jnp.zeros_like(tot)
    for copy in copies:
        copy.wait()

    col = lax.broadcasted_iota(I32, (heads, toks), 1)
    head = lax.broadcasted_iota(I32, (heads, toks), 0)
    match = (col & 1) == lax.div(head, heads // 2)
    col = jnp.where(match, col, 1 << 20)
    total_chunks = tab[4, 0]

    def chunk(c):
        base = c * group
        b = tab[0, base]
        q = jnp.concatenate([q_ref[tab[2, base + g]] for g in range(group)], axis=0)
        s = lax.dot_general(q, kbuf[b], NT, preferred_element_type=F32)
        s = jnp.concatenate(
            [jnp.where(col < tab[1, base + g], s[heads * g: heads * (g + 1)], NEG) for g in range(group)], axis=0)
        m = jnp.max(s, axis=1, keepdims=True)
        w = jnp.exp2((s - m) * coef)
        l = jnp.sum(w, axis=1, keepdims=True)
        o = jnp.dot(w.astype(BF16), vbuf[b], preferred_element_type=F32)
        return o, m, l

    def store(c, res):
        o, m, l = res
        for g in range(group):
            slot = tab[3, c * group + g]
            at = slice(heads * g, heads * (g + 1))
            o_st[slot] = o[at]
            m_st[slot] = jnp.broadcast_to(m[at] * coef, (heads, width))
            l_st[slot] = jnp.broadcast_to(l[at], (heads, width))

    def wait_piece(i, carry):
        for copy in piece(i):
            copy.wait()
        return carry

    def body(i, waited):
        c = i * unroll
        need = 0
        for u in range(unroll):
            need = jnp.maximum(need, tab[0, (c + u) * group])
        need = lax.div(need, step) + 1
        lax.fori_loop(waited, need, wait_piece, 0)
        waited = jnp.maximum(waited, need)
        res = [chunk(c + u) for u in range(unroll)]
        for u in range(unroll):
            store(c + u, res[u])
        return waited

    waited = lax.fori_loop(0, lax.div(total_chunks + unroll - 1, unroll), body, 0)
    lax.fori_loop(waited, PIECES, wait_piece, 0)

    def merge(o, carry):
        m = jnp.full((heads, width), NEG, F32)
        a = jnp.zeros((heads, width), F32)
        l = a
        prev = -1
        for p in range(per_owner):
            slot = o * per_owner + p
            row = ent_s[2, slot]
            valid = ent_s[1, slot] > 0
            mp = jnp.where(valid, m_st[slot + 1], NEG)
            lp = jnp.where(valid, l_st[slot + 1], 0.0)
            op = jnp.where(valid, o_st[slot + 1], 0.0)
            mo = jnp.where(row == prev, m, NEG)
            m = jnp.maximum(mo, mp)
            fa = jnp.exp2(mo - m)
            fb = jnp.exp2(mp - m)
            a = fa * a + fb * op
            l = fa * l + fb * lp
            acc[row] = a
            mx[row] = m
            tot[row] = l
            prev = row
        return carry

    lax.fori_loop(0, owners, merge, 0)

    eye = lax.broadcasted_iota(I32, (128, 128), 0) == lax.broadcasted_iota(I32, (128, 128), 1)

    def finish(d, carry):
        at = pl.ds(d * 16, 16)
        for c in range(2):
            hs = slice(8 * c, 8 * c + 8)
            p_ref[c, d] = acc[at, hs, :].reshape(128, width).astype(BF16)
            m = jnp.sum(jnp.where(eye, mx[at, hs, :].reshape(128, width), 0.0), axis=0, keepdims=True)
            l = jnp.sum(jnp.where(eye, tot[at, hs, :].reshape(128, width), 0.0), axis=0, keepdims=True)
            ml_ref[c, d] = jnp.where(lax.broadcasted_iota(I32, (8, 128), 0) == 0, m, l)
        return carry

    lax.fori_loop(0, rows // 16, finish, 0)


def attend(q, ent, k, v, group=8, unroll=16):
    rows, heads, width = q.shape
    blocks, toks, _ = k.shape
    slots = ent.shape[0]
    nc = slots // group + blocks * (group - 1) // group
    nc = -(-nc // unroll) * unroll
    positions = -(-nc * group // 128) * 128
    vm = pl.BlockSpec(memory_space=pltpu.VMEM)
    return pl.pallas_call(
        functools.partial(attend_kernel, group, unroll),
        out_shape=[jax.ShapeDtypeStruct((2, rows // 16, 128, width), BF16),
                   jax.ShapeDtypeStruct((2, rows // 16, 8, 128), F32)],
        in_specs=[vm, vm, pl.BlockSpec(memory_space=pl.ANY), pl.BlockSpec(memory_space=pl.ANY)],
        out_specs=[vm, vm],
        scratch_shapes=[
            pltpu.VMEM((blocks, toks, width), BF16), pltpu.VMEM((blocks, toks, width), BF16),
            pltpu.VMEM((slots + 1, heads, width), F32), pltpu.VMEM((slots + 1, heads, width), F32),
            pltpu.VMEM((slots + 1, heads, width), F32),
            pltpu.VMEM((rows, heads, width), F32), pltpu.VMEM((rows, heads, width), F32),
            pltpu.VMEM((rows, heads, width), F32),
            pltpu.VMEM((8, positions), I32), pltpu.VMEM((8, slots), I32),
            pltpu.SMEM((8, positions), I32), pltpu.SMEM((8, slots), I32),
            pltpu.SemaphoreType.DMA((PIECES,)), pltpu.SemaphoreType.DMA((PIECES,)), pltpu.SemaphoreType.DMA((2,)),
        ],
        compiler_params=pltpu.CompilerParams(vmem_limit_bytes=56 * 2**20),
        name="attend",
    )(q, ent, k, v)


def local(hidden, query_weight, adapter_down_weight, adapter_up_weight, query_norm_gain, paged_key_cache,
          paged_value_cache, output_weight, holder, holder_block_index, block_used_length, tenant, tenant_adapter):
    peers, planes = lax.axis_size("kv"), lax.axis_size("row")
    count, _, rank = adapter_down_weight.shape
    width = query_norm_gain.shape[0]
    blocks, toks, kv_heads, _ = paged_key_cache.shape
    half = width // 2
    freq = ROPE_BASE ** (-(jnp.arange(half, dtype=jnp.float32) * 2.0) / width)
    freq = jnp.concatenate([freq, freq])[None, :]
    down = jnp.transpose(adapter_down_weight, (0, 2, 1)).reshape(count * rank, -1)
    q, ent = project(hidden.T, query_weight, down, adapter_up_weight, query_norm_gain[None, :], freq, holder, holder_block_index,
                     block_used_length, tenant, tenant_adapter, peers)
    p, ml = attend(q, ent, paged_key_cache.reshape(blocks, toks * kv_heads, width),
                   paged_value_cache.reshape(blocks, toks * kv_heads, width))
    return combine(p, ml, output_weight.T, peers, planes)


def solution(mesh):
    return jax.shard_map(
        local,
        mesh=mesh,
        in_specs=(
            P(None, "kv"),
            P("kv", "row"),
            P(None, "kv", None),
            P(None, None, "row"),
            P(),
            P("kv", None, "row", None),
            P("kv", None, "row", None),
            P("row", "kv"),
            P("kv", None),
            P("kv", None),
            P("kv", None),
            P(),
            P(),
        ),
        out_specs=P("row", "kv"),
        check_vma=False,
    )
```

```python
import functools
import math

import jax
import jax.numpy as jnp
from jax import lax
from jax.experimental import pallas as pl
from jax.experimental.pallas import tpu as pltpu
from jax.sharding import PartitionSpec as P

NEG = -1e30
F32, BF16, I32 = jnp.float32, jnp.bfloat16, jnp.int32
NT = (((1,), (1,)), ((), ()))
TN = (((0,), (0,)), ((), ()))
TT = (((0,), (1,)), ((), ()))
MESH = pl.DeviceIdType.MESH
PIECES = 4
GROUP = 8
UNROLL = 16
SIDE = 4
ADAPTER_SCALE = 0.5
ROPE_BASE = 1000000.0
EPSILON = 1e-06


def iota(shape, dim):
    return lax.broadcasted_iota(I32, shape, dim)


def flat_row(x):
    rows, n = x.shape
    wide = jnp.concatenate([x.astype(F32)] * rows, axis=1)
    keep = lax.div(iota(wide.shape, 1), n) == iota(wide.shape, 0)
    return jnp.sum(jnp.where(keep, wide, 0.0), axis=0, keepdims=True)


def remote(src, dst, send, recv, device):
    return pltpu.make_async_remote_copy(
        src_ref=src, dst_ref=dst, send_sem=send, recv_sem=recv, device_id=device, device_id_type=MESH)


def entries_by_holder(holder, index, used, me, own, peers, cap):
    dest, index, used = flat_row(holder), flat_row(index), flat_row(used)
    count = dest.shape[1]
    to = dest == iota((peers, count), 0).astype(F32)
    earlier = jnp.where(iota((count, count), 0) < iota((count, count), 1), 1.0, 0.0).astype(BF16)
    before = jnp.dot(jnp.where(to, 1.0, 0.0).astype(BF16), earlier, preferred_element_type=F32)
    place = dest * cap + jnp.sum(jnp.where(to, before, 0.0), axis=0, keepdims=True)
    chosen = jnp.where(place == iota((peers * cap, count), 0).astype(F32), 1.0, 0.0).astype(BF16)
    sub = iota((128, count), 0)
    from_row = (me * own + lax.div(iota((1, count), 1), count // own)).astype(F32)
    fields = jnp.where(sub == 0, index, jnp.where(sub == 1, used, jnp.where(sub == 2, from_row, 0.0)))
    return lax.dot_general(chosen, fields.astype(BF16), NT, preferred_element_type=F32).astype(BF16)


def order_entries(ent, blocks, rows, positions, per_group):
    slots = ent.shape[0]
    entf = ent.astype(F32)
    pick = jnp.where(iota((16, 128), 0) == iota((16, 128), 1), 1.0, 0.0).astype(BF16)
    ent_t = lax.dot_general(pick, ent, NT, preferred_element_type=F32)
    blk_r, len_r, row_r = ent_t[0:1], ent_t[1:2], ent_t[2:3]
    valid_c = entf[:, 1:2] > 0
    key_c = jnp.where(valid_c, entf[:, 0:1], 999.0)
    key_r = jnp.where(len_r > 0, blk_r, 999.0)
    earlier = iota((slots, slots), 1) < iota((slots, slots), 0)
    within = jnp.sum(jnp.where((key_c == key_r) & earlier, 1.0, 0.0), axis=1, keepdims=True)
    block_of = iota((blocks, slots), 0).astype(F32) == key_r
    count = jnp.sum(jnp.where(block_of, 1.0, 0.0), axis=1, keepdims=True)
    chunks = jnp.floor((count + (GROUP - 1)) * (1.0 / GROUP))
    below = jnp.where(iota((blocks, blocks), 1) < iota((blocks, blocks), 0), 1.0, 0.0).astype(BF16)
    first = jnp.dot(below, jnp.broadcast_to(chunks, (blocks, 128)).astype(BF16), preferred_element_type=F32)
    own_block = jnp.where(key_c == iota((slots, blocks), 1).astype(F32), 1.0, 0.0).astype(BF16)
    first_c = jnp.dot(own_block, first.astype(BF16), preferred_element_type=F32)[:, 0:1]
    major = jnp.floor(within * (1.0 / GROUP))
    chunk_c, seat_c = first_c + major, within - major * GROUP
    place = jnp.where(valid_c, chunk_c * GROUP + seat_c, -1.0)
    sub = iota((16, slots), 0)
    fields = jnp.where(sub == 0, blk_r, jnp.where(sub == 1, len_r, jnp.where(sub == 2, row_r, 0.0))).astype(BF16)
    chosen = jnp.where(place == iota((slots, positions), 1).astype(F32), 1.0, 0.0).astype(BF16)
    table = jnp.dot(fields, chosen, preferred_element_type=F32)[0:8]
    sub = iota(table.shape, 0)
    table = jnp.where(sub == 1, 2.0 * table, table).astype(I32)
    table = jnp.clip(table, 0, jnp.where(sub == 0, blocks - 1, jnp.where(sub == 1, 1 << 16, rows - 1)))
    lane = iota((slots, 128), 1)
    seats = jnp.where(lane == 0, chunk_c, jnp.where(lane == 1, seat_c, 0.0)).astype(BF16)
    seats = lax.dot_general(pick, seats, NT, preferred_element_type=F32)
    where_r = jnp.where(len_r > 0, seats[0:1] * GROUP + seats[1:2], 0.0)
    local_r = row_r - (lax.div(iota((1, slots), 1), per_group) * 16).astype(F32)
    local_r = jnp.where(len_r > 0, local_r, -1.0)
    by_slot = jnp.clip(jnp.where(iota((8, slots), 0) == 0, where_r, local_r).astype(I32), -1, positions - 1)
    by_slot = jnp.where(iota((8, slots), 0) == 0, jnp.maximum(by_slot, 0), by_slot)
    return table, by_slot


def kernel(ht_h, w_h, dt_h, up_h, gain_h, freq_h, holder_h, index_h, used_h, tenant_h, held_h, k_h, v_h, wo_h,
           out_ref,
           ht, w, dt, up, gain, freq, holder, index, used, tenant, held, tenant_s, held_s, kbuf, vbuf, wo,
           part, pair, mine_a, mine_b, land_a, land_b, sum_a, sum_b, end_a, end_b, total, low_t, turned,
           ent_send, ent, tab_v, slot_v, tab, slot_s, q, o_st, e_st,
           partial, tops, partial_in, tops_in, merged, tops_out, parts, tops_all, flat, attended, terms, summed,
           in_sem, kv_sem, tab_sem, pair_send, pair_recv, a_send, a_recv, b_send, b_recv, a2_send, a2_recv,
           b2_send, b2_recv, en_send, en_recv, ag_send, ag_recv, fw_send, fw_recv,
           x_send, x_recv, p_send, p_recv, t_send, t_recv, ag2_send, ag2_recv, fw2_send, fw2_recv, z_send, z_recv):
    row, me = lax.axis_index("row"), lax.axis_index("kv")
    peers, planes = lax.axis_size("kv"), lax.axis_size("row")
    chips = peers // 2
    chip, core = me // 2, me % 2
    x, y = chip // SIDE, chip % SIDE
    partner = (row, 2 * chip + 1 - core)
    wide = w.shape[1]
    rows, heads, width = q.shape
    own = rows // peers
    cap = ent.shape[0] // peers
    blocks, toks, _ = kbuf.shape
    wide_a = mine_a.shape[3]
    barrier = pltpu.get_barrier_semaphore()

    def greet(i, c):
        pl.semaphore_signal(barrier, inc=1, device_id=(row, (me + i) % peers), device_id_type=MESH)
        return c

    def greet_plane(i, c):
        pl.semaphore_signal(barrier, inc=1, device_id=((row + i) % planes, me), device_id_type=MESH)
        return c

    lax.fori_loop(1, peers, greet, 0)
    lax.fori_loop(1, planes, greet_plane, 0)

    loads = [pltpu.make_async_copy(src, dst, in_sem.at[i]) for i, (src, dst) in enumerate((
        (ht_h, ht), (w_h, w), (holder_h, holder), (index_h, index), (used_h, used), (tenant_h, tenant),
        (held_h, held), (dt_h, dt), (tenant_h, tenant_s), (held_h, held_s), (gain_h, gain), (freq_h, freq),
        (up_h, up), (wo_h, wo)))]
    for copy in loads:
        copy.start()
    step = blocks // PIECES
    pool = []
    for i in range(PIECES):
        at = pl.ds(i * step, step)
        pool += [pltpu.make_async_copy(k_h.at[at], kbuf.at[at], kv_sem.at[2 * i]),
                 pltpu.make_async_copy(v_h.at[at], vbuf.at[at], kv_sem.at[2 * i + 1])]
    for copy in pool:
        copy.start()
    for copy in loads[:8]:
        copy.wait()

    part[:, :wide] = lax.dot_general(ht[...], w[...], TN, preferred_element_type=F32)
    low = lax.dot_general(ht[...], dt[...], TT, preferred_element_type=F32)
    rank = up.shape[1]
    is_tenant = jnp.where(tenant[...] == iota((held.shape[1], rows), 0), 1.0, 0.0).astype(BF16)
    held_b = jnp.broadcast_to(held[...].astype(F32), (16, held.shape[1])).astype(BF16)
    adapter = jnp.dot(held_b, is_tenant, preferred_element_type=F32)[0:8]
    adapter = jnp.transpose(adapter)[:, 0:1].astype(I32)
    low = jnp.where(lax.div(iota(low.shape, 1), rank) == adapter, low, 0.0)
    part[:, wide:] = sum(low[:, 128 * i: 128 * (i + 1)] for i in range(low.shape[1] // 128))
    ent_send[...] = entries_by_holder(holder[...], index[...], used[...], me, own, peers, cap)

    pl.semaphore_wait(barrier, peers + planes - 2)

    def pair_copy(d):
        return remote(part.at[pl.ds((2 * d + 1 - core) * own, own)], pair.at[d],
                      pair_send.at[d], pair_recv.at[d], partner)

    def chip_at(ox, oy):
        return (x + ox) % SIDE, (y + oy) % SIDE

    hops = (2, 1, 3, 0)
    for ox in hops:
        for oy in hops:
            dx, dy = chip_at(ox, oy)
            pair_copy(dx * SIDE + dy).start()

    def a_copy(t, s):
        return remote(mine_a.at[t], land_a.at[s], a_send.at[t], a_recv.at[s], (row, 2 * (t * SIDE + y) + core))

    def b_copy(t, i, s):
        return remote(mine_b.at[t, i], land_b.at[s, i], b_send.at[t, i], b_recv.at[s, i],
                      (row, 2 * (x * SIDE + t) + core))

    for ox in hops:
        for oy in hops:
            dx, dy = chip_at(ox, oy)
            d = dx * SIDE + dy
            pair_copy(d).wait_recv()
            both = part[pl.ds((2 * d + core) * own, own), :] + pair[d]
            mine_a[dx, dy] = both[:, :wide_a]
            mine_b[dy, dx] = both[:, wide_a:]
            if oy:
                b_copy(dy, dx, y).start()
        if ox:
            a_copy(dx, x).start()

    def ent_copy(t, slot):
        return remote(ent_send.at[pl.ds(t * cap, cap)], ent.at[pl.ds(slot * cap, cap)],
                      en_send.at[t], en_recv.at[slot], (row, t))

    def ent_start(i, c):
        ent_copy((me + i) % peers, me).start()
        return c

    lax.fori_loop(1, peers, ent_start, 0)
    at = pl.ds(me * cap, cap)
    ent[at, :] = ent_send[at, :]
    for copy in loads[8:]:
        copy.wait()
    angles = (jnp.sum(used[...], axis=1, keepdims=True) - 1).astype(F32) * freq[...]
    cosine, sine = jnp.cos(angles), jnp.sin(angles)
    sine = jnp.where(iota(sine.shape, 1) < width // 2, -sine, sine)

    def a2_copy(t, s):
        return remote(sum_a.at[t], end_a.at[s], a2_send.at[t], a2_recv.at[s], (row, 2 * (x * SIDE + t) + core))

    def b2_copy(t, s):
        return remote(sum_b.at[t], end_b.at[s], b2_send.at[t], b2_recv.at[s], (row, 2 * (t * SIDE + y) + core))

    steps = (1, 3, 2)
    for o in steps:
        a_copy((x + SIDE - o) % SIDE, (x + SIDE - o) % SIDE).wait_recv()
    sum_a[...] = mine_a[x] + land_a[(x + 1) % SIDE] + land_a[(x + 2) % SIDE] + land_a[(x + 3) % SIDE]
    for o in (2, 1, 3):
        a2_copy((y + o) % SIDE, y).start()
    for o in steps:
        for i in range(SIDE):
            b_copy((y + SIDE - o) % SIDE, i, (y + SIDE - o) % SIDE).wait_recv()
    sum_b[...] = mine_b[y] + land_b[(y + 1) % SIDE] + land_b[(y + 2) % SIDE] + land_b[(y + 3) % SIDE]
    for o in (2, 1, 3):
        b2_copy((x + o) % SIDE, x).start()

    def ent_wait(i, c):
        t = (me + peers - i) % peers
        ent_copy(t, t).wait_recv()
        return c

    lax.fori_loop(1, peers, ent_wait, 0)
    table, by_slot = order_entries(ent[...], blocks, rows, tab.shape[1], 2 * cap)
    tab_v[...] = table
    slot_v[...] = by_slot
    tables = (pltpu.make_async_copy(tab_v, tab, tab_sem.at[0]), pltpu.make_async_copy(slot_v, slot_s, tab_sem.at[1]))
    for copy in tables:
        copy.start()

    for o in steps:
        a2_copy((y + SIDE - o) % SIDE, (y + SIDE - o) % SIDE).wait_recv()
    total[:, :wide_a] = sum_a[y] + end_a[(y + 1) % SIDE] + end_a[(y + 2) % SIDE] + end_a[(y + 3) % SIDE]
    for o in steps:
        b2_copy((x + SIDE - o) % SIDE, (x + SIDE - o) % SIDE).wait_recv()
    total[:, wide_a:] = sum_b[x] + end_b[(x + 1) % SIDE] + end_b[(x + 2) % SIDE] + end_b[(x + 3) % SIDE]

    low_t[...] = jnp.transpose(
        jnp.concatenate([total[:, wide:], jnp.zeros((128 - own, 128), F32)], axis=0)).reshape(low_t.shape)
    for r in range(own):
        adapter = held_s[0, tenant_s[0, me * own + r]]
        column = low_t[lax.rem(adapter, 128 // rank)][:, r:r + 1]
        more = jnp.sum(column * up[adapter], axis=0, keepdims=True)
        total[r:r + 1, :wide] += ADAPTER_SCALE * more
    gain_r = gain[...]
    for h in range(heads):
        t = total[:, h * width:(h + 1) * width]
        t = t * lax.rsqrt(jnp.mean(t * t, axis=1, keepdims=True) + EPSILON) * gain_r
        turned[:, h, :] = t * cosine + pltpu.roll(t, width // 2, 1) * sine
    q[pl.ds(me * own, own)] = turned[...].astype(BF16)

    def spread(copy_of, first_ref, relay_copy):
        def start(i, c):
            i = (5 * i) % chips
            copy_of(((x + i // SIDE) % SIDE) * SIDE + (y + i % SIDE) % SIDE, chip).start()
            return c

        def relay(i, c):
            i = (5 * i) % chips
            s = ((x + SIDE - i // SIDE) % SIDE) * SIDE + (y + SIDE - i % SIDE) % SIDE
            copy_of(s, s).wait_recv()
            relay_copy(s, core).start()
            return c

        def landed(d, c):
            relay_copy(d, 1 - core).wait_recv()
            return c

        lax.fori_loop(1, chips, start, 0)
        relay_copy(chip, core).start()
        lax.fori_loop(1, chips, relay, 0)
        lax.fori_loop(0, chips, landed, 0)

    def spread_end(copy_of, relay_copy):
        def sent(i, c):
            copy_of((chip + i) % chips, chip).wait_send()
            return c

        def relayed(d, c):
            relay_copy(d, core).wait_send()
            return c

        lax.fori_loop(1, chips, sent, 0)
        lax.fori_loop(0, chips, relayed, 0)

    def q_copy(d, s):
        at = pl.ds((2 * s + core) * own, own)
        return remote(q.at[at], q.at[at], ag_send.at[d], ag_recv.at[s], (row, 2 * d + core))

    def q_relay(s, c):
        at = pl.ds((2 * s + c) * own, own)
        return remote(q.at[at], q.at[at], fw_send.at[s], fw_recv.at[s], partner)

    spread(q_copy, None, q_relay)
    for copy in tables:
        copy.wait()
    for copy in pool:
        copy.wait()

    coef = math.log2(math.e) / math.sqrt(width)
    col = iota((heads, toks), 1)
    col = jnp.where((col & 1) == lax.div(iota((heads, toks), 0), heads // 2), col, 1 << 20)

    def chunk(c):
        base = c * GROUP
        b = tab[0, base]
        qs = jnp.concatenate([q[tab[2, base + g]] for g in range(GROUP)], axis=0)
        s = lax.dot_general(qs, kbuf[b], NT, preferred_element_type=F32)
        s = jnp.concatenate(
            [jnp.where(col < tab[1, base + g], s[heads * g: heads * (g + 1)], NEG) for g in range(GROUP)], axis=0)
        m = jnp.max(s, axis=1, keepdims=True)
        wt = jnp.exp2((s - m) * coef)
        l = jnp.sum(wt, axis=1, keepdims=True)
        o = jnp.dot(wt.astype(BF16), vbuf[b], preferred_element_type=F32) / l
        e = jnp.broadcast_to(m * coef + jnp.log2(l), o.shape)
        return o.reshape(GROUP, 2, heads // 2, width), e.reshape(GROUP, 2, heads // 2, width)

    def chunks(i, c):
        done = [chunk(i * UNROLL + u) for u in range(UNROLL)]
        for u in range(UNROLL):
            o, e = done[u]
            at = pl.ds((i * UNROLL + u) * GROUP, GROUP)
            o_st[at] = o
            e_st[at] = e
        return c

    lax.fori_loop(0, tab.shape[1] // (GROUP * UNROLL), chunks, 0)

    half = heads // 2
    lane = iota((half, 128), 1)
    same_head = (lane & (half - 1)) == iota((half, 128), 0)
    lane_row = jnp.where(same_head, lax.div(lane, half), -2)
    slots = 2 * cap

    def merge(d, c):
        for hv in range(2):
            tops_of, outs = [], []
            for p in range(slots):
                at = slot_s[0, d * slots + p]
                tops_of.append(jnp.where(lane_row == slot_s[1, d * slots + p], e_st[at, hv], NEG))
                outs.append(o_st[at, hv])
            es = jnp.concatenate(tops_of, axis=0)
            top = jnp.max(es, axis=0, keepdims=True)
            f = jnp.exp2(es - top)
            l = jnp.sum(f, axis=0, keepdims=True)
            f = (f * (1.0 / l)).astype(BF16)
            os = jnp.concatenate(outs, axis=0).astype(BF16)
            partial[hv, d] = lax.dot_general(f, os, TN, preferred_element_type=F32).astype(BF16)
            tops[hv, pl.ds(d, 1), :] = top + jnp.log2(l)
        return c

    lax.fori_loop(0, chips, merge, 0)

    x_copies = (remote(partial.at[1 - core], partial_in, x_send.at[0], x_recv.at[0], partner),
                remote(tops.at[1 - core], tops_in, x_send.at[1], x_recv.at[1], partner))
    for copy in x_copies[::-1]:
        copy.start()

    def columns(fs):
        n = fs.shape[0]
        return jnp.transpose(jnp.concatenate([fs, jnp.zeros((128 - n, 128), F32)], axis=0))

    x_copies[1].wait_recv()
    t0, t1 = tops[core], tops_in[...]
    top = jnp.maximum(t0, t1)
    f0, f1 = jnp.exp2(t0 - top), jnp.exp2(t1 - top)
    l = f0 + f1
    over = top + jnp.log2(l)
    for d in range(chips):
        tops_out[d] = jnp.broadcast_to(over[d:d + 1], (8, 128))
    f = columns(jnp.concatenate([f0 / l, f1 / l], axis=0))

    def t_copy(d, s):
        return remote(tops_out.at[d], tops_all.at[s], t_send.at[d], t_recv.at[s], (row, 2 * d + core))

    def p_copy(d, s):
        return remote(merged.at[d], parts.at[s], p_send.at[d], p_recv.at[s], (row, 2 * d + core))

    def t_start(i, c):
        i = (5 * i) % chips
        t_copy(((x + i // SIDE) % SIDE) * SIDE + (y + i % SIDE) % SIDE, chip).start()
        return c

    lax.fori_loop(1, chips, t_start, 0)
    x_copies[0].wait_recv()
    for d in range(chips):
        merged[d] = (f[:, d:d + 1] * partial[core, d].astype(F32)
                     + f[:, chips + d:chips + d + 1] * partial_in[d].astype(F32)).astype(BF16)

    def p_start(i, c):
        i = (5 * i) % chips
        p_copy(((x + i // SIDE) % SIDE) * SIDE + (y + i % SIDE) % SIDE, chip).start()
        return c

    lax.fori_loop(1, chips, p_start, 0)
    parts[chip] = merged[chip]
    tops_all[chip] = tops_out[chip]

    def t_wait(i, c):
        s = (chip + i) % chips
        t_copy(s, s).wait_recv()
        return c

    lax.fori_loop(1, chips, t_wait, 0)
    top = tops_all[:, 0, :]
    f = jnp.exp2(top - jnp.max(top, axis=0, keepdims=True))
    f = columns(f / jnp.sum(f, axis=0, keepdims=True))

    def p_wait(i, c):
        s = (chip + i) % chips
        p_copy(s, s).wait_recv()
        return c

    lax.fori_loop(1, chips, p_wait, 0)
    acc = jnp.zeros((128, width), F32)
    for s in range(chips):
        acc += f[:, s:s + 1] * parts[s].astype(F32)
    flat[...] = acc
    pair_rows = 2 * own
    here = pl.ds(chip * pair_rows, pair_rows)
    for h in range(half):
        attended[core, here, h * width:(h + 1) * width] = flat[pl.ds(h, pair_rows, stride=half), :].astype(BF16)

    def at_copy(d, s):
        at = pl.ds(s * pair_rows, pair_rows)
        return remote(attended.at[core, at], attended.at[core, at], ag2_send.at[d], ag2_recv.at[s], (row, 2 * d + core))

    def at_relay(s, c):
        at = pl.ds(s * pair_rows, pair_rows)
        return remote(attended.at[c, at], attended.at[c, at], fw2_send.at[s], fw2_recv.at[s], partner)

    spread(at_copy, None, at_relay)
    cols = half * width
    terms[...] = (lax.dot_general(attended[0], wo[:, :cols], NT, preferred_element_type=F32)
                  + lax.dot_general(attended[1], wo[:, cols:], NT, preferred_element_type=F32))
    out_rows = out_ref.shape[0]

    def z_copy(z, s):
        return remote(terms.at[pl.ds(z * out_rows, out_rows)], summed.at[s], z_send.at[z], z_recv.at[s], (z, me))

    for i in range(1, planes):
        z_copy((row + i) % planes, row).start()

    def pair_sent(d, c):
        pair_copy(d).wait_send()
        return c

    lax.fori_loop(0, chips, pair_sent, 0)
    for o in (1, 2, 3):
        a_copy((x + o) % SIDE, x).wait_send()
        for i in range(SIDE):
            b_copy((y + o) % SIDE, i, y).wait_send()
        a2_copy((y + o) % SIDE, y).wait_send()
        b2_copy((x + o) % SIDE, x).wait_send()

    def ent_sent(i, c):
        ent_copy((me + i) % peers, me).wait_send()
        return c

    lax.fori_loop(1, peers, ent_sent, 0)
    spread_end(q_copy, q_relay)
    for copy in x_copies:
        copy.wait_send()

    def tp_sent(i, c):
        d = (chip + i) % chips
        t_copy(d, chip).wait_send()
        p_copy(d, chip).wait_send()
        return c

    lax.fori_loop(1, chips, tp_sent, 0)
    spread_end(at_copy, at_relay)

    result = terms[pl.ds(row * out_rows, out_rows), :]
    for i in range(1, planes):
        z = (row + i) % planes
        z_copy(z, z).wait_recv()
        result += summed[z]
    out_ref[...] = result.astype(BF16)
    for i in range(1, planes):
        z_copy((row + i) % planes, row).wait_send()


def run(ht, w, dt, up, gain, freq, holder, index, used, tenant, held, k, v, wo, peers, planes):
    rows, wide, width = ht.shape[1], w.shape[1], gain.shape[1]
    own = rows // peers
    cap = 2 * own * holder.shape[1] // peers
    chips = peers // 2
    heads = wide // width
    blocks, toks, _ = k.shape
    slots = peers * cap
    count = -(-(slots // GROUP + blocks * (GROUP - 1) // GROUP) // UNROLL) * UNROLL
    positions = count * GROUP
    wide_a = (wide + 128) // 256 * 128 + 128
    wide_b = wide + 128 - wide_a
    cols = wo.shape[0]
    vm = pltpu.VMEM
    dma = pltpu.SemaphoreType.DMA
    args = (ht, w, dt, up, gain, freq, holder, index, used, tenant, held, k, v, wo)
    return pl.pallas_call(
        kernel,
        out_shape=jax.ShapeDtypeStruct((rows // planes, cols), BF16),
        in_specs=[pl.BlockSpec(memory_space=pltpu.HBM)] * len(args),
        out_specs=pl.BlockSpec(memory_space=pltpu.VMEM),
        scratch_shapes=[vm(a.shape, a.dtype) for a in args[:11]] + [
            pltpu.SMEM(tenant.shape, I32), pltpu.SMEM(held.shape, I32),
            vm(k.shape, BF16), vm(v.shape, BF16), vm(wo.shape, BF16),
            vm((rows, wide + 128), F32), vm((chips, own, wide + 128), F32),
            vm((SIDE, SIDE, own, wide_a), F32), vm((SIDE, SIDE, own, wide_b), F32),
            vm((SIDE, SIDE, own, wide_a), F32), vm((SIDE, SIDE, own, wide_b), F32),
            vm((SIDE, own, wide_a), F32), vm((SIDE, own, wide_b), F32),
            vm((SIDE, own, wide_a), F32), vm((SIDE, own, wide_b), F32),
            vm((own, wide + 128), F32), vm((128 // up.shape[1], up.shape[1], 128), F32), vm((own, heads, width), F32),
            vm((slots, 128), BF16), vm((slots, 128), BF16), vm((8, positions), I32), vm((8, slots), I32),
            pltpu.SMEM((8, positions), I32), pltpu.SMEM((8, slots), I32),
            vm((rows, heads, width), BF16),
            vm((positions, 2, heads // 2, width), F32), vm((positions, 2, heads // 2, width), F32),
            vm((2, chips, 128, width), BF16), vm((2, chips, 128), F32),
            vm((chips, 128, width), BF16), vm((chips, 128), F32),
            vm((chips, 128, width), BF16), vm((chips, 8, 128), F32),
            vm((chips, 128, width), BF16), vm((chips, 8, 128), F32), vm((128, width), F32),
            vm((2, rows, wide // 2), BF16), vm((rows, cols), F32), vm((planes, rows // planes, cols), F32),
            dma((14,)), dma((2 * PIECES,)), dma((2,)), dma((chips,)), dma((chips,)),
            dma((SIDE,)), dma((SIDE,)), dma((SIDE, SIDE)), dma((SIDE, SIDE)),
            dma((SIDE,)), dma((SIDE,)), dma((SIDE,)), dma((SIDE,)),
            dma((peers,)), dma((peers,)), dma((chips,)), dma((chips,)), dma((chips,)), dma((chips,)),
            dma((2,)), dma((2,)), dma((chips,)), dma((chips,)), dma((chips,)), dma((chips,)),
            dma((chips,)), dma((chips,)), dma((chips,)), dma((chips,)), dma((planes,)), dma((planes,)),
        ],
        compiler_params=pltpu.CompilerParams(
            vmem_limit_bytes=62 * 2**20, collective_id=0, has_side_effects=True),
        name="decode",
    )(*args)


def local(hidden, query_weight, adapter_down_weight, adapter_up_weight, query_norm_gain, paged_key_cache,
          paged_value_cache, output_weight, holder, holder_block_index, block_used_length, tenant, tenant_adapter):
    peers, planes = lax.axis_size("kv"), lax.axis_size("row")
    count, _, rank = adapter_down_weight.shape
    width = query_norm_gain.shape[0]
    blocks, toks, kv_heads, _ = paged_key_cache.shape
    half = width // 2
    freq = ROPE_BASE ** (-(jnp.arange(half, dtype=jnp.float32) * 2.0) / width)
    freq = jnp.concatenate([freq, freq])[None, :]
    down = jnp.transpose(adapter_down_weight, (0, 2, 1)).reshape(count * rank, -1)
    pool = (blocks, toks * kv_heads, width)
    return run(hidden.T, query_weight, down, adapter_up_weight, query_norm_gain[None, :], freq, holder,
               holder_block_index, block_used_length, tenant[None, :], tenant_adapter[None, :],
               paged_key_cache.reshape(pool), paged_value_cache.reshape(pool), output_weight.T, peers, planes)


def solution(mesh):
    return jax.shard_map(
        local,
        mesh=mesh,
        in_specs=(
            P(None, "kv"),
            P("kv", "row"),
            P(None, "kv", None),
            P(None, None, "row"),
            P(),
            P("kv", None, "row", None),
            P("kv", None, "row", None),
            P("row", "kv"),
            P("kv", None),
            P("kv", None),
            P("kv", None),
            P(),
            P(),
        ),
        out_specs=P("row", "kv"),
        check_vma=False,
    )
```

```python
import functools
import math

import jax
import jax.numpy as jnp
from jax import lax
from jax.experimental import pallas as pl
from jax.experimental.pallas import tpu as pltpu
from jax.sharding import PartitionSpec as P

NEG = -1e30
F32, BF16, I32 = jnp.float32, jnp.bfloat16, jnp.int32
NT = (((1,), (1,)), ((), ()))
TN = (((0,), (0,)), ((), ()))
TT = (((0,), (1,)), ((), ()))
MESH = pl.DeviceIdType.MESH
PIECES = 4
GROUP = 4
UNROLL = 56
SIDE = 4
ADAPTER_SCALE = 0.5
ROPE_BASE = 1000000.0
EPSILON = 1e-06


def iota(shape, dim):
    return lax.broadcasted_iota(I32, shape, dim)


def flat_row(x):
    rows, n = x.shape
    wide = jnp.concatenate([x.astype(F32)] * rows, axis=1)
    keep = lax.div(iota(wide.shape, 1), n) == iota(wide.shape, 0)
    return jnp.sum(jnp.where(keep, wide, 0.0), axis=0, keepdims=True)


def remote(src, dst, send, recv, device):
    return pltpu.make_async_remote_copy(
        src_ref=src, dst_ref=dst, send_sem=send, recv_sem=recv, device_id=device, device_id_type=MESH)


def entries_by_holder(holder, index, used, me, own, peers, cap):
    dest, index, used = flat_row(holder), flat_row(index), flat_row(used)
    count = dest.shape[1]
    to = dest == iota((peers, count), 0).astype(F32)
    earlier = jnp.where(iota((count, count), 0) < iota((count, count), 1), 1.0, 0.0).astype(BF16)
    before = jnp.dot(jnp.where(to, 1.0, 0.0).astype(BF16), earlier, preferred_element_type=F32)
    place = dest * cap + jnp.sum(jnp.where(to, before, 0.0), axis=0, keepdims=True)
    chosen = jnp.where(place == iota((peers * cap, count), 0).astype(F32), 1.0, 0.0).astype(BF16)
    sub = iota((128, count), 0)
    from_row = (me * own + lax.div(iota((1, count), 1), count // own)).astype(F32)
    fields = jnp.where(sub == 0, index, jnp.where(sub == 1, used, jnp.where(sub == 2, from_row, 0.0)))
    return lax.dot_general(chosen, fields.astype(BF16), NT, preferred_element_type=F32).astype(BF16)


def order_entries(ent, blocks, rows, positions, per_group):
    slots = ent.shape[0]
    entf = ent.astype(F32)
    pick = jnp.where(iota((16, 128), 0) == iota((16, 128), 1), 1.0, 0.0).astype(BF16)
    ent_t = lax.dot_general(pick, ent, NT, preferred_element_type=F32)
    blk_r, len_r, row_r = ent_t[0:1], ent_t[1:2], ent_t[2:3]
    valid_c = entf[:, 1:2] > 0
    key_c = jnp.where(valid_c, entf[:, 0:1], 999.0)
    key_r = jnp.where(len_r > 0, blk_r, 999.0)
    earlier = iota((slots, slots), 1) < iota((slots, slots), 0)
    within = jnp.sum(jnp.where((key_c == key_r) & earlier, 1.0, 0.0), axis=1, keepdims=True)
    block_of = iota((blocks, slots), 0).astype(F32) == key_r
    count = jnp.sum(jnp.where(block_of, 1.0, 0.0), axis=1, keepdims=True)
    chunks = jnp.floor((count + (GROUP - 1)) * (1.0 / GROUP))
    below = jnp.where(iota((blocks, blocks), 1) < iota((blocks, blocks), 0), 1.0, 0.0).astype(BF16)
    first = jnp.dot(below, jnp.broadcast_to(chunks, (blocks, 128)).astype(BF16), preferred_element_type=F32)
    own_block = jnp.where(key_c == iota((slots, blocks), 1).astype(F32), 1.0, 0.0).astype(BF16)
    first_c = jnp.dot(own_block, first.astype(BF16), preferred_element_type=F32)[:, 0:1]
    major = jnp.floor(within * (1.0 / GROUP))
    chunk_c, seat_c = first_c + major, within - major * GROUP
    place = jnp.where(valid_c, chunk_c * GROUP + seat_c, -1.0)
    sub = iota((16, slots), 0)
    fields = jnp.where(sub == 0, blk_r, jnp.where(sub == 1, len_r, jnp.where(sub == 2, row_r, 0.0))).astype(BF16)
    chosen = jnp.where(place == iota((slots, positions), 1).astype(F32), 1.0, 0.0).astype(BF16)
    table = jnp.dot(fields, chosen, preferred_element_type=F32)[0:8]
    sub = iota(table.shape, 0)
    table = table.astype(I32)
    table = jnp.clip(table, 0, jnp.where(sub == 0, blocks - 1, jnp.where(sub == 1, 1 << 16, rows - 1)))
    lane = iota((slots, 128), 1)
    seats = jnp.where(lane == 0, chunk_c, jnp.where(lane == 1, seat_c, 0.0)).astype(BF16)
    seats = lax.dot_general(pick, seats, NT, preferred_element_type=F32)
    where_r = jnp.where(len_r > 0, seats[0:1] * GROUP + seats[1:2], 0.0)
    local_r = row_r - (lax.div(iota((1, slots), 1), per_group) * 16).astype(F32)
    local_r = jnp.where(len_r > 0, local_r, -1.0)
    by_slot = jnp.clip(jnp.where(iota((8, slots), 0) == 0, where_r, local_r).astype(I32), -1, positions - 1)
    by_slot = jnp.where(iota((8, slots), 0) == 0, jnp.maximum(by_slot, 0), by_slot)
    return table, by_slot


def kernel(ht_h, w_h, dt_h, up_h, gain_h, freq_h, holder_h, index_h, used_h, tenant_h, held_h, k_h, v_h, wo_h,
           out_ref,
           ht, w, dt, up, gain, freq, holder, index, used, tenant, held, tenant_s, held_s, kbuf, vbuf, wo, wo_in,
           part, pair, mine_a, mine_b, land_a, land_b, sum_a, sum_b, end_a, end_b, total, low_t, turned,
           ent_send, ent, tab_v, slot_v, tab, slot_s, q, o_st, e_st,
           partial, tops, partial_in, tops_in, merged, tops_out, parts, tops_all, flat, attended, terms, summed,
           in_sem, kv_sem, tab_sem, pair_send, pair_recv, a_send, a_recv, b_send, b_recv, a2_send, a2_recv,
           b2_send, b2_recv, en_send, en_recv, ag_send, ag_recv, fw_send, fw_recv,
           wo_send, wo_recv, x_send, x_recv, p_send, p_recv, t_send, t_recv, ag2_send, ag2_recv, z_send, z_recv):
    row, me = lax.axis_index("row"), lax.axis_index("kv")
    peers, planes = lax.axis_size("kv"), lax.axis_size("row")
    chips = peers // 2
    chip, core = me // 2, me % 2
    x, y = chip // SIDE, chip % SIDE
    partner = (row, 2 * chip + 1 - core)
    wide = w.shape[1]
    rows, heads, width = q.shape
    own = rows // peers
    cap = ent.shape[0] // peers
    blocks, toks, _ = kbuf.shape
    wide_a = mine_a.shape[3]
    barrier = pltpu.get_barrier_semaphore()

    def greet(i, c):
        pl.semaphore_signal(barrier, inc=1, device_id=(row, (me + i) % peers), device_id_type=MESH)
        return c

    def greet_plane(i, c):
        pl.semaphore_signal(barrier, inc=1, device_id=((row + i) % planes, me), device_id_type=MESH)
        pl.semaphore_signal(barrier, inc=1, device_id=((row + i) % planes, partner[1]), device_id_type=MESH)
        return c

    lax.fori_loop(1, peers, greet, 0)
    lax.fori_loop(1, planes, greet_plane, 0)

    loads = [pltpu.make_async_copy(src, dst, in_sem.at[i]) for i, (src, dst) in enumerate((
        (ht_h, ht), (w_h, w), (holder_h, holder), (index_h, index), (used_h, used), (tenant_h, tenant),
        (held_h, held), (dt_h, dt), (tenant_h, tenant_s), (held_h, held_s), (gain_h, gain), (freq_h, freq),
        (up_h, up), (wo_h.at[:, :wide // 2], wo.at[0]), (wo_h.at[:, wide // 2:], wo.at[1])))]
    for copy in loads:
        copy.start()
    step = blocks // PIECES
    pool = []
    for i in range(PIECES):
        at = pl.ds(i * step, step)
        pool += [pltpu.make_async_copy(k_h.at[at], kbuf.at[at], kv_sem.at[2 * i]),
                 pltpu.make_async_copy(v_h.at[at], vbuf.at[at], kv_sem.at[2 * i + 1])]
    for copy in pool:
        copy.start()
    for copy in loads[:8]:
        copy.wait()

    part[:, :wide] = lax.dot_general(ht[...], w[...], TN, preferred_element_type=F32)
    low = lax.dot_general(ht[...], dt[...], TT, preferred_element_type=F32)
    rank = up.shape[1]
    is_tenant = jnp.where(tenant[...] == iota((held.shape[1], rows), 0), 1.0, 0.0).astype(BF16)
    held_b = jnp.broadcast_to(held[...].astype(F32), (16, held.shape[1])).astype(BF16)
    adapter = jnp.dot(held_b, is_tenant, preferred_element_type=F32)[0:8]
    adapter = jnp.transpose(adapter)[:, 0:1].astype(I32)
    low = jnp.where(lax.div(iota(low.shape, 1), rank) == adapter, low, 0.0)
    part[:, wide:] = sum(low[:, 128 * i: 128 * (i + 1)] for i in range(low.shape[1] // 128))
    ent_send[...] = entries_by_holder(holder[...], index[...], used[...], me, own, peers, cap)

    pl.semaphore_wait(barrier, peers - 1 + 2 * (planes - 1))

    def pair_copy(d):
        return remote(part.at[pl.ds((2 * d + 1 - core) * own, own)], pair.at[d],
                      pair_send.at[d], pair_recv.at[d], partner)

    def chip_at(ox, oy):
        return (x + ox) % SIDE, (y + oy) % SIDE

    hops = (2, 1, 3, 0)
    for ox in hops:
        for oy in hops:
            dx, dy = chip_at(ox, oy)
            pair_copy(dx * SIDE + dy).start()

    def a_copy(t, s):
        return remote(mine_a.at[t], land_a.at[s], a_send.at[t], a_recv.at[s], (row, 2 * (t * SIDE + y) + core))

    def b_copy(t, i, s):
        return remote(mine_b.at[t, i], land_b.at[s, i], b_send.at[t, i], b_recv.at[s, i],
                      (row, 2 * (x * SIDE + t) + core))

    for ox in hops:
        for oy in hops:
            dx, dy = chip_at(ox, oy)
            d = dx * SIDE + dy
            pair_copy(d).wait_recv()
            both = part[pl.ds((2 * d + core) * own, own), :] + pair[d]
            mine_a[dx, dy] = both[:, :wide_a]
            mine_b[dy, dx] = both[:, wide_a:]
            if oy:
                b_copy(dy, dx, y).start()
        if ox:
            a_copy(dx, x).start()

    def ent_copy(t, slot):
        return remote(ent_send.at[pl.ds(t * cap, cap)], ent.at[pl.ds(slot * cap, cap)],
                      en_send.at[t], en_recv.at[slot], (row, t))

    def ent_start(i, c):
        ent_copy((me + i) % peers, me).start()
        return c

    lax.fori_loop(1, peers, ent_start, 0)
    at = pl.ds(me * cap, cap)
    ent[at, :] = ent_send[at, :]
    for copy in loads[8:]:
        copy.wait()
    angles = (jnp.sum(used[...], axis=1, keepdims=True) - 1).astype(F32) * freq[...]
    cosine, sine = jnp.cos(angles), jnp.sin(angles)
    sine = jnp.where(iota(sine.shape, 1) < width // 2, -sine, sine)

    wo_copy = remote(wo.at[1 - core], wo_in, wo_send, wo_recv, partner)
    wo_copy.start()

    for copy in pool:
        copy.wait()

    def turn_keys(b, c):
        kbuf[b] = jnp.transpose(kbuf[b].reshape(toks // 2, 2 * width))
        return c

    lax.fori_loop(0, blocks, turn_keys, 0, unroll=4)

    def a2_copy(t, s):
        return remote(sum_a.at[t], end_a.at[s], a2_send.at[t], a2_recv.at[s], (row, 2 * (x * SIDE + t) + core))

    def b2_copy(t, s):
        return remote(sum_b.at[t], end_b.at[s], b2_send.at[t], b2_recv.at[s], (row, 2 * (t * SIDE + y) + core))

    steps = (1, 3, 2)
    for o in steps:
        a_copy((x + SIDE - o) % SIDE, (x + SIDE - o) % SIDE).wait_recv()
    sum_a[...] = mine_a[x] + land_a[(x + 1) % SIDE] + land_a[(x + 2) % SIDE] + land_a[(x + 3) % SIDE]
    for o in (2, 1, 3):
        a2_copy((y + o) % SIDE, y).start()
    for o in steps:
        for i in range(SIDE):
            b_copy((y + SIDE - o) % SIDE, i, (y + SIDE - o) % SIDE).wait_recv()
    sum_b[...] = mine_b[y] + land_b[(y + 1) % SIDE] + land_b[(y + 2) % SIDE] + land_b[(y + 3) % SIDE]
    for o in (2, 1, 3):
        b2_copy((x + o) % SIDE, x).start()

    def ent_wait(i, c):
        t = (me + peers - i) % peers
        ent_copy(t, t).wait_recv()
        return c

    lax.fori_loop(1, peers, ent_wait, 0)
    table, by_slot = order_entries(ent[...], blocks, rows, tab.shape[1], 2 * cap)
    tab_v[...] = table
    slot_v[...] = by_slot
    tables = (pltpu.make_async_copy(tab_v, tab, tab_sem.at[0]), pltpu.make_async_copy(slot_v, slot_s, tab_sem.at[1]))
    for copy in tables:
        copy.start()

    for o in steps:
        a2_copy((y + SIDE - o) % SIDE, (y + SIDE - o) % SIDE).wait_recv()
    total[:, :wide_a] = sum_a[y] + end_a[(y + 1) % SIDE] + end_a[(y + 2) % SIDE] + end_a[(y + 3) % SIDE]
    for o in steps:
        b2_copy((x + SIDE - o) % SIDE, (x + SIDE - o) % SIDE).wait_recv()
    total[:, wide_a:] = sum_b[x] + end_b[(x + 1) % SIDE] + end_b[(x + 2) % SIDE] + end_b[(x + 3) % SIDE]

    low_t[...] = jnp.transpose(
        jnp.concatenate([total[:, wide:], jnp.zeros((128 - own, 128), F32)], axis=0)).reshape(low_t.shape)
    for r in range(own):
        adapter = held_s[0, tenant_s[0, me * own + r]]
        column = low_t[lax.rem(adapter, 128 // rank)][:, r:r + 1]
        more = jnp.sum(column * up[adapter], axis=0, keepdims=True)
        total[r:r + 1, :wide] += ADAPTER_SCALE * more
    gain_r = gain[...]
    for h in range(heads):
        t = total[:, h * width:(h + 1) * width]
        t = t * lax.rsqrt(jnp.mean(t * t, axis=1, keepdims=True) + EPSILON) * gain_r
        turned[:, h, :] = t * cosine + pltpu.roll(t, width // 2, 1) * sine
    q[pl.ds(me * own, own)] = turned[...].astype(BF16)

    def chip_by(i, sign):
        dx, dy = i // SIDE, i % SIDE
        return ((x + sign * dx + SIDE) % SIDE) * SIDE + (y + sign * dy + SIDE) % SIDE

    far = sorted(range(1, chips), key=lambda i: -(min(i // SIDE, SIDE - i // SIDE) + min(i % SIDE, SIDE - i % SIDE)))

    def q_copy(d, s):
        at = pl.ds((2 * s + core) * own, own)
        return remote(q.at[at], q.at[at], ag_send.at[d], ag_recv.at[s], (row, 2 * d + core))

    def q_relay(s, c):
        at = pl.ds((2 * s + c) * own, own)
        return remote(q.at[at], q.at[at], fw_send.at[s], fw_recv.at[s], partner)

    for i in far:
        q_copy(chip_by(i, 1), chip).start()
    q_relay(chip, core).start()

    def turn_values(b, c):
        both = vbuf[b].reshape(toks // 2, 2 * width)
        vbuf[b, :toks // 2] = both[:, :width]
        vbuf[b, toks // 2:] = both[:, width:]
        return c

    lax.fori_loop(0, blocks, turn_values, 0, unroll=4)

    def pair_sent(d, c):
        pair_copy(d).wait_send()
        return c

    lax.fori_loop(0, chips, pair_sent, 0)
    for o in (1, 2, 3):
        a_copy((x + o) % SIDE, x).wait_send()
        for i in range(SIDE):
            b_copy((y + o) % SIDE, i, y).wait_send()
        a2_copy((y + o) % SIDE, y).wait_send()
        b2_copy((x + o) % SIDE, x).wait_send()
    for copy in tables:
        copy.wait()

    for i in far:
        s = chip_by(i, -1)
        q_copy(s, s).wait_recv()
        q_relay(s, core).start()

    def q_landed(d, c):
        q_relay(d, 1 - core).wait_recv()
        return c

    lax.fori_loop(0, chips, q_landed, 0)

    coef = math.log2(math.e) / math.sqrt(width)
    half = heads // 2
    col = iota((heads, toks // 2), 1)
    upper = iota((heads, width), 0) < half
    none = jnp.zeros((heads, width), BF16)

    def chunk(c):
        base = c * GROUP
        b = tab[0, base]
        qs = [q[tab[2, base + g]] for g in range(GROUP)]
        qs = jnp.concatenate([jnp.concatenate(
            [jnp.where(upper, one, none), jnp.where(upper, none, one)], axis=1) for one in qs], axis=0)
        s = jnp.dot(qs, kbuf[b], preferred_element_type=F32)
        s = jnp.concatenate(
            [jnp.where(col < tab[1, base + g], s[heads * g: heads * (g + 1)], NEG) for g in range(GROUP)], axis=0)
        m = jnp.max(s, axis=1, keepdims=True)
        wt = jnp.exp2((s - m) * coef)
        l = jnp.sum(wt, axis=1, keepdims=True)
        vs = jnp.concatenate([vbuf[b, :toks // 2], vbuf[b, toks // 2:]], axis=1)
        o = jnp.dot(wt.astype(BF16), vs, preferred_element_type=F32).reshape(GROUP, 2, half, 2 * width)
        o = jnp.concatenate([o[:, 0:1, :, :width], o[:, 1:2, :, width:]], axis=1).reshape(GROUP * heads, width) / l
        e = jnp.broadcast_to(m * coef + jnp.log2(l), o.shape)
        return o.reshape(GROUP, 2, half, width), e.reshape(GROUP, 2, half, width)

    def chunks(i, c):
        done = [chunk(i * UNROLL + u) for u in range(UNROLL)]
        for u in range(UNROLL):
            o, e = done[u]
            at = pl.ds((i * UNROLL + u) * GROUP, GROUP)
            o_st[at] = o
            e_st[at] = e
        return c

    lax.fori_loop(0, tab.shape[1] // (GROUP * UNROLL), chunks, 0)

    lane = iota((half, 128), 1)
    same_head = (lane & (half - 1)) == iota((half, 128), 0)
    lane_row = jnp.where(same_head, lax.div(lane, half), -2)
    slots = 2 * cap

    def merge(d, hv):
        tops_of, outs = [], []
        for p in range(slots):
            at = slot_s[0, d * slots + p]
            tops_of.append(jnp.where(lane_row == slot_s[1, d * slots + p], e_st[at, hv], NEG))
            outs.append(o_st[at, hv])
        es = jnp.concatenate(tops_of, axis=0)
        top = jnp.max(es, axis=0, keepdims=True)
        f = jnp.exp2(es - top)
        l = jnp.sum(f, axis=0, keepdims=True)
        f = (f * (1.0 / l)).astype(BF16)
        os = jnp.concatenate(outs, axis=0).astype(BF16)
        return lax.dot_general(f, os, TN, preferred_element_type=F32).astype(BF16), top + jnp.log2(l)

    many = chips // PIECES

    def x_copy(i):
        at = pl.ds(i * many, many)
        return remote(partial.at[1 - core, at], partial_in.at[at], x_send.at[i], x_recv.at[i], partner)

    tops_copy = remote(tops.at[1 - core], tops_in, x_send.at[PIECES], x_recv.at[PIECES], partner)

    for hv in (1 - core, core):
        def merges(i, c, hv=hv):
            done = [merge(i * many + u, hv) for u in range(many)]
            for u in range(many):
                partial[hv, i * many + u] = done[u][0]
                tops[hv, pl.ds(i * many + u, 1), :] = done[u][1]
            return c

        def merges_sent(i, c):
            merges(i, c)
            x_copy(i).start()
            return c

        if hv is not core:
            lax.fori_loop(0, PIECES, merges_sent, 0)
            tops_copy.start()
        else:
            lax.fori_loop(0, PIECES, merges, 0)

    def columns(fs):
        n = fs.shape[0]
        return jnp.transpose(jnp.concatenate([fs, jnp.zeros((128 - n, 128), F32)], axis=0))

    order = far + [0]
    tops_copy.wait_recv()
    t0 = jnp.concatenate([tops[core, pl.ds(chip_by(i, 1), 1), :] for i in order], axis=0)
    t1 = jnp.concatenate([tops_in[pl.ds(chip_by(i, 1), 1), :] for i in order], axis=0)
    top = jnp.maximum(t0, t1)
    f0, f1 = jnp.exp2(t0 - top), jnp.exp2(t1 - top)
    l = f0 + f1
    over = top + jnp.log2(l)
    for k in range(chips):
        tops_out[k] = jnp.broadcast_to(over[k:k + 1], (8, 128))
    f = columns(jnp.concatenate([f0 / l, f1 / l], axis=0))

    def t_copy(k, d, s):
        return remote(tops_out.at[k], tops_all.at[s], t_send.at[k], t_recv.at[s], (row, 2 * d + core))

    def p_copy(k, d, s):
        return remote(merged.at[k], parts.at[s], p_send.at[k], p_recv.at[s], (row, 2 * d + core))

    for k, i in enumerate(order):
        if i:
            t_copy(k, chip_by(i, 1), chip).start()
    for i in range(PIECES):
        x_copy(i).wait_recv()
    for k, i in enumerate(order):
        d = chip_by(i, 1)
        both = (f[:, k:k + 1] * partial[core, d].astype(F32)
                + f[:, chips + k:chips + k + 1] * partial_in[d].astype(F32)).astype(BF16)
        if i:
            merged[k] = both
            p_copy(k, d, chip).start()
        else:
            parts[chip] = both
            tops_all[chip] = tops_out[k]

    def ent_sent(i, c):
        ent_copy((me + i) % peers, me).wait_send()
        return c

    lax.fori_loop(1, peers, ent_sent, 0)

    def q_sent(i, c):
        q_copy((chip + i) % chips, chip).wait_send()
        return c

    lax.fori_loop(1, chips, q_sent, 0)

    def q_relayed(d, c):
        q_relay(d, core).wait_send()
        return c

    lax.fori_loop(0, chips, q_relayed, 0)
    for i in range(PIECES):
        x_copy(i).wait_send()
    tops_copy.wait_send()
    wo_copy.wait()

    for i in far[::-1]:
        s = chip_by(i, -1)
        t_copy(0, s, s).wait_recv()
    top = tops_all[:, 0, :]
    f = jnp.exp2(top - jnp.max(top, axis=0, keepdims=True))
    f = columns(f / jnp.sum(f, axis=0, keepdims=True))
    for i in far[::-1]:
        s = chip_by(i, -1)
        p_copy(0, s, s).wait_recv()
    acc = jnp.zeros((128, width), F32)
    for s in range(chips):
        acc += f[:, s:s + 1] * parts[s].astype(F32)
    flat[...] = acc
    pair_rows = 2 * own
    here = pl.ds(chip * pair_rows, pair_rows)
    for h in range(half):
        attended[here, h * width:(h + 1) * width] = flat[pl.ds(h, pair_rows, stride=half), :].astype(BF16)

    def at_copy(d, s):
        at = pl.ds(s * pair_rows, pair_rows)
        return remote(attended.at[at], attended.at[at], ag2_send.at[d], ag2_recv.at[s], (row, 2 * d + core))

    for i in far:
        at_copy(chip_by(i, 1), chip).start()
    for k, i in enumerate(far):
        t_copy(k, chip_by(i, 1), chip).wait_send()
        p_copy(k, chip_by(i, 1), chip).wait_send()
    for i in far[::-1]:
        s = chip_by(i, -1)
        at_copy(s, s).wait_recv()
    out_rows = out_ref.shape[0]

    def z_copy(c, z, s):
        return remote(terms.at[c, pl.ds(z * out_rows, out_rows)], summed.at[c, s], z_send.at[c, z], z_recv.at[c, s],
                      (z, partner[1] if c else me))

    terms[1] = lax.dot_general(attended[...], wo_in[...], NT, preferred_element_type=F32)
    for i in (2, 1, 3, 0):
        z_copy(1, (row + i) % planes, row).start()
    terms[0] = lax.dot_general(attended[...], wo[core], NT, preferred_element_type=F32)
    for i in (2, 1, 3):
        z_copy(0, (row + i) % planes, row).start()
    for i in far:
        at_copy(chip_by(i, 1), chip).wait_send()

    result = terms[0, pl.ds(row * out_rows, out_rows), :]
    for c in (1, 0):
        for i in range(c ^ 1, planes):
            z = (row + i) % planes
            z_copy(c, z, z).wait_recv()
            result += summed[c, z]
    out_ref[...] = result.astype(BF16)
    for c in (1, 0):
        for i in range(c ^ 1, planes):
            z_copy(c, (row + i) % planes, row).wait_send()


def run(ht, w, dt, up, gain, freq, holder, index, used, tenant, held, k, v, wo, peers, planes):
    rows, wide, width = ht.shape[1], w.shape[1], gain.shape[1]
    own = rows // peers
    cap = 2 * own * holder.shape[1] // peers
    chips = peers // 2
    heads = wide // width
    blocks, toks, _ = k.shape
    slots = peers * cap
    count = -(-(slots // GROUP + blocks * (GROUP - 1) // GROUP) // UNROLL) * UNROLL
    positions = count * GROUP
    wide_a = (wide + 128) // 256 * 128 + 128
    wide_b = wide + 128 - wide_a
    cols = wo.shape[0]
    vm = pltpu.VMEM
    dma = pltpu.SemaphoreType.DMA
    args = (ht, w, dt, up, gain, freq, holder, index, used, tenant, held, k, v, wo)
    return pl.pallas_call(
        kernel,
        out_shape=jax.ShapeDtypeStruct((rows // planes, cols), BF16),
        in_specs=[pl.BlockSpec(memory_space=pltpu.HBM)] * len(args),
        out_specs=pl.BlockSpec(memory_space=pltpu.VMEM),
        scratch_shapes=[vm(a.shape, a.dtype) for a in args[:11]] + [
            pltpu.SMEM(tenant.shape, I32), pltpu.SMEM(held.shape, I32),
            vm(k.shape, BF16), vm(v.shape, BF16), vm((2, cols, wide // 2), BF16), vm((cols, wide // 2), BF16),
            vm((rows, wide + 128), F32), vm((chips, own, wide + 128), F32),
            vm((SIDE, SIDE, own, wide_a), F32), vm((SIDE, SIDE, own, wide_b), F32),
            vm((SIDE, SIDE, own, wide_a), F32), vm((SIDE, SIDE, own, wide_b), F32),
            vm((SIDE, own, wide_a), F32), vm((SIDE, own, wide_b), F32),
            vm((SIDE, own, wide_a), F32), vm((SIDE, own, wide_b), F32),
            vm((own, wide + 128), F32), vm((128 // up.shape[1], up.shape[1], 128), F32), vm((own, heads, width), F32),
            vm((slots, 128), BF16), vm((slots, 128), BF16), vm((8, positions), I32), vm((8, slots), I32),
            pltpu.SMEM((8, positions), I32), pltpu.SMEM((8, slots), I32),
            vm((rows, heads, width), BF16),
            vm((positions, 2, heads // 2, width), F32), vm((positions, 2, heads // 2, width), F32),
            vm((2, chips, 128, width), BF16), vm((2, chips, 128), F32),
            vm((chips, 128, width), BF16), vm((chips, 128), F32),
            vm((chips, 128, width), BF16), vm((chips, 8, 128), F32),
            vm((chips, 128, width), BF16), vm((chips, 8, 128), F32), vm((128, width), F32),
            vm((rows, wide // 2), BF16), vm((2, rows, cols), F32), vm((2, planes, rows // planes, cols), F32),
            dma((15,)), dma((2 * PIECES,)), dma((2,)), dma((chips,)), dma((chips,)),
            dma((SIDE,)), dma((SIDE,)), dma((SIDE, SIDE)), dma((SIDE, SIDE)),
            dma((SIDE,)), dma((SIDE,)), dma((SIDE,)), dma((SIDE,)),
            dma((peers,)), dma((peers,)), dma((chips,)), dma((chips,)), dma((chips,)), dma((chips,)),
            dma, dma, dma((PIECES + 1,)), dma((PIECES + 1,)), dma((chips,)), dma((chips,)), dma((chips,)), dma((chips,)),
            dma((chips,)), dma((chips,)), dma((2, planes)), dma((2, planes)),
        ],
        compiler_params=pltpu.CompilerParams(
            vmem_limit_bytes=62 * 2**20, collective_id=0, has_side_effects=True),
        name="decode",
    )(*args)


def local(hidden, query_weight, adapter_down_weight, adapter_up_weight, query_norm_gain, paged_key_cache,
          paged_value_cache, output_weight, holder, holder_block_index, block_used_length, tenant, tenant_adapter):
    peers, planes = lax.axis_size("kv"), lax.axis_size("row")
    count, _, rank = adapter_down_weight.shape
    width = query_norm_gain.shape[0]
    blocks, toks, kv_heads, _ = paged_key_cache.shape
    half = width // 2
    freq = ROPE_BASE ** (-(jnp.arange(half, dtype=jnp.float32) * 2.0) / width)
    freq = jnp.concatenate([freq, freq])[None, :]
    down = jnp.transpose(adapter_down_weight, (0, 2, 1)).reshape(count * rank, -1)
    pool = (blocks, toks * kv_heads, width)
    return run(hidden.T, query_weight, down, adapter_up_weight, query_norm_gain[None, :], freq, holder,
               holder_block_index, block_used_length, tenant[None, :], tenant_adapter[None, :],
               paged_key_cache.reshape(pool), paged_value_cache.reshape(pool), output_weight.T, peers, planes)


def solution(mesh):
    return jax.shard_map(
        local,
        mesh=mesh,
        in_specs=(
            P(None, "kv"),
            P("kv", "row"),
            P(None, "kv", None),
            P(None, None, "row"),
            P(),
            P("kv", None, "row", None),
            P("kv", None, "row", None),
            P("row", "kv"),
            P("kv", None),
            P("kv", None),
            P("kv", None),
            P(),
            P(),
        ),
        out_specs=P("row", "kv"),
        check_vma=False,
    )
```

```python
import functools
import math

import jax
import jax.numpy as jnp
from jax import lax
from jax.experimental import pallas as pl
from jax.experimental.pallas import tpu as pltpu
from jax.sharding import PartitionSpec as P

NEG = -1e30
F32, BF16, I32 = jnp.float32, jnp.bfloat16, jnp.int32
NT = (((1,), (1,)), ((), ()))
TN = (((0,), (0,)), ((), ()))
TT = (((0,), (1,)), ((), ()))
MESH = pl.DeviceIdType.MESH
PIECES = 4
GROUP = 4
UNROLL = 224
SIDE = 4
ADAPTER_SCALE = 0.5
ROPE_BASE = 1000000.0
EPSILON = 1e-06


def iota(shape, dim):
    return lax.broadcasted_iota(I32, shape, dim)


def flat_row(x):
    rows, n = x.shape
    wide = jnp.concatenate([x.astype(F32)] * rows, axis=1)
    keep = lax.div(iota(wide.shape, 1), n) == iota(wide.shape, 0)
    return jnp.sum(jnp.where(keep, wide, 0.0), axis=0, keepdims=True)


def remote(src, dst, send, recv, device):
    return pltpu.make_async_remote_copy(
        src_ref=src, dst_ref=dst, send_sem=send, recv_sem=recv, device_id=device, device_id_type=MESH)


def entries_by_holder(holder, index, used, me, own, peers, cap):
    dest, index, used = flat_row(holder), flat_row(index), flat_row(used)
    count = dest.shape[1]
    to = dest == iota((peers, count), 0).astype(F32)
    earlier = jnp.where(iota((count, count), 0) < iota((count, count), 1), 1.0, 0.0).astype(BF16)
    before = jnp.dot(jnp.where(to, 1.0, 0.0).astype(BF16), earlier, preferred_element_type=F32)
    place = dest * cap + jnp.sum(jnp.where(to, before, 0.0), axis=0, keepdims=True)
    chosen = jnp.where(place == iota((peers * cap, count), 0).astype(F32), 1.0, 0.0).astype(BF16)
    sub = iota((128, count), 0)
    from_row = (me * own + lax.div(iota((1, count), 1), count // own)).astype(F32)
    fields = jnp.where(sub == 0, index, jnp.where(sub == 1, used, jnp.where(sub == 2, from_row, 0.0)))
    return lax.dot_general(chosen, fields.astype(BF16), NT, preferred_element_type=F32).astype(BF16)


def order_entries(ent, blocks, rows, positions, per_group):
    slots = ent.shape[0]
    entf = ent.astype(F32)
    pick = jnp.where(iota((16, 128), 0) == iota((16, 128), 1), 1.0, 0.0).astype(BF16)
    ent_t = lax.dot_general(pick, ent, NT, preferred_element_type=F32)
    blk_r, len_r, row_r = ent_t[0:1], ent_t[1:2], ent_t[2:3]
    valid_c = entf[:, 1:2] > 0
    key_c = jnp.where(valid_c, entf[:, 0:1], 999.0)
    key_r = jnp.where(len_r > 0, blk_r, 999.0)
    earlier = iota((slots, slots), 1) < iota((slots, slots), 0)
    within = jnp.sum(jnp.where((key_c == key_r) & earlier, 1.0, 0.0), axis=1, keepdims=True)
    block_of = iota((blocks, slots), 0).astype(F32) == key_r
    count = jnp.sum(jnp.where(block_of, 1.0, 0.0), axis=1, keepdims=True)
    chunks = jnp.floor((count + (GROUP - 1)) * (1.0 / GROUP))
    below = jnp.where(iota((blocks, blocks), 1) < iota((blocks, blocks), 0), 1.0, 0.0).astype(BF16)
    first = jnp.dot(below, jnp.broadcast_to(chunks, (blocks, 128)).astype(BF16), preferred_element_type=F32)
    own_block = jnp.where(key_c == iota((slots, blocks), 1).astype(F32), 1.0, 0.0).astype(BF16)
    first_c = jnp.dot(own_block, first.astype(BF16), preferred_element_type=F32)[:, 0:1]
    major = jnp.floor(within * (1.0 / GROUP))
    chunk_c, seat_c = first_c + major, within - major * GROUP
    place = jnp.where(valid_c, chunk_c * GROUP + seat_c, -1.0)
    sub = iota((16, slots), 0)
    fields = jnp.where(sub == 0, blk_r, jnp.where(sub == 1, len_r, jnp.where(sub == 2, row_r, 0.0))).astype(BF16)
    chosen = jnp.where(place == iota((slots, positions), 1).astype(F32), 1.0, 0.0).astype(BF16)
    table = jnp.dot(fields, chosen, preferred_element_type=F32)[0:8]
    sub = iota(table.shape, 0)
    table = table.astype(I32)
    table = jnp.clip(table, 0, jnp.where(sub == 0, blocks - 1, jnp.where(sub == 1, 1 << 16, rows - 1)))
    lane = iota((slots, 128), 1)
    seats = jnp.where(lane == 0, chunk_c, jnp.where(lane == 1, seat_c, 0.0)).astype(BF16)
    seats = lax.dot_general(pick, seats, NT, preferred_element_type=F32)
    where_r = jnp.where(len_r > 0, seats[0:1] * GROUP + seats[1:2], 0.0)
    local_r = row_r - (lax.div(iota((1, slots), 1), per_group) * 16).astype(F32)
    local_r = jnp.where(len_r > 0, local_r, -1.0)
    by_slot = jnp.clip(jnp.where(iota((8, slots), 0) == 0, where_r, local_r).astype(I32), -1, positions - 1)
    by_slot = jnp.where(iota((8, slots), 0) == 0, jnp.maximum(by_slot, 0), by_slot)
    return table, by_slot


def kernel(ht_h, w_h, dt_h, up_h, gain_h, freq_h, holder_h, index_h, used_h, tenant_h, held_h, k_h, v_h, wo_h,
           out_ref,
           ht, w, dt, up, gain, freq, holder, index, used, tenant, held, tenant_s, held_s, kbuf, vbuf, wo, wo_in,
           part, pair, mine_a, mine_b, land_a, land_b, sum_a, sum_b, end_a, end_b, total, low_t, turned,
           ent_send, ent, tab_v, slot_v, tab, slot_s, q, o_st, e_st,
           partial, tops, partial_in, tops_in, merged, tops_out, parts, tops_all, flat, attended, terms, summed,
           in_sem, kv_sem, tab_sem, pair_send, pair_recv, a_send, a_recv, b_send, b_recv, a2_send, a2_recv,
           b2_send, b2_recv, en_send, en_recv, ag_send, ag_recv, fw_send, fw_recv,
           wo_send, wo_recv, x_send, x_recv, p_send, p_recv, t_send, t_recv, ag2_send, ag2_recv, z_send, z_recv):
    row, me = lax.axis_index("row"), lax.axis_index("kv")
    peers, planes = lax.axis_size("kv"), lax.axis_size("row")
    chips = peers // 2
    chip, core = me // 2, me % 2
    x, y = chip // SIDE, chip % SIDE
    partner = (row, 2 * chip + 1 - core)
    wide = w.shape[1]
    rows, heads, width = q.shape
    own = rows // peers
    cap = ent.shape[0] // peers
    blocks, toks, _ = kbuf.shape
    wide_a = mine_a.shape[3]
    barrier = pltpu.get_barrier_semaphore()

    def greet(i, c):
        pl.semaphore_signal(barrier, inc=1, device_id=(row, (me + i) % peers), device_id_type=MESH)
        return c

    def greet_plane(i, c):
        pl.semaphore_signal(barrier, inc=1, device_id=((row + i) % planes, me), device_id_type=MESH)
        pl.semaphore_signal(barrier, inc=1, device_id=((row + i) % planes, partner[1]), device_id_type=MESH)
        return c

    lax.fori_loop(1, peers, greet, 0)
    lax.fori_loop(1, planes, greet_plane, 0)

    loads = [pltpu.make_async_copy(src, dst, in_sem.at[i]) for i, (src, dst) in enumerate((
        (ht_h, ht), (w_h, w), (holder_h, holder), (index_h, index), (used_h, used), (tenant_h, tenant),
        (held_h, held), (dt_h, dt), (tenant_h, tenant_s), (held_h, held_s), (gain_h, gain), (freq_h, freq),
        (up_h, up), (wo_h.at[:, :wide // 2], wo.at[0]), (wo_h.at[:, wide // 2:], wo.at[1])))]
    for copy in loads:
        copy.start()
    step = blocks // PIECES
    pool = []
    for i in range(PIECES):
        at = pl.ds(i * step, step)
        pool += [pltpu.make_async_copy(k_h.at[at], kbuf.at[at], kv_sem.at[2 * i]),
                 pltpu.make_async_copy(v_h.at[at], vbuf.at[at], kv_sem.at[2 * i + 1])]
    for copy in pool:
        copy.start()
    for copy in loads[:8]:
        copy.wait()

    part[:, :wide] = lax.dot_general(ht[...], w[...], TN, preferred_element_type=F32)
    low = lax.dot_general(ht[...], dt[...], TT, preferred_element_type=F32)
    rank = up.shape[1]
    is_tenant = jnp.where(tenant[...] == iota((held.shape[1], rows), 0), 1.0, 0.0).astype(BF16)
    held_b = jnp.broadcast_to(held[...].astype(F32), (16, held.shape[1])).astype(BF16)
    adapter = jnp.dot(held_b, is_tenant, preferred_element_type=F32)[0:8]
    adapter = jnp.transpose(adapter)[:, 0:1].astype(I32)
    low = jnp.where(lax.div(iota(low.shape, 1), rank) == adapter, low, 0.0)
    part[:, wide:] = sum(low[:, 128 * i: 128 * (i + 1)] for i in range(low.shape[1] // 128))

    pl.semaphore_wait(barrier, peers - 1 + 2 * (planes - 1))

    def pair_copy(d):
        return remote(part.at[pl.ds((2 * d + 1 - core) * own, own)], pair.at[d],
                      pair_send.at[d], pair_recv.at[d], partner)

    def chip_at(ox, oy):
        return (x + ox) % SIDE, (y + oy) % SIDE

    hops = (2, 1, 3, 0)
    for ox in hops:
        for oy in hops:
            dx, dy = chip_at(ox, oy)
            pair_copy(dx * SIDE + dy).start()

    ent_send[...] = entries_by_holder(holder[...], index[...], used[...], me, own, peers, cap)

    def a_copy(t, s):
        return remote(mine_a.at[t], land_a.at[s], a_send.at[t], a_recv.at[s], (row, 2 * (t * SIDE + y) + core))

    def b_copy(t, i, s):
        return remote(mine_b.at[t, i], land_b.at[s, i], b_send.at[t, i], b_recv.at[s, i],
                      (row, 2 * (x * SIDE + t) + core))

    for ox in hops:
        for oy in hops:
            dx, dy = chip_at(ox, oy)
            d = dx * SIDE + dy
            pair_copy(d).wait_recv()
            both = part[pl.ds((2 * d + core) * own, own), :] + pair[d]
            mine_a[dx, dy] = both[:, :wide_a]
            mine_b[dy, dx] = both[:, wide_a:]
            if oy:
                b_copy(dy, dx, y).start()
        if ox:
            a_copy(dx, x).start()

    def ent_copy(t, slot):
        return remote(ent_send.at[pl.ds(t * cap, cap)], ent.at[pl.ds(slot * cap, cap)],
                      en_send.at[t], en_recv.at[slot], (row, t))

    def ent_start(i, c):
        ent_copy((me + i) % peers, me).start()
        return c

    lax.fori_loop(1, peers, ent_start, 0)
    at = pl.ds(me * cap, cap)
    ent[at, :] = ent_send[at, :]
    for copy in loads[8:]:
        copy.wait()
    angles = (jnp.sum(used[...], axis=1, keepdims=True) - 1).astype(F32) * freq[...]
    cosine, sine = jnp.cos(angles), jnp.sin(angles)
    sine = jnp.where(iota(sine.shape, 1) < width // 2, -sine, sine)

    wo_copy = remote(wo.at[1 - core], wo_in, wo_send, wo_recv, partner)
    wo_copy.start()

    def a2_copy(t, s):
        return remote(sum_a.at[t], end_a.at[s], a2_send.at[t], a2_recv.at[s], (row, 2 * (x * SIDE + t) + core))

    def b2_copy(t, s):
        return remote(sum_b.at[t], end_b.at[s], b2_send.at[t], b2_recv.at[s], (row, 2 * (t * SIDE + y) + core))

    steps = (1, 3, 2)
    for o in steps:
        a_copy((x + SIDE - o) % SIDE, (x + SIDE - o) % SIDE).wait_recv()
    sum_a[...] = mine_a[x] + land_a[(x + 1) % SIDE] + land_a[(x + 2) % SIDE] + land_a[(x + 3) % SIDE]
    for o in (2, 1, 3):
        a2_copy((y + o) % SIDE, y).start()
    for o in steps:
        for i in range(SIDE):
            b_copy((y + SIDE - o) % SIDE, i, (y + SIDE - o) % SIDE).wait_recv()
    sum_b[...] = mine_b[y] + land_b[(y + 1) % SIDE] + land_b[(y + 2) % SIDE] + land_b[(y + 3) % SIDE]
    for o in (2, 1, 3):
        b2_copy((x + o) % SIDE, x).start()

    def ent_wait(i, c):
        t = (me + peers - i) % peers
        ent_copy(t, t).wait_recv()
        return c

    lax.fori_loop(1, peers, ent_wait, 0)
    table, by_slot = order_entries(ent[...], blocks, rows, tab.shape[1], 2 * cap)
    tab_v[...] = table
    slot_v[...] = by_slot
    tables = (pltpu.make_async_copy(tab_v, tab, tab_sem.at[0]), pltpu.make_async_copy(slot_v, slot_s, tab_sem.at[1]))
    for copy in tables:
        copy.start()

    for o in steps:
        a2_copy((y + SIDE - o) % SIDE, (y + SIDE - o) % SIDE).wait_recv()
    total[:, :wide_a] = sum_a[y] + end_a[(y + 1) % SIDE] + end_a[(y + 2) % SIDE] + end_a[(y + 3) % SIDE]
    for o in steps:
        b2_copy((x + SIDE - o) % SIDE, (x + SIDE - o) % SIDE).wait_recv()
    total[:, wide_a:] = sum_b[x] + end_b[(x + 1) % SIDE] + end_b[(x + 2) % SIDE] + end_b[(x + 3) % SIDE]

    low_t[...] = jnp.transpose(
        jnp.concatenate([total[:, wide:], jnp.zeros((128 - own, 128), F32)], axis=0)).reshape(low_t.shape)
    for r in range(own):
        adapter = held_s[0, tenant_s[0, me * own + r]]
        column = low_t[lax.rem(adapter, 128 // rank)][:, r:r + 1]
        more = jnp.sum(column * up[adapter], axis=0, keepdims=True)
        total[r:r + 1, :wide] += ADAPTER_SCALE * more
    gain_r = gain[...]
    for h in range(heads):
        t = total[:, h * width:(h + 1) * width]
        t = t * lax.rsqrt(jnp.mean(t * t, axis=1, keepdims=True) + EPSILON) * gain_r
        turned[:, h, :] = t * cosine + pltpu.roll(t, width // 2, 1) * sine
    q[pl.ds(me * own, own)] = turned[...].astype(BF16)

    def chip_by(i, sign):
        dx, dy = i // SIDE, i % SIDE
        return ((x + sign * dx + SIDE) % SIDE) * SIDE + (y + sign * dy + SIDE) % SIDE

    far = sorted(range(1, chips), key=lambda i: -(min(i // SIDE, SIDE - i // SIDE) + min(i % SIDE, SIDE - i % SIDE)))

    def q_copy(d, s):
        at = pl.ds((2 * s + core) * own, own)
        return remote(q.at[at], q.at[at], ag_send.at[d], ag_recv.at[s], (row, 2 * d + core))

    def q_relay(s, c):
        at = pl.ds((2 * s + c) * own, own)
        return remote(q.at[at], q.at[at], fw_send.at[s], fw_recv.at[s], partner)

    for i in far:
        q_copy(chip_by(i, 1), chip).start()
    q_relay(chip, core).start()

    def regroup(b, c):
        kbuf[b] = jnp.transpose(kbuf[b].reshape(toks // 2, 2 * width))
        both = vbuf[b].reshape(toks // 2, 2 * width)
        vbuf[b, :toks // 2] = both[:, :width]
        vbuf[b, toks // 2:] = both[:, width:]
        return c

    share = blocks // chips
    for copy in pool:
        copy.wait()
    lax.fori_loop(0, share, regroup, 0, unroll=4)

    def pair_sent(d, c):
        pair_copy(d).wait_send()
        return c

    lax.fori_loop(0, chips, pair_sent, 0)
    for o in (1, 2, 3):
        a_copy((x + o) % SIDE, x).wait_send()
        for i in range(SIDE):
            b_copy((y + o) % SIDE, i, y).wait_send()
        a2_copy((y + o) % SIDE, y).wait_send()
        b2_copy((x + o) % SIDE, x).wait_send()
    for copy in tables:
        copy.wait()

    for i in far[::-1]:
        s = chip_by(i, -1)
        q_copy(s, s).wait_recv()
        q_relay(s, core).start()
        at = (1 + far.index(i)) * share
        lax.fori_loop(at, at + share, regroup, 0, unroll=4)

    def q_landed(d, c):
        q_relay(d, 1 - core).wait_recv()
        return c

    lax.fori_loop(0, chips, q_landed, 0)

    coef = math.log2(math.e) / math.sqrt(width)
    half = heads // 2
    col = iota((heads, toks // 2), 1)
    upper = iota((heads, width), 0) < half
    none = jnp.zeros((heads, width), BF16)

    def chunk(c):
        base = c * GROUP
        b = tab[0, base]
        qs = [q[tab[2, base + g]] for g in range(GROUP)]
        qs = jnp.concatenate([jnp.concatenate(
            [jnp.where(upper, one, none), jnp.where(upper, none, one)], axis=1) for one in qs], axis=0)
        s = jnp.dot(qs, kbuf[b], preferred_element_type=F32)
        s = jnp.concatenate(
            [jnp.where(col < tab[1, base + g], s[heads * g: heads * (g + 1)], NEG) for g in range(GROUP)], axis=0)
        m = jnp.max(s, axis=1, keepdims=True)
        wt = jnp.exp2((s - m) * coef)
        l = jnp.sum(wt, axis=1, keepdims=True)
        vs = jnp.concatenate([vbuf[b, :toks // 2], vbuf[b, toks // 2:]], axis=1)
        o = jnp.dot(wt.astype(BF16), vs, preferred_element_type=F32).reshape(GROUP, 2, half, 2 * width)
        o = jnp.concatenate([o[:, 0:1, :, :width], o[:, 1:2, :, width:]], axis=1).reshape(GROUP * heads, width) / l
        e = jnp.broadcast_to(m * coef + jnp.log2(l), o.shape)
        return o.reshape(GROUP, 2, half, width), e.reshape(GROUP, 2, half, width)

    def chunks(i, c):
        done = [chunk(i * UNROLL + u) for u in range(UNROLL)]
        for u in range(UNROLL):
            o, e = done[u]
            at = pl.ds((i * UNROLL + u) * GROUP, GROUP)
            o_st[at] = o
            e_st[at] = e
        return c

    lax.fori_loop(0, tab.shape[1] // (GROUP * UNROLL), chunks, 0)

    lane = iota((half, 128), 1)
    same_head = (lane & (half - 1)) == iota((half, 128), 0)
    lane_row = jnp.where(same_head, lax.div(lane, half), -2)
    slots = 2 * cap

    def merge(d, hv):
        tops_of, outs = [], []
        for p in range(slots):
            at = slot_s[0, d * slots + p]
            tops_of.append(jnp.where(lane_row == slot_s[1, d * slots + p], e_st[at, hv], NEG))
            outs.append(o_st[at, hv])
        es = jnp.concatenate(tops_of, axis=0)
        top = jnp.max(es, axis=0, keepdims=True)
        f = jnp.exp2(es - top)
        l = jnp.sum(f, axis=0, keepdims=True)
        f = (f * (1.0 / l)).astype(BF16)
        os = jnp.concatenate(outs, axis=0).astype(BF16)
        return lax.dot_general(f, os, TN, preferred_element_type=F32).astype(BF16), top + jnp.log2(l)

    def merges(hv):
        done = [merge(d, hv) for d in range(chips)]
        for d in range(chips):
            partial[hv, d] = done[d][0]
        tops[hv] = jnp.concatenate([one[1] for one in done], axis=0)

    x_copies = (remote(tops.at[1 - core], tops_in, x_send.at[0], x_recv.at[0], partner),
                remote(partial.at[1 - core], partial_in, x_send.at[1], x_recv.at[1], partner))

    merges(1 - core)
    for copy in x_copies:
        copy.start()
    merges(core)

    def columns(fs):
        n = fs.shape[0]
        return jnp.transpose(jnp.concatenate([fs, jnp.zeros((128 - n, 128), F32)], axis=0))

    order = far + [0]
    x_copies[0].wait_recv()
    t0 = jnp.concatenate([tops[core, pl.ds(chip_by(i, 1), 1), :] for i in order], axis=0)
    t1 = jnp.concatenate([tops_in[pl.ds(chip_by(i, 1), 1), :] for i in order], axis=0)
    top = jnp.maximum(t0, t1)
    f0, f1 = jnp.exp2(t0 - top), jnp.exp2(t1 - top)
    l = f0 + f1
    over = top + jnp.log2(l)
    for k in range(chips):
        tops_out[k] = jnp.broadcast_to(over[k:k + 1], (8, 128))
    f = columns(jnp.concatenate([f0 / l, f1 / l], axis=0))

    def t_copy(k, d, s):
        return remote(tops_out.at[k], tops_all.at[s], t_send.at[k], t_recv.at[s], (row, 2 * d + core))

    def p_copy(k, d, s):
        return remote(merged.at[k], parts.at[s], p_send.at[k], p_recv.at[s], (row, 2 * d + core))

    for k, i in enumerate(order):
        if i:
            t_copy(k, chip_by(i, 1), chip).start()
    x_copies[1].wait_recv()
    for k, i in enumerate(order):
        d = chip_by(i, 1)
        both = (f[:, k:k + 1] * partial[core, d].astype(F32)
                + f[:, chips + k:chips + k + 1] * partial_in[d].astype(F32)).astype(BF16)
        if i:
            merged[k] = both
            p_copy(k, d, chip).start()
        else:
            parts[chip] = both
            tops_all[chip] = tops_out[k]

    def ent_sent(i, c):
        ent_copy((me + i) % peers, me).wait_send()
        return c

    lax.fori_loop(1, peers, ent_sent, 0)

    def q_sent(i, c):
        q_copy((chip + i) % chips, chip).wait_send()
        return c

    lax.fori_loop(1, chips, q_sent, 0)

    def q_relayed(d, c):
        q_relay(d, core).wait_send()
        return c

    lax.fori_loop(0, chips, q_relayed, 0)
    for copy in x_copies:
        copy.wait_send()
    wo_copy.wait()

    for i in far[::-1]:
        s = chip_by(i, -1)
        t_copy(0, s, s).wait_recv()
    top = tops_all[:, 0, :]
    f = jnp.exp2(top - jnp.max(top, axis=0, keepdims=True))
    f = columns(f / jnp.sum(f, axis=0, keepdims=True))
    for i in far[::-1]:
        s = chip_by(i, -1)
        p_copy(0, s, s).wait_recv()
    acc = jnp.zeros((128, width), F32)
    for s in range(chips):
        acc += f[:, s:s + 1] * parts[s].astype(F32)
    flat[...] = acc
    pair_rows = 2 * own
    here = pl.ds(chip * pair_rows, pair_rows)
    for h in range(half):
        attended[here, h * width:(h + 1) * width] = flat[pl.ds(h, pair_rows, stride=half), :].astype(BF16)

    def at_copy(d, s):
        at = pl.ds(s * pair_rows, pair_rows)
        return remote(attended.at[at], attended.at[at], ag2_send.at[d], ag2_recv.at[s], (row, 2 * d + core))

    for i in far:
        at_copy(chip_by(i, 1), chip).start()
    for k, i in enumerate(far):
        t_copy(k, chip_by(i, 1), chip).wait_send()
        p_copy(k, chip_by(i, 1), chip).wait_send()
    for i in far[::-1]:
        s = chip_by(i, -1)
        at_copy(s, s).wait_recv()
    out_rows = out_ref.shape[0]

    def z_copy(c, z, s):
        return remote(terms.at[c, pl.ds(z * out_rows, out_rows)], summed.at[c, s], z_send.at[c, z], z_recv.at[c, s],
                      (z, partner[1] if c else me))

    terms[1] = lax.dot_general(attended[...], wo_in[...], NT, preferred_element_type=F32).astype(BF16)
    for i in (2, 1, 3, 0):
        z_copy(1, (row + i) % planes, row).start()
    terms[0] = lax.dot_general(attended[...], wo[core], NT, preferred_element_type=F32).astype(BF16)
    for i in (2, 1, 3):
        z_copy(0, (row + i) % planes, row).start()
    for i in far:
        at_copy(chip_by(i, 1), chip).wait_send()

    result = terms[0, pl.ds(row * out_rows, out_rows), :].astype(F32)
    for c in (1, 0):
        for i in range(c ^ 1, planes):
            z = (row + i) % planes
            z_copy(c, z, z).wait_recv()
            result += summed[c, z].astype(F32)
    out_ref[...] = result.astype(BF16)
    for c in (1, 0):
        for i in range(c ^ 1, planes):
            z_copy(c, (row + i) % planes, row).wait_send()


def run(ht, w, dt, up, gain, freq, holder, index, used, tenant, held, k, v, wo, peers, planes):
    rows, wide, width = ht.shape[1], w.shape[1], gain.shape[1]
    own = rows // peers
    cap = 2 * own * holder.shape[1] // peers
    chips = peers // 2
    heads = wide // width
    blocks, toks, _ = k.shape
    slots = peers * cap
    count = -(-(slots // GROUP + blocks * (GROUP - 1) // GROUP) // UNROLL) * UNROLL
    positions = count * GROUP
    wide_a = (wide + 128) // 256 * 128 + 128
    wide_b = wide + 128 - wide_a
    cols = wo.shape[0]
    vm = pltpu.VMEM
    dma = pltpu.SemaphoreType.DMA
    args = (ht, w, dt, up, gain, freq, holder, index, used, tenant, held, k, v, wo)
    return pl.pallas_call(
        kernel,
        out_shape=jax.ShapeDtypeStruct((rows // planes, cols), BF16),
        in_specs=[pl.BlockSpec(memory_space=pltpu.HBM)] * len(args),
        out_specs=pl.BlockSpec(memory_space=pltpu.VMEM),
        scratch_shapes=[vm(a.shape, a.dtype) for a in args[:11]] + [
            pltpu.SMEM(tenant.shape, I32), pltpu.SMEM(held.shape, I32),
            vm(k.shape, BF16), vm(v.shape, BF16), vm((2, cols, wide // 2), BF16), vm((cols, wide // 2), BF16),
            vm((rows, wide + 128), F32), vm((chips, own, wide + 128), F32),
            vm((SIDE, SIDE, own, wide_a), F32), vm((SIDE, SIDE, own, wide_b), F32),
            vm((SIDE, SIDE, own, wide_a), F32), vm((SIDE, SIDE, own, wide_b), F32),
            vm((SIDE, own, wide_a), F32), vm((SIDE, own, wide_b), F32),
            vm((SIDE, own, wide_a), F32), vm((SIDE, own, wide_b), F32),
            vm((own, wide + 128), F32), vm((128 // up.shape[1], up.shape[1], 128), F32), vm((own, heads, width), F32),
            vm((slots, 128), BF16), vm((slots, 128), BF16), vm((8, positions), I32), vm((8, slots), I32),
            pltpu.SMEM((8, positions), I32), pltpu.SMEM((8, slots), I32),
            vm((rows, heads, width), BF16),
            vm((positions, 2, heads // 2, width), F32), vm((positions, 2, heads // 2, width), F32),
            vm((2, chips, 128, width), BF16), vm((2, chips, 128), F32),
            vm((chips, 128, width), BF16), vm((chips, 128), F32),
            vm((chips, 128, width), BF16), vm((chips, 8, 128), F32),
            vm((chips, 128, width), BF16), vm((chips, 8, 128), F32), vm((128, width), F32),
            vm((rows, wide // 2), BF16), vm((2, rows, cols), BF16), vm((2, planes, rows // planes, cols), BF16),
            dma((15,)), dma((2 * PIECES,)), dma((2,)), dma((chips,)), dma((chips,)),
            dma((SIDE,)), dma((SIDE,)), dma((SIDE, SIDE)), dma((SIDE, SIDE)),
            dma((SIDE,)), dma((SIDE,)), dma((SIDE,)), dma((SIDE,)),
            dma((peers,)), dma((peers,)), dma((chips,)), dma((chips,)), dma((chips,)), dma((chips,)),
            dma, dma, dma((2,)), dma((2,)), dma((chips,)), dma((chips,)), dma((chips,)), dma((chips,)),
            dma((chips,)), dma((chips,)), dma((2, planes)), dma((2, planes)),
        ],
        compiler_params=pltpu.CompilerParams(
            vmem_limit_bytes=62 * 2**20, collective_id=0, has_side_effects=True),
        name="decode",
    )(*args)


def local(hidden, query_weight, adapter_down_weight, adapter_up_weight, query_norm_gain, paged_key_cache,
          paged_value_cache, output_weight, holder, holder_block_index, block_used_length, tenant, tenant_adapter):
    peers, planes = lax.axis_size("kv"), lax.axis_size("row")
    count, _, rank = adapter_down_weight.shape
    width = query_norm_gain.shape[0]
    blocks, toks, kv_heads, _ = paged_key_cache.shape
    half = width // 2
    freq = ROPE_BASE ** (-(jnp.arange(half, dtype=jnp.float32) * 2.0) / width)
    freq = jnp.concatenate([freq, freq])[None, :]
    down = jnp.transpose(adapter_down_weight, (0, 2, 1)).reshape(count * rank, -1)
    pool = (blocks, toks * kv_heads, width)
    return run(hidden.T, query_weight, down, adapter_up_weight, query_norm_gain[None, :], freq, holder,
               holder_block_index, block_used_length, tenant[None, :], tenant_adapter[None, :],
               paged_key_cache.reshape(pool), paged_value_cache.reshape(pool), output_weight.T, peers, planes)


def solution(mesh):
    return jax.shard_map(
        local,
        mesh=mesh,
        in_specs=(
            P(None, "kv"),
            P("kv", "row"),
            P(None, "kv", None),
            P(None, None, "row"),
            P(),
            P("kv", None, "row", None),
            P("kv", None, "row", None),
            P("row", "kv"),
            P("kv", None),
            P("kv", None),
            P("kv", None),
            P(),
            P(),
        ),
        out_specs=P("row", "kv"),
        check_vma=False,
    )
```

```python
import functools
import math

import jax
import jax.numpy as jnp
from jax import lax
from jax.experimental import pallas as pl
from jax.experimental.pallas import tpu as pltpu
from jax.sharding import PartitionSpec as P

NEG = -1e30
F32, BF16, I32 = jnp.float32, jnp.bfloat16, jnp.int32
NT = (((1,), (1,)), ((), ()))
TN = (((0,), (0,)), ((), ()))
TT = (((0,), (1,)), ((), ()))
MESH = pl.DeviceIdType.MESH
PIECES = 4
GROUP = 4
UNROLL = 224
SIDE = 4
ADAPTER_SCALE = 0.5
ROPE_BASE = 1000000.0
EPSILON = 1e-06


def iota(shape, dim):
    return lax.broadcasted_iota(I32, shape, dim)


def flat_row(x):
    rows, n = x.shape
    wide = jnp.concatenate([x.astype(F32)] * rows, axis=1)
    keep = lax.div(iota(wide.shape, 1), n) == iota(wide.shape, 0)
    return jnp.sum(jnp.where(keep, wide, 0.0), axis=0, keepdims=True)


def remote(src, dst, send, recv, device):
    return pltpu.make_async_remote_copy(
        src_ref=src, dst_ref=dst, send_sem=send, recv_sem=recv, device_id=device, device_id_type=MESH)


def entries_by_holder(holder, index, used, me, own, peers, cap):
    dest, index, used = flat_row(holder), flat_row(index), flat_row(used)
    count = dest.shape[1]
    to = dest == iota((peers, count), 0).astype(F32)
    earlier = jnp.where(iota((count, count), 0) < iota((count, count), 1), 1.0, 0.0).astype(BF16)
    before = jnp.dot(jnp.where(to, 1.0, 0.0).astype(BF16), earlier, preferred_element_type=F32)
    place = dest * cap + jnp.sum(jnp.where(to, before, 0.0), axis=0, keepdims=True)
    chosen = jnp.where(place == iota((peers * cap, count), 0).astype(F32), 1.0, 0.0).astype(BF16)
    sub = iota((128, count), 0)
    from_row = (me * own + lax.div(iota((1, count), 1), count // own)).astype(F32)
    fields = jnp.where(sub == 0, index, jnp.where(sub == 1, used, jnp.where(sub == 2, from_row, 0.0)))
    return lax.dot_general(chosen, fields.astype(BF16), NT, preferred_element_type=F32).astype(BF16)


def order_entries(ent, blocks, rows, positions, per_group):
    slots = ent.shape[0]
    entf = ent.astype(F32)
    pick = jnp.where(iota((16, 128), 0) == iota((16, 128), 1), 1.0, 0.0).astype(BF16)
    ent_t = lax.dot_general(pick, ent, NT, preferred_element_type=F32)
    blk_r, len_r, row_r = ent_t[0:1], ent_t[1:2], ent_t[2:3]
    valid_c = entf[:, 1:2] > 0
    key_c = jnp.where(valid_c, entf[:, 0:1], 999.0)
    key_r = jnp.where(len_r > 0, blk_r, 999.0)
    earlier = iota((slots, slots), 1) < iota((slots, slots), 0)
    within = jnp.sum(jnp.where((key_c == key_r) & earlier, 1.0, 0.0), axis=1, keepdims=True)
    block_of = iota((blocks, slots), 0).astype(F32) == key_r
    count = jnp.sum(jnp.where(block_of, 1.0, 0.0), axis=1, keepdims=True)
    chunks = jnp.floor((count + (GROUP - 1)) * (1.0 / GROUP))
    below = jnp.where(iota((blocks, blocks), 1) < iota((blocks, blocks), 0), 1.0, 0.0).astype(BF16)
    first = jnp.dot(below, jnp.broadcast_to(chunks, (blocks, 128)).astype(BF16), preferred_element_type=F32)
    own_block = jnp.where(key_c == iota((slots, blocks), 1).astype(F32), 1.0, 0.0).astype(BF16)
    first_c = jnp.dot(own_block, first.astype(BF16), preferred_element_type=F32)[:, 0:1]
    major = jnp.floor(within * (1.0 / GROUP))
    chunk_c, seat_c = first_c + major, within - major * GROUP
    place = jnp.where(valid_c, chunk_c * GROUP + seat_c, -1.0)
    sub = iota((16, slots), 0)
    fields = jnp.where(sub == 0, blk_r, jnp.where(sub == 1, len_r, jnp.where(sub == 2, row_r, 0.0))).astype(BF16)
    chosen = jnp.where(place == iota((slots, positions), 1).astype(F32), 1.0, 0.0).astype(BF16)
    table = jnp.dot(fields, chosen, preferred_element_type=F32)[0:8]
    sub = iota(table.shape, 0)
    table = table.astype(I32)
    table = jnp.clip(table, 0, jnp.where(sub == 0, blocks - 1, jnp.where(sub == 1, 1 << 16, rows - 1)))
    lane = iota((slots, 128), 1)
    seats = jnp.where(lane == 0, chunk_c, jnp.where(lane == 1, seat_c, 0.0)).astype(BF16)
    seats = lax.dot_general(pick, seats, NT, preferred_element_type=F32)
    where_r = jnp.where(len_r > 0, seats[0:1] * GROUP + seats[1:2], 0.0)
    local_r = row_r - (lax.div(iota((1, slots), 1), per_group) * 16).astype(F32)
    local_r = jnp.where(len_r > 0, local_r, -1.0)
    by_slot = jnp.clip(jnp.where(iota((8, slots), 0) == 0, where_r, local_r).astype(I32), -1, positions - 1)
    by_slot = jnp.where(iota((8, slots), 0) == 0, jnp.maximum(by_slot, 0), by_slot)
    return table, by_slot


def kernel(ht_h, w_h, dt_h, up_h, gain_h, freq_h, holder_h, index_h, used_h, tenant_h, held_h, k_h, v_h, wo_h,
           out_ref,
           ht, w, dt, up, gain, freq, holder, index, used, tenant, held, tenant_s, held_s, kbuf, vbuf, wo, wo_in,
           part, pair, mine_a, mine_b, land_a, land_b, sum_a, sum_b, end_a, end_b, total, low_t, turned,
           ent_send, ent, tab_v, slot_v, tab, slot_s, q, o_st, e_st,
           partial, tops, partial_in, tops_in, merged, tops_out, parts, tops_all, flat, attended, terms, summed,
           in_sem, kv_sem, tab_sem, pair_send, pair_recv, a_send, a_recv, b_send, b_recv, a2_send, a2_recv,
           b2_send, b2_recv, en_send, en_recv, ag_send, ag_recv, fw_send, fw_recv,
           wo_send, wo_recv, x_send, x_recv, p_send, p_recv, t_send, t_recv, ag2_send, ag2_recv, z_send, z_recv):
    row, me = lax.axis_index("row"), lax.axis_index("kv")
    peers, planes = lax.axis_size("kv"), lax.axis_size("row")
    chips = peers // 2
    chip, core = me // 2, me % 2
    x, y = chip // SIDE, chip % SIDE
    partner = (row, 2 * chip + 1 - core)
    wide = w.shape[1]
    rows, heads, width = q.shape
    own = rows // peers
    cap = ent.shape[0] // peers
    blocks, toks, _ = kbuf.shape
    wide_a = mine_a.shape[3]
    barrier = pltpu.get_barrier_semaphore()

    def greet(i, c):
        pl.semaphore_signal(barrier, inc=1, device_id=(row, (me + i) % peers), device_id_type=MESH)
        return c

    def greet_plane(i, c):
        pl.semaphore_signal(barrier, inc=1, device_id=((row + i) % planes, me), device_id_type=MESH)
        pl.semaphore_signal(barrier, inc=1, device_id=((row + i) % planes, partner[1]), device_id_type=MESH)
        return c

    loads = [pltpu.make_async_copy(src, dst, in_sem.at[i]) for i, (src, dst) in enumerate((
        (ht_h, ht), (w_h, w), (holder_h, holder), (index_h, index), (used_h, used), (tenant_h, tenant),
        (held_h, held), (dt_h, dt), (tenant_h, tenant_s), (held_h, held_s), (gain_h, gain), (freq_h, freq),
        (up_h, up), (wo_h.at[:, :wide // 2], wo.at[0]), (wo_h.at[:, wide // 2:], wo.at[1])))]
    for copy in loads[:8]:
        copy.start()
    lax.fori_loop(1, peers, greet, 0)
    lax.fori_loop(1, planes, greet_plane, 0)
    step = blocks // PIECES
    pool = []
    for i in range(PIECES):
        at = pl.ds(i * step, step)
        pool += [pltpu.make_async_copy(k_h.at[at], kbuf.at[at], kv_sem.at[2 * i]),
                 pltpu.make_async_copy(v_h.at[at], vbuf.at[at], kv_sem.at[2 * i + 1])]
    for copy in loads[:8]:
        copy.wait()
    for copy in loads[8:] + pool:
        copy.start()

    part[:, :wide] = lax.dot_general(ht[...], w[...], TN, preferred_element_type=F32)
    low = lax.dot_general(ht[...], dt[...], TT, preferred_element_type=F32)
    rank = up.shape[1]
    is_tenant = jnp.where(tenant[...] == iota((held.shape[1], rows), 0), 1.0, 0.0).astype(BF16)
    held_b = jnp.broadcast_to(held[...].astype(F32), (16, held.shape[1])).astype(BF16)
    adapter = jnp.dot(held_b, is_tenant, preferred_element_type=F32)[0:8]
    adapter = jnp.transpose(adapter)[:, 0:1].astype(I32)
    low = jnp.where(lax.div(iota(low.shape, 1), rank) == adapter, low, 0.0)
    part[:, wide:] = sum(low[:, 128 * i: 128 * (i + 1)] for i in range(low.shape[1] // 128))

    pl.semaphore_wait(barrier, peers - 1 + 2 * (planes - 1))

    def pair_copy(d):
        return remote(part.at[pl.ds((2 * d + 1 - core) * own, own)], pair.at[d],
                      pair_send.at[d], pair_recv.at[d], partner)

    def chip_at(ox, oy):
        return (x + ox) % SIDE, (y + oy) % SIDE

    hops = (2, 1, 3, 0)
    for ox in hops:
        for oy in hops:
            dx, dy = chip_at(ox, oy)
            pair_copy(dx * SIDE + dy).start()

    ent_send[...] = entries_by_holder(holder[...], index[...], used[...], me, own, peers, cap)

    def a_copy(t, s):
        return remote(mine_a.at[t], land_a.at[s], a_send.at[t], a_recv.at[s], (row, 2 * (t * SIDE + y) + core))

    def b_copy(t, i, s):
        return remote(mine_b.at[t, i], land_b.at[s, i], b_send.at[t, i], b_recv.at[s, i],
                      (row, 2 * (x * SIDE + t) + core))

    for ox in hops:
        for oy in hops:
            dx, dy = chip_at(ox, oy)
            d = dx * SIDE + dy
            pair_copy(d).wait_recv()
            both = part[pl.ds((2 * d + core) * own, own), :] + pair[d]
            mine_a[dx, dy] = both[:, :wide_a]
            mine_b[dy, dx] = both[:, wide_a:]
            if oy:
                b_copy(dy, dx, y).start()
        if ox:
            a_copy(dx, x).start()

    def ent_copy(t, slot):
        return remote(ent_send.at[pl.ds(t * cap, cap)], ent.at[pl.ds(slot * cap, cap)],
                      en_send.at[t], en_recv.at[slot], (row, t))

    def ent_start(i, c):
        ent_copy((me + i) % peers, me).start()
        return c

    lax.fori_loop(1, peers, ent_start, 0)
    at = pl.ds(me * cap, cap)
    ent[at, :] = ent_send[at, :]
    for copy in loads[8:]:
        copy.wait()
    angles = (jnp.sum(used[...], axis=1, keepdims=True) - 1).astype(F32) * freq[...]
    cosine, sine = jnp.cos(angles), jnp.sin(angles)
    sine = jnp.where(iota(sine.shape, 1) < width // 2, -sine, sine)

    wo_copy = remote(wo.at[1 - core], wo_in, wo_send, wo_recv, partner)
    wo_copy.start()

    for copy in pool:
        copy.wait()

    def turn_keys(b, c):
        kbuf[b] = jnp.transpose(kbuf[b].reshape(toks // 2, 2 * width))
        return c

    lax.fori_loop(0, blocks, turn_keys, 0, unroll=4)

    def a2_copy(t, s):
        return remote(sum_a.at[t], end_a.at[s], a2_send.at[t], a2_recv.at[s], (row, 2 * (x * SIDE + t) + core))

    def b2_copy(t, s):
        return remote(sum_b.at[t], end_b.at[s], b2_send.at[t], b2_recv.at[s], (row, 2 * (t * SIDE + y) + core))

    steps = (1, 3, 2)
    for o in steps:
        a_copy((x + SIDE - o) % SIDE, (x + SIDE - o) % SIDE).wait_recv()
    sum_a[...] = mine_a[x] + land_a[(x + 1) % SIDE] + land_a[(x + 2) % SIDE] + land_a[(x + 3) % SIDE]
    for o in (2, 1, 3):
        a2_copy((y + o) % SIDE, y).start()
    for o in steps:
        for i in range(SIDE):
            b_copy((y + SIDE - o) % SIDE, i, (y + SIDE - o) % SIDE).wait_recv()
    sum_b[...] = mine_b[y] + land_b[(y + 1) % SIDE] + land_b[(y + 2) % SIDE] + land_b[(y + 3) % SIDE]
    for o in (2, 1, 3):
        b2_copy((x + o) % SIDE, x).start()

    def ent_wait(i, c):
        t = (me + peers - i) % peers
        ent_copy(t, t).wait_recv()
        return c

    lax.fori_loop(1, peers, ent_wait, 0)
    table, by_slot = order_entries(ent[...], blocks, rows, tab.shape[1], 2 * cap)
    tab_v[...] = table
    slot_v[...] = by_slot
    tables = (pltpu.make_async_copy(tab_v, tab, tab_sem.at[0]), pltpu.make_async_copy(slot_v, slot_s, tab_sem.at[1]))
    for copy in tables:
        copy.start()

    for o in steps:
        a2_copy((y + SIDE - o) % SIDE, (y + SIDE - o) % SIDE).wait_recv()
    total[:, :wide_a] = sum_a[y] + end_a[(y + 1) % SIDE] + end_a[(y + 2) % SIDE] + end_a[(y + 3) % SIDE]
    for o in steps:
        b2_copy((x + SIDE - o) % SIDE, (x + SIDE - o) % SIDE).wait_recv()
    total[:, wide_a:] = sum_b[x] + end_b[(x + 1) % SIDE] + end_b[(x + 2) % SIDE] + end_b[(x + 3) % SIDE]

    low_t[...] = jnp.transpose(
        jnp.concatenate([total[:, wide:], jnp.zeros((128 - own, 128), F32)], axis=0)).reshape(low_t.shape)
    for r in range(own):
        adapter = held_s[0, tenant_s[0, me * own + r]]
        column = low_t[lax.rem(adapter, 128 // rank)][:, r:r + 1]
        more = jnp.sum(column * up[adapter], axis=0, keepdims=True)
        total[r:r + 1, :wide] += ADAPTER_SCALE * more
    gain_r = gain[...]
    for h in range(heads):
        t = total[:, h * width:(h + 1) * width]
        t = t * lax.rsqrt(jnp.mean(t * t, axis=1, keepdims=True) + EPSILON) * gain_r
        turned[:, h, :] = t * cosine + pltpu.roll(t, width // 2, 1) * sine
    q[pl.ds(me * own, own)] = turned[...].astype(BF16)

    def chip_by(i, sign):
        dx, dy = i // SIDE, i % SIDE
        return ((x + sign * dx + SIDE) % SIDE) * SIDE + (y + sign * dy + SIDE) % SIDE

    far = sorted(range(1, chips), key=lambda i: -(min(i // SIDE, SIDE - i // SIDE) + min(i % SIDE, SIDE - i % SIDE)))

    def q_copy(d, s):
        at = pl.ds((2 * s + core) * own, own)
        return remote(q.at[at], q.at[at], ag_send.at[d], ag_recv.at[s], (row, 2 * d + core))

    def q_relay(s, c):
        at = pl.ds((2 * s + c) * own, own)
        return remote(q.at[at], q.at[at], fw_send.at[s], fw_recv.at[s], partner)

    for i in far:
        q_copy(chip_by(i, 1), chip).start()
    q_relay(chip, core).start()

    def turn_values(b, c):
        both = vbuf[b].reshape(toks // 2, 2 * width)
        vbuf[b, :toks // 2] = both[:, :width]
        vbuf[b, toks // 2:] = both[:, width:]
        return c

    lax.fori_loop(0, blocks, turn_values, 0, unroll=4)

    def pair_sent(d, c):
        pair_copy(d).wait_send()
        return c

    lax.fori_loop(0, chips, pair_sent, 0)
    for o in (1, 2, 3):
        a_copy((x + o) % SIDE, x).wait_send()
        for i in range(SIDE):
            b_copy((y + o) % SIDE, i, y).wait_send()
        a2_copy((y + o) % SIDE, y).wait_send()
        b2_copy((x + o) % SIDE, x).wait_send()
    for copy in tables:
        copy.wait()

    for i in far:
        s = chip_by(i, -1)
        q_copy(s, s).wait_recv()
        q_relay(s, core).start()

    def q_landed(d, c):
        q_relay(d, 1 - core).wait_recv()
        return c

    lax.fori_loop(0, chips, q_landed, 0)

    coef = math.log2(math.e) / math.sqrt(width)
    half = heads // 2
    col = iota((heads, toks // 2), 1)
    upper = iota((heads, width), 0) < half
    none = jnp.zeros((heads, width), BF16)

    def chunk(c):
        base = c * GROUP
        b = tab[0, base]
        qs = [q[tab[2, base + g]] for g in range(GROUP)]
        qs = jnp.concatenate([jnp.concatenate(
            [jnp.where(upper, one, none), jnp.where(upper, none, one)], axis=1) for one in qs], axis=0)
        s = jnp.dot(qs, kbuf[b], preferred_element_type=F32)
        s = jnp.concatenate(
            [jnp.where(col < tab[1, base + g], s[heads * g: heads * (g + 1)], NEG) for g in range(GROUP)], axis=0)
        m = jnp.max(s, axis=1, keepdims=True)
        wt = jnp.exp2((s - m) * coef)
        l = jnp.sum(wt, axis=1, keepdims=True)
        vs = jnp.concatenate([vbuf[b, :toks // 2], vbuf[b, toks // 2:]], axis=1)
        o = jnp.dot(wt.astype(BF16), vs, preferred_element_type=F32).reshape(GROUP, 2, half, 2 * width)
        o = jnp.concatenate([o[:, 0:1, :, :width], o[:, 1:2, :, width:]], axis=1).reshape(GROUP * heads, width) / l
        e = jnp.broadcast_to(m * coef + jnp.log2(l), o.shape)
        return o.reshape(GROUP, 2, half, width), e.reshape(GROUP, 2, half, width)

    def chunks(i, c):
        done = [chunk(i * UNROLL + u) for u in range(UNROLL)]
        for u in range(UNROLL):
            o, e = done[u]
            at = pl.ds((i * UNROLL + u) * GROUP, GROUP)
            o_st[at] = o
            e_st[at] = e
        return c

    lax.fori_loop(0, tab.shape[1] // (GROUP * UNROLL), chunks, 0)

    lane = iota((half, 128), 1)
    same_head = (lane & (half - 1)) == iota((half, 128), 0)
    lane_row = jnp.where(same_head, lax.div(lane, half), -2)
    slots = 2 * cap

    def merge(d, hv):
        tops_of, outs = [], []
        for p in range(slots):
            at = slot_s[0, d * slots + p]
            tops_of.append(jnp.where(lane_row == slot_s[1, d * slots + p], e_st[at, hv], NEG))
            outs.append(o_st[at, hv])
        es = jnp.concatenate(tops_of, axis=0)
        top = jnp.max(es, axis=0, keepdims=True)
        f = jnp.exp2(es - top)
        l = jnp.sum(f, axis=0, keepdims=True)
        f = (f * (1.0 / l)).astype(BF16)
        os = jnp.concatenate(outs, axis=0).astype(BF16)
        return lax.dot_general(f, os, TN, preferred_element_type=F32).astype(BF16), top + jnp.log2(l)

    def merges(hv):
        done = [merge(d, hv) for d in range(chips)]
        for d in range(chips):
            partial[hv, d] = done[d][0]
        tops[hv] = jnp.concatenate([one[1] for one in done], axis=0)

    x_copies = (remote(tops.at[1 - core], tops_in, x_send.at[0], x_recv.at[0], partner),
                remote(partial.at[1 - core], partial_in, x_send.at[1], x_recv.at[1], partner))

    merges(1 - core)
    for copy in x_copies:
        copy.start()
    merges(core)

    def columns(fs):
        n = fs.shape[0]
        return jnp.transpose(jnp.concatenate([fs, jnp.zeros((128 - n, 128), F32)], axis=0))

    order = far + [0]
    x_copies[0].wait_recv()
    t0 = jnp.concatenate([tops[core, pl.ds(chip_by(i, 1), 1), :] for i in order], axis=0)
    t1 = jnp.concatenate([tops_in[pl.ds(chip_by(i, 1), 1), :] for i in order], axis=0)
    top = jnp.maximum(t0, t1)
    f0, f1 = jnp.exp2(t0 - top), jnp.exp2(t1 - top)
    l = f0 + f1
    over = top + jnp.log2(l)
    for k in range(chips):
        tops_out[k] = jnp.broadcast_to(over[k:k + 1], (8, 128))
    f = columns(jnp.concatenate([f0 / l, f1 / l], axis=0))

    def t_copy(k, d, s):
        return remote(tops_out.at[k], tops_all.at[s], t_send.at[k], t_recv.at[s], (row, 2 * d + core))

    def p_copy(k, d, s):
        return remote(merged.at[k], parts.at[s], p_send.at[k], p_recv.at[s], (row, 2 * d + core))

    for k, i in enumerate(order):
        if i:
            t_copy(k, chip_by(i, 1), chip).start()
    x_copies[1].wait_recv()
    for k, i in enumerate(order):
        d = chip_by(i, 1)
        both = (f[:, k:k + 1] * partial[core, d].astype(F32)
                + f[:, chips + k:chips + k + 1] * partial_in[d].astype(F32)).astype(BF16)
        if i:
            merged[k] = both
            p_copy(k, d, chip).start()
        else:
            parts[chip] = both
            tops_all[chip] = tops_out[k]

    def ent_sent(i, c):
        ent_copy((me + i) % peers, me).wait_send()
        return c

    lax.fori_loop(1, peers, ent_sent, 0)

    def q_sent(i, c):
        q_copy((chip + i) % chips, chip).wait_send()
        return c

    lax.fori_loop(1, chips, q_sent, 0)

    def q_relayed(d, c):
        q_relay(d, core).wait_send()
        return c

    lax.fori_loop(0, chips, q_relayed, 0)
    for copy in x_copies:
        copy.wait_send()
    wo_copy.wait()

    for i in far[::-1]:
        s = chip_by(i, -1)
        t_copy(0, s, s).wait_recv()
    top = tops_all[:, 0, :]
    f = jnp.exp2(top - jnp.max(top, axis=0, keepdims=True))
    f = columns(f / jnp.sum(f, axis=0, keepdims=True))
    for i in far[::-1]:
        s = chip_by(i, -1)
        p_copy(0, s, s).wait_recv()
    acc = jnp.zeros((128, width), F32)
    for s in range(chips):
        acc += f[:, s:s + 1] * parts[s].astype(F32)
    flat[...] = acc
    pair_rows = 2 * own
    here = pl.ds(chip * pair_rows, pair_rows)
    for h in range(half):
        attended[here, h * width:(h + 1) * width] = flat[pl.ds(h, pair_rows, stride=half), :].astype(BF16)

    def at_copy(d, s):
        at = pl.ds(s * pair_rows, pair_rows)
        return remote(attended.at[at], attended.at[at], ag2_send.at[d], ag2_recv.at[s], (row, 2 * d + core))

    for i in far:
        at_copy(chip_by(i, 1), chip).start()
    for k, i in enumerate(far):
        t_copy(k, chip_by(i, 1), chip).wait_send()
        p_copy(k, chip_by(i, 1), chip).wait_send()
    for i in far[::-1]:
        s = chip_by(i, -1)
        at_copy(s, s).wait_recv()
    out_rows = out_ref.shape[0]

    def z_copy(c, z, s):
        return remote(terms.at[c, pl.ds(z * out_rows, out_rows)], summed.at[c, s], z_send.at[c, z], z_recv.at[c, s],
                      (z, partner[1] if c else me))

    terms[1] = lax.dot_general(attended[...], wo_in[...], NT, preferred_element_type=F32).astype(BF16)
    for i in (2, 1, 3, 0):
        z_copy(1, (row + i) % planes, row).start()
    terms[0] = lax.dot_general(attended[...], wo[core], NT, preferred_element_type=F32).astype(BF16)
    for i in (2, 1, 3):
        z_copy(0, (row + i) % planes, row).start()
    for i in far:
        at_copy(chip_by(i, 1), chip).wait_send()

    result = terms[0, pl.ds(row * out_rows, out_rows), :].astype(F32)
    for c in (1, 0):
        for i in range(c ^ 1, planes):
            z = (row + i) % planes
            z_copy(c, z, z).wait_recv()
            result += summed[c, z].astype(F32)
    out_ref[...] = result.astype(BF16)
    for c in (1, 0):
        for i in range(c ^ 1, planes):
            z_copy(c, (row + i) % planes, row).wait_send()


def run(ht, w, dt, up, gain, freq, holder, index, used, tenant, held, k, v, wo, peers, planes):
    rows, wide, width = ht.shape[1], w.shape[1], gain.shape[1]
    own = rows // peers
    cap = 2 * own * holder.shape[1] // peers
    chips = peers // 2
    heads = wide // width
    blocks, toks, _ = k.shape
    slots = peers * cap
    count = -(-(slots // GROUP + blocks * (GROUP - 1) // GROUP) // UNROLL) * UNROLL
    positions = count * GROUP
    wide_a = (wide + 128) // 256 * 128 + 128
    wide_b = wide + 128 - wide_a
    cols = wo.shape[0]
    vm = pltpu.VMEM
    dma = pltpu.SemaphoreType.DMA
    args = (ht, w, dt, up, gain, freq, holder, index, used, tenant, held, k, v, wo)
    return pl.pallas_call(
        kernel,
        out_shape=jax.ShapeDtypeStruct((rows // planes, cols), BF16),
        in_specs=[pl.BlockSpec(memory_space=pltpu.HBM)] * len(args),
        out_specs=pl.BlockSpec(memory_space=pltpu.VMEM),
        scratch_shapes=[vm(a.shape, a.dtype) for a in args[:11]] + [
            pltpu.SMEM(tenant.shape, I32), pltpu.SMEM(held.shape, I32),
            vm(k.shape, BF16), vm(v.shape, BF16), vm((2, cols, wide // 2), BF16), vm((cols, wide // 2), BF16),
            vm((rows, wide + 128), F32), vm((chips, own, wide + 128), F32),
            vm((SIDE, SIDE, own, wide_a), F32), vm((SIDE, SIDE, own, wide_b), F32),
            vm((SIDE, SIDE, own, wide_a), F32), vm((SIDE, SIDE, own, wide_b), F32),
            vm((SIDE, own, wide_a), F32), vm((SIDE, own, wide_b), F32),
            vm((SIDE, own, wide_a), F32), vm((SIDE, own, wide_b), F32),
            vm((own, wide + 128), F32), vm((128 // up.shape[1], up.shape[1], 128), F32), vm((own, heads, width), F32),
            vm((slots, 128), BF16), vm((slots, 128), BF16), vm((8, positions), I32), vm((8, slots), I32),
            pltpu.SMEM((8, positions), I32), pltpu.SMEM((8, slots), I32),
            vm((rows, heads, width), BF16),
            vm((positions, 2, heads // 2, width), F32), vm((positions, 2, heads // 2, width), F32),
            vm((2, chips, 128, width), BF16), vm((2, chips, 128), F32),
            vm((chips, 128, width), BF16), vm((chips, 128), F32),
            vm((chips, 128, width), BF16), vm((chips, 8, 128), F32),
            vm((chips, 128, width), BF16), vm((chips, 8, 128), F32), vm((128, width), F32),
            vm((rows, wide // 2), BF16), vm((2, rows, cols), BF16), vm((2, planes, rows // planes, cols), BF16),
            dma((15,)), dma((2 * PIECES,)), dma((2,)), dma((chips,)), dma((chips,)),
            dma((SIDE,)), dma((SIDE,)), dma((SIDE, SIDE)), dma((SIDE, SIDE)),
            dma((SIDE,)), dma((SIDE,)), dma((SIDE,)), dma((SIDE,)),
            dma((peers,)), dma((peers,)), dma((chips,)), dma((chips,)), dma((chips,)), dma((chips,)),
            dma, dma, dma((2,)), dma((2,)), dma((chips,)), dma((chips,)), dma((chips,)), dma((chips,)),
            dma((chips,)), dma((chips,)), dma((2, planes)), dma((2, planes)),
        ],
        compiler_params=pltpu.CompilerParams(
            vmem_limit_bytes=62 * 2**20, collective_id=0, has_side_effects=True),
        name="decode",
    )(*args)


def local(hidden, query_weight, adapter_down_weight, adapter_up_weight, query_norm_gain, paged_key_cache,
          paged_value_cache, output_weight, holder, holder_block_index, block_used_length, tenant, tenant_adapter):
    peers, planes = lax.axis_size("kv"), lax.axis_size("row")
    count, _, rank = adapter_down_weight.shape
    width = query_norm_gain.shape[0]
    blocks, toks, kv_heads, _ = paged_key_cache.shape
    half = width // 2
    freq = ROPE_BASE ** (-(jnp.arange(half, dtype=jnp.float32) * 2.0) / width)
    freq = jnp.concatenate([freq, freq])[None, :]
    down = jnp.transpose(adapter_down_weight, (0, 2, 1)).reshape(count * rank, -1)
    pool = (blocks, toks * kv_heads, width)
    return run(hidden.T, query_weight, down, adapter_up_weight, query_norm_gain[None, :], freq, holder,
               holder_block_index, block_used_length, tenant[None, :], tenant_adapter[None, :],
               paged_key_cache.reshape(pool), paged_value_cache.reshape(pool), output_weight.T, peers, planes)


def solution(mesh):
    return jax.shard_map(
        local,
        mesh=mesh,
        in_specs=(
            P(None, "kv"),
            P("kv", "row"),
            P(None, "kv", None),
            P(None, None, "row"),
            P(),
            P("kv", None, "row", None),
            P("kv", None, "row", None),
            P("row", "kv"),
            P("kv", None),
            P("kv", None),
            P("kv", None),
            P(),
            P(),
        ),
        out_specs=P("row", "kv"),
        check_vma=False,
    )
```

```python
import functools
import math

import jax
import jax.numpy as jnp
import numpy as np
from jax import lax
from jax.experimental import pallas as pl
from jax.experimental.pallas import tpu as pltpu
from jax.sharding import PartitionSpec as P

NEG = -1e30
F32, BF16, I32 = jnp.float32, jnp.bfloat16, jnp.int32
NT = (((1,), (1,)), ((), ()))
TN = (((0,), (0,)), ((), ()))
TT = (((0,), (1,)), ((), ()))
MESH = pl.DeviceIdType.MESH
PIECES = 4
GROUP = 4
UNROLL = 224
SIDE = 4
ADAPTER_SCALE = 0.5
ROPE_BASE = 1000000.0
EPSILON = 1e-06


def iota(shape, dim):
    return lax.broadcasted_iota(I32, shape, dim)


def flat_row(x):
    rows, n = x.shape
    wide = jnp.concatenate([x.astype(F32)] * rows, axis=1)
    keep = lax.div(iota(wide.shape, 1), n) == iota(wide.shape, 0)
    return jnp.sum(jnp.where(keep, wide, 0.0), axis=0, keepdims=True)


def remote(src, dst, send, recv, device):
    return pltpu.make_async_remote_copy(
        src_ref=src, dst_ref=dst, send_sem=send, recv_sem=recv, device_id=device, device_id_type=MESH)


def entries_by_holder(holder, index, used, me, own, peers, cap):
    dest, index, used = flat_row(holder), flat_row(index), flat_row(used)
    count = dest.shape[1]
    to = dest == iota((peers, count), 0).astype(F32)
    earlier = jnp.where(iota((count, count), 0) < iota((count, count), 1), 1.0, 0.0).astype(BF16)
    before = jnp.dot(jnp.where(to, 1.0, 0.0).astype(BF16), earlier, preferred_element_type=F32)
    place = dest * cap + jnp.sum(jnp.where(to, before, 0.0), axis=0, keepdims=True)
    chosen = jnp.where(place == iota((peers * cap, count), 0).astype(F32), 1.0, 0.0).astype(BF16)
    sub = iota((128, count), 0)
    from_row = (me * own + lax.div(iota((1, count), 1), count // own)).astype(F32)
    fields = jnp.where(sub == 0, index, jnp.where(sub == 1, used, jnp.where(sub == 2, from_row, 0.0)))
    return lax.dot_general(chosen, fields.astype(BF16), NT, preferred_element_type=F32).astype(BF16)


def order_entries(ent, blocks, rows, positions, per_group):
    slots = ent.shape[0]
    entf = ent.astype(F32)
    pick = jnp.where(iota((16, 128), 0) == iota((16, 128), 1), 1.0, 0.0).astype(BF16)
    ent_t = lax.dot_general(pick, ent, NT, preferred_element_type=F32)
    blk_r, len_r, row_r = ent_t[0:1], ent_t[1:2], ent_t[2:3]
    valid_c = entf[:, 1:2] > 0
    key_c = jnp.where(valid_c, entf[:, 0:1], 999.0)
    key_r = jnp.where(len_r > 0, blk_r, 999.0)
    earlier = iota((slots, slots), 1) < iota((slots, slots), 0)
    within = jnp.sum(jnp.where((key_c == key_r) & earlier, 1.0, 0.0), axis=1, keepdims=True)
    block_of = iota((blocks, slots), 0).astype(F32) == key_r
    count = jnp.sum(jnp.where(block_of, 1.0, 0.0), axis=1, keepdims=True)
    chunks = jnp.floor((count + (GROUP - 1)) * (1.0 / GROUP))
    below = jnp.where(iota((blocks, blocks), 1) < iota((blocks, blocks), 0), 1.0, 0.0).astype(BF16)
    first = jnp.dot(below, jnp.broadcast_to(chunks, (blocks, 128)).astype(BF16), preferred_element_type=F32)
    own_block = jnp.where(key_c == iota((slots, blocks), 1).astype(F32), 1.0, 0.0).astype(BF16)
    first_c = jnp.dot(own_block, first.astype(BF16), preferred_element_type=F32)[:, 0:1]
    major = jnp.floor(within * (1.0 / GROUP))
    chunk_c, seat_c = first_c + major, within - major * GROUP
    place = jnp.where(valid_c, chunk_c * GROUP + seat_c, -1.0)
    sub = iota((16, slots), 0)
    fields = jnp.where(sub == 0, blk_r, jnp.where(sub == 1, len_r, jnp.where(sub == 2, row_r, 0.0))).astype(BF16)
    chosen = jnp.where(place == iota((slots, positions), 1).astype(F32), 1.0, 0.0).astype(BF16)
    table = jnp.dot(fields, chosen, preferred_element_type=F32)[0:8]
    sub = iota(table.shape, 0)
    table = table.astype(I32)
    table = jnp.clip(table, 0, jnp.where(sub == 0, blocks - 1, jnp.where(sub == 1, 1 << 16, rows - 1)))
    lane = iota((slots, 128), 1)
    seats = jnp.where(lane == 0, chunk_c, jnp.where(lane == 1, seat_c, 0.0)).astype(BF16)
    seats = lax.dot_general(pick, seats, NT, preferred_element_type=F32)
    where_r = jnp.where(len_r > 0, seats[0:1] * GROUP + seats[1:2], 0.0)
    local_r = row_r - (lax.div(iota((1, slots), 1), per_group) * 16).astype(F32)
    local_r = jnp.where(len_r > 0, local_r, -1.0)
    by_slot = jnp.clip(jnp.where(iota((8, slots), 0) == 0, where_r, local_r).astype(I32), -1, positions - 1)
    by_slot = jnp.where(iota((8, slots), 0) == 0, jnp.maximum(by_slot, 0), by_slot)
    return table, by_slot


def kernel(ht_h, w_h, dt_h, up_h, gain_h, freq_h, holder_h, index_h, used_h, tenant_h, held_h, k_h, v_h, wo_h,
           out_ref,
           ht, w, dt, up, gain, freq, holder, index, used, tenant, held, tenant_s, held_s, kbuf, vbuf, wo, wo_in, wo_t,
           part, pair, mine_a, mine_b, land_a, land_b, sum_a, sum_b, end_a, end_b, total, low_t, turned,
           ent_send, ent, tab_v, slot_v, tab, slot_s, q, o_st, e_st,
           partial, tops, partial_in, tops_in, merged, tops_out, parts, tops_all, flat, attended, terms, summed,
           in_sem, kv_sem, tab_sem, pair_send, pair_recv, a_send, a_recv, b_send, b_recv, a2_send, a2_recv,
           b2_send, b2_recv, en_send, en_recv, ag_send, ag_recv, fw_send, fw_recv,
           wo_send, wo_recv, x_send, x_recv, p_send, p_recv, t_send, t_recv, ag2_send, ag2_recv, z_send, z_recv):
    row, me = lax.axis_index("row"), lax.axis_index("kv")
    peers, planes = lax.axis_size("kv"), lax.axis_size("row")
    chips = peers // 2
    chip, core = me // 2, me % 2
    x, y = chip // SIDE, chip % SIDE
    partner = (row, 2 * chip + 1 - core)
    wide = w.shape[1]
    rows, heads, width = q.shape
    own = rows // peers
    cap = ent.shape[0] // peers
    blocks, toks, _ = kbuf.shape
    wide_a = mine_a.shape[3]
    barrier = pltpu.get_barrier_semaphore()

    def greet(i, c):
        pl.semaphore_signal(barrier, inc=1, device_id=(row, (me + i) % peers), device_id_type=MESH)
        return c

    def greet_plane(i, c):
        pl.semaphore_signal(barrier, inc=1, device_id=((row + i) % planes, me), device_id_type=MESH)
        pl.semaphore_signal(barrier, inc=1, device_id=((row + i) % planes, partner[1]), device_id_type=MESH)
        return c

    loads = [pltpu.make_async_copy(src, dst, in_sem.at[i]) for i, (src, dst) in enumerate((
        (ht_h, ht), (w_h, w), (holder_h, holder), (index_h, index), (used_h, used), (tenant_h, tenant),
        (held_h, held), (dt_h, dt), (tenant_h, tenant_s), (held_h, held_s), (gain_h, gain), (freq_h, freq),
        (up_h, up), (wo_h.at[:, :wide // 2], wo.at[0]), (wo_h.at[:, wide // 2:], wo.at[1])))]
    for copy in loads[:8]:
        copy.start()
    lax.fori_loop(1, peers, greet, 0)
    lax.fori_loop(1, planes, greet_plane, 0)
    step = blocks // PIECES
    pool = []
    for i in range(PIECES):
        at = pl.ds(i * step, step)
        pool += [pltpu.make_async_copy(k_h.at[at], kbuf.at[at], kv_sem.at[2 * i]),
                 pltpu.make_async_copy(v_h.at[at], vbuf.at[at], kv_sem.at[2 * i + 1])]
    for copy in loads[:8]:
        copy.wait()
    for copy in loads[8:] + pool:
        copy.start()

    part[:, :wide] = lax.dot_general(ht[...], w[...], TN, preferred_element_type=F32)
    low = lax.dot_general(ht[...], dt[...], TT, preferred_element_type=F32)
    rank = up.shape[1]
    is_tenant = jnp.where(tenant[...] == iota((held.shape[1], rows), 0), 1.0, 0.0).astype(BF16)
    held_b = jnp.broadcast_to(held[...].astype(F32), (16, held.shape[1])).astype(BF16)
    adapter = jnp.dot(held_b, is_tenant, preferred_element_type=F32)[0:8]
    adapter = jnp.transpose(adapter)[:, 0:1].astype(I32)
    low = jnp.where(lax.div(iota(low.shape, 1), rank) == adapter, low, 0.0)
    part[:, wide:] = sum(low[:, 128 * i: 128 * (i + 1)] for i in range(low.shape[1] // 128))

    pl.semaphore_wait(barrier, peers - 1 + 2 * (planes - 1))

    def pair_copy(d):
        return remote(part.at[pl.ds((2 * d + 1 - core) * own, own)], pair.at[d],
                      pair_send.at[d], pair_recv.at[d], partner)

    def chip_at(ox, oy):
        return (x + ox) % SIDE, (y + oy) % SIDE

    hops = (2, 1, 3, 0)
    for ox in hops:
        for oy in hops:
            dx, dy = chip_at(ox, oy)
            pair_copy(dx * SIDE + dy).start()

    ent_send[...] = entries_by_holder(holder[...], index[...], used[...], me, own, peers, cap)

    def a_copy(t, s):
        return remote(mine_a.at[t], land_a.at[s], a_send.at[t], a_recv.at[s], (row, 2 * (t * SIDE + y) + core))

    def b_copy(t, i, s):
        return remote(mine_b.at[t, i], land_b.at[s, i], b_send.at[t, i], b_recv.at[s, i],
                      (row, 2 * (x * SIDE + t) + core))

    for ox in hops:
        for oy in hops:
            dx, dy = chip_at(ox, oy)
            d = dx * SIDE + dy
            pair_copy(d).wait_recv()
            both = part[pl.ds((2 * d + core) * own, own), :] + pair[d]
            mine_a[dx, dy] = both[:, :wide_a]
            mine_b[dy, dx] = both[:, wide_a:]
            if oy:
                b_copy(dy, dx, y).start()
        if ox:
            a_copy(dx, x).start()

    def ent_copy(t, slot):
        return remote(ent_send.at[pl.ds(t * cap, cap)], ent.at[pl.ds(slot * cap, cap)],
                      en_send.at[t], en_recv.at[slot], (row, t))

    def ent_start(i, c):
        ent_copy((me + i) % peers, me).start()
        return c

    lax.fori_loop(1, peers, ent_start, 0)
    at = pl.ds(me * cap, cap)
    ent[at, :] = ent_send[at, :]
    for copy in loads[8:]:
        copy.wait()
    angles = (jnp.sum(used[...], axis=1, keepdims=True) - 1).astype(F32) * freq[...]
    cosine, sine = jnp.cos(angles), jnp.sin(angles)
    sine = jnp.where(iota(sine.shape, 1) < width // 2, -sine, sine)

    wo_copy = remote(wo.at[1 - core], wo_in, wo_send, wo_recv, partner)
    wo_copy.start()

    for copy in pool:
        copy.wait()

    def turn_keys(b, c):
        kbuf[b] = jnp.transpose(kbuf[b].reshape(toks // 2, 2 * width))
        return c

    lax.fori_loop(0, blocks, turn_keys, 0, unroll=4)

    def a2_copy(t, s):
        return remote(sum_a.at[t], end_a.at[s], a2_send.at[t], a2_recv.at[s], (row, 2 * (x * SIDE + t) + core))

    def b2_copy(t, s):
        return remote(sum_b.at[t], end_b.at[s], b2_send.at[t], b2_recv.at[s], (row, 2 * (t * SIDE + y) + core))

    steps = (1, 3, 2)
    for o in steps:
        a_copy((x + SIDE - o) % SIDE, (x + SIDE - o) % SIDE).wait_recv()
    sum_a[...] = mine_a[x] + land_a[(x + 1) % SIDE] + land_a[(x + 2) % SIDE] + land_a[(x + 3) % SIDE]
    for o in (2, 1, 3):
        a2_copy((y + o) % SIDE, y).start()
    for o in steps:
        for i in range(SIDE):
            b_copy((y + SIDE - o) % SIDE, i, (y + SIDE - o) % SIDE).wait_recv()
    sum_b[...] = mine_b[y] + land_b[(y + 1) % SIDE] + land_b[(y + 2) % SIDE] + land_b[(y + 3) % SIDE]
    for o in (2, 1, 3):
        b2_copy((x + o) % SIDE, x).start()

    for o in steps:
        a2_copy((y + SIDE - o) % SIDE, (y + SIDE - o) % SIDE).wait_recv()
    total[:, :wide_a] = sum_a[y] + end_a[(y + 1) % SIDE] + end_a[(y + 2) % SIDE] + end_a[(y + 3) % SIDE]
    for o in steps:
        b2_copy((x + SIDE - o) % SIDE, (x + SIDE - o) % SIDE).wait_recv()
    total[:, wide_a:] = sum_b[x] + end_b[(x + 1) % SIDE] + end_b[(x + 2) % SIDE] + end_b[(x + 3) % SIDE]

    low_t[...] = jnp.transpose(
        jnp.concatenate([total[:, wide:], jnp.zeros((128 - own, 128), F32)], axis=0)).reshape(low_t.shape)
    for r in range(own):
        adapter = held_s[0, tenant_s[0, me * own + r]]
        column = low_t[lax.rem(adapter, 128 // rank)][:, r:r + 1]
        more = jnp.sum(column * up[adapter], axis=0, keepdims=True)
        total[r:r + 1, :wide] += ADAPTER_SCALE * more
    gain_r = gain[...]
    for h in range(heads):
        t = total[:, h * width:(h + 1) * width]
        t = t * lax.rsqrt(jnp.mean(t * t, axis=1, keepdims=True) + EPSILON) * gain_r
        turned[:, h, :] = t * cosine + pltpu.roll(t, width // 2, 1) * sine
    q[pl.ds(me * own, own)] = turned[...].astype(BF16)

    def chip_by(i, sign):
        dx, dy = i // SIDE, i % SIDE
        return ((x + sign * dx + SIDE) % SIDE) * SIDE + (y + sign * dy + SIDE) % SIDE

    far = sorted(range(1, chips), key=lambda i: -(min(i // SIDE, SIDE - i // SIDE) + min(i % SIDE, SIDE - i % SIDE)))

    def q_copy(d, s):
        at = pl.ds((2 * s + core) * own, own)
        return remote(q.at[at], q.at[at], ag_send.at[d], ag_recv.at[s], (row, 2 * d + core))

    def q_relay(s, c):
        at = pl.ds((2 * s + c) * own, own)
        return remote(q.at[at], q.at[at], fw_send.at[s], fw_recv.at[s], partner)

    for i in far:
        q_copy(chip_by(i, 1), chip).start()
    q_relay(chip, core).start()

    def turn_values(b, c):
        both = vbuf[b].reshape(toks // 2, 2 * width)
        vbuf[b, :toks // 2] = both[:, :width]
        vbuf[b, toks // 2:] = both[:, width:]
        return c

    lax.fori_loop(0, blocks, turn_values, 0, unroll=4)

    def ent_wait(i, c):
        t = (me + peers - i) % peers
        ent_copy(t, t).wait_recv()
        return c

    lax.fori_loop(1, peers, ent_wait, 0)
    table, by_slot = order_entries(ent[...], blocks, rows, tab.shape[1], 2 * cap)
    tab_v[...] = table
    slot_v[...] = by_slot
    tables = (pltpu.make_async_copy(tab_v, tab, tab_sem.at[0]), pltpu.make_async_copy(slot_v, slot_s, tab_sem.at[1]))
    for copy in tables:
        copy.start()

    def pair_sent(d, c):
        pair_copy(d).wait_send()
        return c

    lax.fori_loop(0, chips, pair_sent, 0)
    for o in (1, 2, 3):
        a_copy((x + o) % SIDE, x).wait_send()
        for i in range(SIDE):
            b_copy((y + o) % SIDE, i, y).wait_send()
        a2_copy((y + o) % SIDE, y).wait_send()
        b2_copy((x + o) % SIDE, x).wait_send()

    for i in far:
        s = chip_by(i, -1)
        q_copy(s, s).wait_recv()
        q_relay(s, core).start()

    def q_landed(d, c):
        q_relay(d, 1 - core).wait_recv()
        return c

    lax.fori_loop(0, chips, q_landed, 0)
    for copy in tables:
        copy.wait()

    coef = math.log2(math.e) / math.sqrt(width)
    half = heads // 2
    col = iota((heads, toks // 2), 1)
    upper = iota((heads, width), 0) < half
    none = jnp.zeros((heads, width), BF16)

    def chunk(c):
        base = c * GROUP
        b = tab[0, base]
        qs = [q[tab[2, base + g]] for g in range(GROUP)]
        qs = jnp.concatenate([jnp.concatenate(
            [jnp.where(upper, one, none), jnp.where(upper, none, one)], axis=1) for one in qs], axis=0)
        s = jnp.dot(qs, kbuf[b], preferred_element_type=F32)
        s = jnp.concatenate(
            [jnp.where(col < tab[1, base + g], s[heads * g: heads * (g + 1)], NEG) for g in range(GROUP)], axis=0)
        m = jnp.max(s, axis=1, keepdims=True)
        wt = jnp.exp2((s - m) * coef)
        l = jnp.sum(wt, axis=1, keepdims=True)
        vs = jnp.concatenate([vbuf[b, :toks // 2], vbuf[b, toks // 2:]], axis=1)
        o = jnp.dot(wt.astype(BF16), vs, preferred_element_type=F32).reshape(GROUP, 2, half, 2 * width)
        o = jnp.concatenate([o[:, 0:1, :, :width], o[:, 1:2, :, width:]], axis=1).reshape(GROUP * heads, width) / l
        e = jnp.broadcast_to(m * coef + jnp.log2(l), o.shape)
        return o.reshape(GROUP, 2, half, width), e.reshape(GROUP, 2, half, width)

    def chunks(i, c):
        done = [chunk(i * UNROLL + u) for u in range(UNROLL)]
        for u in range(UNROLL):
            o, e = done[u]
            at = pl.ds((i * UNROLL + u) * GROUP, GROUP)
            o_st[at] = o
            e_st[at] = e
        return c

    lax.fori_loop(0, tab.shape[1] // (GROUP * UNROLL), chunks, 0)

    lane = iota((half, 128), 1)
    same_head = (lane & (half - 1)) == iota((half, 128), 0)
    lane_row = jnp.where(same_head, lax.div(lane, half), -2)
    slots = 2 * cap

    def merge(d, hv):
        tops_of, outs = [], []
        for p in range(slots):
            at = slot_s[0, d * slots + p]
            tops_of.append(jnp.where(lane_row == slot_s[1, d * slots + p], e_st[at, hv], NEG))
            outs.append(o_st[at, hv])
        es = jnp.concatenate(tops_of, axis=0)
        top = jnp.max(es, axis=0, keepdims=True)
        f = jnp.exp2(es - top)
        l = jnp.sum(f, axis=0, keepdims=True)
        f = (f * (1.0 / l)).astype(BF16)
        os = jnp.concatenate(outs, axis=0).astype(BF16)
        return lax.dot_general(f, os, TN, preferred_element_type=F32).astype(BF16), top + jnp.log2(l)

    def merges(hv):
        done = [merge(d, hv) for d in range(chips)]
        for d in range(chips):
            partial[hv, d] = done[d][0]
        tops[hv] = jnp.concatenate([one[1] for one in done], axis=0)

    x_copies = (remote(tops.at[1 - core], tops_in, x_send.at[0], x_recv.at[0], partner),
                remote(partial.at[1 - core], partial_in, x_send.at[1], x_recv.at[1], partner))

    merges(1 - core)
    for copy in x_copies:
        copy.start()
    merges(core)

    def columns(fs):
        n = fs.shape[0]
        return jnp.transpose(jnp.concatenate([fs, jnp.zeros((128 - n, 128), F32)], axis=0))

    order = far + [0]
    x_copies[0].wait_recv()
    t0 = jnp.concatenate([tops[core, pl.ds(chip_by(i, 1), 1), :] for i in order], axis=0)
    t1 = jnp.concatenate([tops_in[pl.ds(chip_by(i, 1), 1), :] for i in order], axis=0)
    top = jnp.maximum(t0, t1)
    f0, f1 = jnp.exp2(t0 - top), jnp.exp2(t1 - top)
    l = f0 + f1
    over = top + jnp.log2(l)
    for k in range(chips):
        tops_out[k] = jnp.broadcast_to(over[k:k + 1], (8, 128))
    f = columns(jnp.concatenate([f0 / l, f1 / l], axis=0))

    def t_copy(k, d, s):
        return remote(tops_out.at[k], tops_all.at[s], t_send.at[k], t_recv.at[s], (row, 2 * d + core))

    def p_copy(k, d, s):
        return remote(merged.at[k], parts.at[s], p_send.at[k], p_recv.at[s], (row, 2 * d + core))

    for k, i in enumerate(order):
        if i:
            t_copy(k, chip_by(i, 1), chip).start()
    x_copies[1].wait_recv()
    for k, i in enumerate(order):
        d = chip_by(i, 1)
        both = (f[:, k:k + 1] * partial[core, d].astype(F32)
                + f[:, chips + k:chips + k + 1] * partial_in[d].astype(F32)).astype(BF16)
        if i:
            merged[k] = both
            p_copy(k, d, chip).start()
        else:
            parts[chip] = both
            tops_all[chip] = tops_out[k]

    def ent_sent(i, c):
        ent_copy((me + i) % peers, me).wait_send()
        return c

    lax.fori_loop(1, peers, ent_sent, 0)

    def q_sent(i, c):
        q_copy((chip + i) % chips, chip).wait_send()
        return c

    lax.fori_loop(1, chips, q_sent, 0)

    def q_relayed(d, c):
        q_relay(d, core).wait_send()
        return c

    lax.fori_loop(0, chips, q_relayed, 0)
    for copy in x_copies:
        copy.wait_send()
    wo_copy.wait()
    wo_t[0] = jnp.transpose(wo[core])
    wo_t[1] = jnp.transpose(wo_in[...])

    for i in far[::-1]:
        s = chip_by(i, -1)
        t_copy(0, s, s).wait_recv()
    top = tops_all[:, 0, :]
    f = jnp.exp2(top - jnp.max(top, axis=0, keepdims=True))
    f = columns(f / jnp.sum(f, axis=0, keepdims=True))
    for i in far[::-1]:
        s = chip_by(i, -1)
        p_copy(0, s, s).wait_recv()
    acc = jnp.zeros((128, width), F32)
    for s in range(chips):
        acc += f[:, s:s + 1] * parts[s].astype(F32)
    flat[...] = acc
    pair_rows = 2 * own
    here = pl.ds(chip * pair_rows, pair_rows)
    for h in range(half):
        attended[here, h * width:(h + 1) * width] = flat[pl.ds(h, pair_rows, stride=half), :].astype(BF16)

    def at_copy(d, s):
        at = pl.ds(s * pair_rows, pair_rows)
        return remote(attended.at[at], attended.at[at], ag2_send.at[d], ag2_recv.at[s], (row, 2 * d + core))

    by_row = [SIDE * ox + oy for ox in hops for oy in hops]
    for i in by_row[:-1]:
        at_copy(chip_by(i, 1), chip).start()
    for k, i in enumerate(far):
        t_copy(k, chip_by(i, 1), chip).wait_send()
        p_copy(k, chip_by(i, 1), chip).wait_send()
    out_rows = out_ref.shape[0]

    def z_copy(c, z, s):
        return remote(terms.at[c, pl.ds(z * out_rows, out_rows)], summed.at[c, s], z_send.at[c, z], z_recv.at[c, s],
                      (z, partner[1] if c else me))

    for ox in hops:
        for oy in hops:
            if ox or oy:
                s = chip_by(SIDE * ox + oy, -1)
                at_copy(s, s).wait_recv()
        z = (x + SIDE - ox) % SIDE
        at = pl.ds(z * out_rows, out_rows)
        some = attended[at, :]
        terms[1, at, :] = jnp.dot(some, wo_t[1], preferred_element_type=F32).astype(BF16)
        z_copy(1, z, row).start()
        terms[0, at, :] = jnp.dot(some, wo_t[0], preferred_element_type=F32).astype(BF16)

        @pl.when(z != row)
        def _():
            z_copy(0, z, row).start()

    for i in far:
        at_copy(chip_by(i, 1), chip).wait_send()

    result = terms[0, pl.ds(row * out_rows, out_rows), :].astype(F32)
    for c in (1, 0):
        for i in range(c ^ 1, planes):
            z = (row + i) % planes
            z_copy(c, z, z).wait_recv()
            result += summed[c, z].astype(F32)
    out_ref[...] = result
    for c in (1, 0):
        for i in range(c ^ 1, planes):
            z_copy(c, (row + i) % planes, row).wait_send()


def run(ht, w, dt, up, gain, freq, holder, index, used, tenant, held, k, v, wo, peers, planes):
    rows, wide, width = ht.shape[1], w.shape[1], gain.shape[1]
    own = rows // peers
    cap = 2 * own * holder.shape[1] // peers
    chips = peers // 2
    heads = wide // width
    blocks, toks, _ = k.shape
    slots = peers * cap
    count = -(-(slots // GROUP + blocks * (GROUP - 1) // GROUP) // UNROLL) * UNROLL
    positions = count * GROUP
    wide_a = (wide + 128) // 256 * 128 + 128
    wide_b = wide + 128 - wide_a
    cols = wo.shape[0]
    vm = pltpu.VMEM
    dma = pltpu.SemaphoreType.DMA
    args = (ht, w, dt, up, gain, freq, holder, index, used, tenant, held, k, v, wo)
    return pl.pallas_call(
        kernel,
        out_shape=jax.ShapeDtypeStruct((rows // planes, cols), F32),
        in_specs=[pl.BlockSpec(memory_space=pltpu.HBM)] * len(args),
        out_specs=pl.BlockSpec(memory_space=pltpu.VMEM),
        scratch_shapes=[vm(a.shape, a.dtype) for a in args[:11]] + [
            pltpu.SMEM(tenant.shape, I32), pltpu.SMEM(held.shape, I32),
            vm(k.shape, BF16), vm(v.shape, BF16), vm((2, cols, wide // 2), BF16), vm((cols, wide // 2), BF16), vm((2, wide // 2, cols), BF16),
            vm((rows, wide + 128), F32), vm((chips, own, wide + 128), F32),
            vm((SIDE, SIDE, own, wide_a), F32), vm((SIDE, SIDE, own, wide_b), F32),
            vm((SIDE, SIDE, own, wide_a), F32), vm((SIDE, SIDE, own, wide_b), F32),
            vm((SIDE, own, wide_a), F32), vm((SIDE, own, wide_b), F32),
            vm((SIDE, own, wide_a), F32), vm((SIDE, own, wide_b), F32),
            vm((own, wide + 128), F32), vm((128 // up.shape[1], up.shape[1], 128), F32), vm((own, heads, width), F32),
            vm((slots, 128), BF16), vm((slots, 128), BF16), vm((8, positions), I32), vm((8, slots), I32),
            pltpu.SMEM((8, positions), I32), pltpu.SMEM((8, slots), I32),
            vm((rows, heads, width), BF16),
            vm((positions, 2, heads // 2, width), F32), vm((positions, 2, heads // 2, width), F32),
            vm((2, chips, 128, width), BF16), vm((2, chips, 128), F32),
            vm((chips, 128, width), BF16), vm((chips, 128), F32),
            vm((chips, 128, width), BF16), vm((chips, 8, 128), F32),
            vm((chips, 128, width), BF16), vm((chips, 8, 128), F32), vm((128, width), F32),
            vm((rows, wide // 2), BF16), vm((2, rows, cols), BF16), vm((2, planes, rows // planes, cols), BF16),
            dma((15,)), dma((2 * PIECES,)), dma((2,)), dma((chips,)), dma((chips,)),
            dma((SIDE,)), dma((SIDE,)), dma((SIDE, SIDE)), dma((SIDE, SIDE)),
            dma((SIDE,)), dma((SIDE,)), dma((SIDE,)), dma((SIDE,)),
            dma((peers,)), dma((peers,)), dma((chips,)), dma((chips,)), dma((chips,)), dma((chips,)),
            dma, dma, dma((2,)), dma((2,)), dma((chips,)), dma((chips,)), dma((chips,)), dma((chips,)),
            dma((chips,)), dma((chips,)), dma((2, planes)), dma((2, planes)),
        ],
        compiler_params=pltpu.CompilerParams(
            vmem_limit_bytes=62 * 2**20, collective_id=0, has_side_effects=True),
        name="decode",
    )(*args)


def local(hidden, query_weight, adapter_down_weight, adapter_up_weight, query_norm_gain, paged_key_cache,
          paged_value_cache, output_weight, holder, holder_block_index, block_used_length, tenant, tenant_adapter):
    peers, planes = lax.axis_size("kv"), lax.axis_size("row")
    count, _, rank = adapter_down_weight.shape
    width = query_norm_gain.shape[0]
    blocks, toks, kv_heads, _ = paged_key_cache.shape
    half = width // 2
    freq = (ROPE_BASE ** (-(np.arange(half) * 2.0) / width)).astype(np.float32)
    freq = jnp.asarray(np.concatenate([freq, freq])[None, :])
    down = jnp.transpose(adapter_down_weight, (0, 2, 1)).reshape(count * rank, -1)
    pool = (blocks, toks * kv_heads, width)
    return run(hidden.T, query_weight, down, adapter_up_weight, query_norm_gain[None, :], freq, holder,
               holder_block_index, block_used_length, tenant[None, :], tenant_adapter[None, :],
               paged_key_cache.reshape(pool), paged_value_cache.reshape(pool), output_weight.T, peers, planes).astype(BF16)


def solution(mesh):
    return jax.shard_map(
        local,
        mesh=mesh,
        in_specs=(
            P(None, "kv"),
            P("kv", "row"),
            P(None, "kv", None),
            P(None, None, "row"),
            P(),
            P("kv", None, "row", None),
            P("kv", None, "row", None),
            P("row", "kv"),
            P("kv", None),
            P("kv", None),
            P("kv", None),
            P(),
            P(),
        ),
        out_specs=P("row", "kv"),
        check_vma=False,
    )
```

```python
import functools
import math

import jax
import jax.numpy as jnp
import numpy as np
from jax import lax
from jax.experimental import pallas as pl
from jax.experimental.pallas import tpu as pltpu
from jax.sharding import PartitionSpec as P

NEG = -1e30
F32, BF16, I32 = jnp.float32, jnp.bfloat16, jnp.int32
NT = (((1,), (1,)), ((), ()))
TN = (((0,), (0,)), ((), ()))
TT = (((0,), (1,)), ((), ()))
MESH = pl.DeviceIdType.MESH
PIECES = 4
GROUP = 4
UNROLL = 224
SIDE = 4
ADAPTER_SCALE = 0.5
ROPE_BASE = 1000000.0
EPSILON = 1e-06


def iota(shape, dim):
    return lax.broadcasted_iota(I32, shape, dim)


def flat_row(x):
    rows, n = x.shape
    wide = jnp.concatenate([x.astype(F32)] * rows, axis=1)
    keep = lax.div(iota(wide.shape, 1), n) == iota(wide.shape, 0)
    return jnp.sum(jnp.where(keep, wide, 0.0), axis=0, keepdims=True)


def remote(src, dst, send, recv, device):
    return pltpu.make_async_remote_copy(
        src_ref=src, dst_ref=dst, send_sem=send, recv_sem=recv, device_id=device, device_id_type=MESH)


def entries_by_holder(holder, index, used, me, own, peers, cap):
    dest, index, used = flat_row(holder), flat_row(index), flat_row(used)
    count = dest.shape[1]
    to = dest == iota((peers, count), 0).astype(F32)
    earlier = jnp.where(iota((count, count), 0) < iota((count, count), 1), 1.0, 0.0).astype(BF16)
    before = jnp.dot(jnp.where(to, 1.0, 0.0).astype(BF16), earlier, preferred_element_type=F32)
    place = dest * cap + jnp.sum(jnp.where(to, before, 0.0), axis=0, keepdims=True)
    chosen = jnp.where(place == iota((peers * cap, count), 0).astype(F32), 1.0, 0.0).astype(BF16)
    sub = iota((128, count), 0)
    from_row = (me * own + lax.div(iota((1, count), 1), count // own)).astype(F32)
    fields = jnp.where(sub == 0, index, jnp.where(sub == 1, used, jnp.where(sub == 2, from_row, 0.0)))
    return lax.dot_general(chosen, fields.astype(BF16), NT, preferred_element_type=F32).astype(BF16)


def order_entries(ent, blocks, rows, positions, per_group):
    slots = ent.shape[0]
    entf = ent.astype(F32)
    pick = jnp.where(iota((16, 128), 0) == iota((16, 128), 1), 1.0, 0.0).astype(BF16)
    ent_t = lax.dot_general(pick, ent, NT, preferred_element_type=F32)
    blk_r, len_r, row_r = ent_t[0:1], ent_t[1:2], ent_t[2:3]
    valid_c = entf[:, 1:2] > 0
    key_c = jnp.where(valid_c, entf[:, 0:1], 999.0)
    key_r = jnp.where(len_r > 0, blk_r, 999.0)
    earlier = iota((slots, slots), 1) < iota((slots, slots), 0)
    within = jnp.sum(jnp.where((key_c == key_r) & earlier, 1.0, 0.0), axis=1, keepdims=True)
    block_of = iota((blocks, slots), 0).astype(F32) == key_r
    count = jnp.sum(jnp.where(block_of, 1.0, 0.0), axis=1, keepdims=True)
    chunks = jnp.floor((count + (GROUP - 1)) * (1.0 / GROUP))
    below = jnp.where(iota((blocks, blocks), 1) < iota((blocks, blocks), 0), 1.0, 0.0).astype(BF16)
    first = jnp.dot(below, jnp.broadcast_to(chunks, (blocks, 128)).astype(BF16), preferred_element_type=F32)
    own_block = jnp.where(key_c == iota((slots, blocks), 1).astype(F32), 1.0, 0.0).astype(BF16)
    first_c = jnp.dot(own_block, first.astype(BF16), preferred_element_type=F32)[:, 0:1]
    major = jnp.floor(within * (1.0 / GROUP))
    chunk_c, seat_c = first_c + major, within - major * GROUP
    place = jnp.where(valid_c, chunk_c * GROUP + seat_c, -1.0)
    sub = iota((16, slots), 0)
    fields = jnp.where(sub == 0, blk_r, jnp.where(sub == 1, len_r, jnp.where(sub == 2, row_r, 0.0))).astype(BF16)
    chosen = jnp.where(place == iota((slots, positions), 1).astype(F32), 1.0, 0.0).astype(BF16)
    table = jnp.dot(fields, chosen, preferred_element_type=F32)[0:8]
    sub = iota(table.shape, 0)
    table = table.astype(I32)
    table = jnp.clip(table, 0, jnp.where(sub == 0, blocks - 1, jnp.where(sub == 1, 1 << 16, rows - 1)))
    lane = iota((slots, 128), 1)
    seats = jnp.where(lane == 0, chunk_c, jnp.where(lane == 1, seat_c, 0.0)).astype(BF16)
    seats = lax.dot_general(pick, seats, NT, preferred_element_type=F32)
    where_r = jnp.where(len_r > 0, seats[0:1] * GROUP + seats[1:2], 0.0)
    local_r = row_r - (lax.div(iota((1, slots), 1), per_group) * 16).astype(F32)
    local_r = jnp.where(len_r > 0, local_r, -1.0)
    by_slot = jnp.clip(jnp.where(iota((8, slots), 0) == 0, where_r, local_r).astype(I32), -1, positions - 1)
    by_slot = jnp.where(iota((8, slots), 0) == 0, jnp.maximum(by_slot, 0), by_slot)
    return table, by_slot


def kernel(ht_h, w_h, dt_h, up_h, gain_h, freq_h, holder_h, index_h, used_h, tenant_h, held_h, k_h, v_h, wo_h,
           out_ref,
           ht, w, dt, up, gain, freq, holder, index, used, tenant, held, tenant_s, held_s, kbuf, vbuf, wo, wo_in, wo_t,
           part, pair, mine_a, mine_b, land_a, land_b, sum_a, sum_b, end_a, end_b, total, low_t, turned,
           ent_send, ent, tab_v, slot_v, tab, slot_s, q, o_st, e_st,
           partial, tops, partial_in, tops_in, merged, tops_out, parts, tops_all, attended, terms, summed,
           in_sem, kv_sem, tab_sem, pair_send, pair_recv, a_send, a_recv, b_send, b_recv, a2_send, a2_recv,
           b2_send, b2_recv, en_send, en_recv, ag_send, ag_recv, fw_send, fw_recv,
           wo_send, wo_recv, x_send, x_recv, p_send, p_recv, t_send, t_recv, ag2_send, ag2_recv, z_send, z_recv):
    row, me = lax.axis_index("row"), lax.axis_index("kv")
    peers, planes = lax.axis_size("kv"), lax.axis_size("row")
    chips = peers // 2
    chip, core = me // 2, me % 2
    x, y = chip // SIDE, chip % SIDE
    partner = (row, 2 * chip + 1 - core)
    wide = w.shape[1]
    rows, heads, width = q.shape
    own = rows // peers
    cap = ent.shape[0] // peers
    blocks, toks, _ = kbuf.shape
    wide_a = mine_a.shape[3]
    barrier = pltpu.get_barrier_semaphore()

    def greet(i, c):
        pl.semaphore_signal(barrier, inc=1, device_id=(row, (me + i) % peers), device_id_type=MESH)
        return c

    def greet_plane(i, c):
        pl.semaphore_signal(barrier, inc=1, device_id=((row + i) % planes, me), device_id_type=MESH)
        pl.semaphore_signal(barrier, inc=1, device_id=((row + i) % planes, partner[1]), device_id_type=MESH)
        return c

    loads = [pltpu.make_async_copy(src, dst, in_sem.at[i]) for i, (src, dst) in enumerate((
        (ht_h, ht), (w_h, w), (holder_h, holder), (index_h, index), (used_h, used), (tenant_h, tenant),
        (held_h, held), (dt_h, dt), (tenant_h, tenant_s), (held_h, held_s), (gain_h, gain), (freq_h, freq),
        (up_h, up), (wo_h.at[:, :wide // 2], wo.at[0]), (wo_h.at[:, wide // 2:], wo.at[1])))]
    for copy in loads[:8]:
        copy.start()
    lax.fori_loop(1, peers, greet, 0)
    lax.fori_loop(1, planes, greet_plane, 0)
    step = blocks // PIECES
    pool = []
    for i in range(PIECES):
        at = pl.ds(i * step, step)
        pool += [pltpu.make_async_copy(k_h.at[at], kbuf.at[at], kv_sem.at[2 * i]),
                 pltpu.make_async_copy(v_h.at[at], vbuf.at[at], kv_sem.at[2 * i + 1])]
    for copy in loads[:8]:
        copy.wait()
    for copy in loads[8:] + pool:
        copy.start()

    part[:, :wide] = lax.dot_general(ht[...], w[...], TN, preferred_element_type=F32)
    low = lax.dot_general(ht[...], dt[...], TT, preferred_element_type=F32)
    rank = up.shape[1]
    is_tenant = jnp.where(tenant[...] == iota((held.shape[1], rows), 0), 1.0, 0.0).astype(BF16)
    held_b = jnp.broadcast_to(held[...].astype(F32), (16, held.shape[1])).astype(BF16)
    adapter = jnp.dot(held_b, is_tenant, preferred_element_type=F32)[0:8]
    adapter = jnp.transpose(adapter)[:, 0:1].astype(I32)
    low = jnp.where(lax.div(iota(low.shape, 1), rank) == adapter, low, 0.0)
    part[:, wide:] = sum(low[:, 128 * i: 128 * (i + 1)] for i in range(low.shape[1] // 128))

    pl.semaphore_wait(barrier, peers - 1 + 2 * (planes - 1))

    def pair_copy(d):
        return remote(part.at[pl.ds((2 * d + 1 - core) * own, own)], pair.at[d],
                      pair_send.at[d], pair_recv.at[d], partner)

    def chip_at(ox, oy):
        return (x + ox) % SIDE, (y + oy) % SIDE

    hops = (2, 1, 3, 0)
    for ox in hops:
        for oy in hops:
            dx, dy = chip_at(ox, oy)
            pair_copy(dx * SIDE + dy).start()

    ent_send[...] = entries_by_holder(holder[...], index[...], used[...], me, own, peers, cap)

    def a_copy(t, s):
        return remote(mine_a.at[t], land_a.at[s], a_send.at[t], a_recv.at[s], (row, 2 * (t * SIDE + y) + core))

    def b_copy(t, i, s):
        return remote(mine_b.at[t, i], land_b.at[s, i], b_send.at[t, i], b_recv.at[s, i],
                      (row, 2 * (x * SIDE + t) + core))

    for ox in hops:
        for oy in hops:
            dx, dy = chip_at(ox, oy)
            d = dx * SIDE + dy
            pair_copy(d).wait_recv()
            both = part[pl.ds((2 * d + core) * own, own), :] + pair[d]
            mine_a[dx, dy] = both[:, :wide_a]
            mine_b[dy, dx] = both[:, wide_a:]
            if oy:
                b_copy(dy, dx, y).start()
        if ox:
            a_copy(dx, x).start()

    def ent_copy(t, slot):
        return remote(ent_send.at[pl.ds(t * cap, cap)], ent.at[pl.ds(slot * cap, cap)],
                      en_send.at[t], en_recv.at[slot], (row, t))

    def ent_start(i, c):
        ent_copy((me + i) % peers, me).start()
        return c

    lax.fori_loop(1, peers, ent_start, 0)
    at = pl.ds(me * cap, cap)
    ent[at, :] = ent_send[at, :]
    for copy in loads[8:]:
        copy.wait()
    angles = (jnp.sum(used[...], axis=1, keepdims=True) - 1).astype(F32) * freq[...]
    cosine, sine = jnp.cos(angles), jnp.sin(angles)
    sine = jnp.where(iota(sine.shape, 1) < width // 2, -sine, sine)

    wo_copy = remote(wo.at[1 - core], wo_in, wo_send, wo_recv, partner)
    wo_copy.start()

    for copy in pool:
        copy.wait()

    def turn_keys(b, c):
        kbuf[b] = jnp.transpose(kbuf[b].reshape(toks // 2, 2 * width))
        return c

    lax.fori_loop(0, blocks, turn_keys, 0, unroll=4)

    def a2_copy(t, s):
        return remote(sum_a.at[t], end_a.at[s], a2_send.at[t], a2_recv.at[s], (row, 2 * (x * SIDE + t) + core))

    def b2_copy(t, s):
        return remote(sum_b.at[t], end_b.at[s], b2_send.at[t], b2_recv.at[s], (row, 2 * (t * SIDE + y) + core))

    steps = (1, 3, 2)
    for o in steps:
        a_copy((x + SIDE - o) % SIDE, (x + SIDE - o) % SIDE).wait_recv()
    sum_a[...] = mine_a[x] + land_a[(x + 1) % SIDE] + land_a[(x + 2) % SIDE] + land_a[(x + 3) % SIDE]
    for o in (2, 1, 3):
        a2_copy((y + o) % SIDE, y).start()
    for o in steps:
        for i in range(SIDE):
            b_copy((y + SIDE - o) % SIDE, i, (y + SIDE - o) % SIDE).wait_recv()
    sum_b[...] = mine_b[y] + land_b[(y + 1) % SIDE] + land_b[(y + 2) % SIDE] + land_b[(y + 3) % SIDE]
    for o in (2, 1, 3):
        b2_copy((x + o) % SIDE, x).start()

    for o in steps:
        a2_copy((y + SIDE - o) % SIDE, (y + SIDE - o) % SIDE).wait_recv()
    total[:, :wide_a] = sum_a[y] + end_a[(y + 1) % SIDE] + end_a[(y + 2) % SIDE] + end_a[(y + 3) % SIDE]
    for o in steps:
        b2_copy((x + SIDE - o) % SIDE, (x + SIDE - o) % SIDE).wait_recv()
    total[:, wide_a:] = sum_b[x] + end_b[(x + 1) % SIDE] + end_b[(x + 2) % SIDE] + end_b[(x + 3) % SIDE]

    low_t[...] = jnp.transpose(
        jnp.concatenate([total[:, wide:], jnp.zeros((128 - own, 128), F32)], axis=0)).reshape(low_t.shape)
    for r in range(own):
        adapter = held_s[0, tenant_s[0, me * own + r]]
        column = low_t[lax.rem(adapter, 128 // rank)][:, r:r + 1]
        more = jnp.sum(column * up[adapter], axis=0, keepdims=True)
        total[r:r + 1, :wide] += ADAPTER_SCALE * more
    gain_r = gain[...]
    for h in range(heads):
        t = total[:, h * width:(h + 1) * width]
        t = t * lax.rsqrt(jnp.mean(t * t, axis=1, keepdims=True) + EPSILON) * gain_r
        turned[:, h, :] = t * cosine + pltpu.roll(t, width // 2, 1) * sine
    q[pl.ds(me * own, own)] = turned[...].astype(BF16)

    def chip_by(i, sign):
        i = lax.rem(5 * i, chips)
        dx, dy = lax.div(i, SIDE), lax.rem(i, SIDE)
        return (lax.rem(x + sign * dx + SIDE, SIDE)) * SIDE + lax.rem(y + sign * dy + SIDE, SIDE)

    def each(first, last, do):
        def step(i, c):
            do(i)
            return c

        lax.fori_loop(first, last, step, 0)

    def q_copy(d, s):
        at = pl.ds((2 * s + core) * own, own)
        return remote(q.at[at], q.at[at], ag_send.at[d], ag_recv.at[s], (row, 2 * d + core))

    def q_relay(s, c):
        at = pl.ds((2 * s + c) * own, own)
        return remote(q.at[at], q.at[at], fw_send.at[s], fw_recv.at[s], partner)

    each(1, chips, lambda i: q_copy(chip_by(i, 1), chip).start())
    q_relay(chip, core).start()

    def turn_values(b, c):
        both = vbuf[b].reshape(toks // 2, 2 * width)
        vbuf[b, :toks // 2] = both[:, :width]
        vbuf[b, toks // 2:] = both[:, width:]
        return c

    lax.fori_loop(0, blocks, turn_values, 0, unroll=4)

    def ent_wait(i, c):
        t = (me + peers - i) % peers
        ent_copy(t, t).wait_recv()
        return c

    lax.fori_loop(1, peers, ent_wait, 0)
    table, by_slot = order_entries(ent[...], blocks, rows, tab.shape[1], 2 * cap)
    tab_v[...] = table
    slot_v[...] = by_slot
    tables = (pltpu.make_async_copy(tab_v, tab, tab_sem.at[0]), pltpu.make_async_copy(slot_v, slot_s, tab_sem.at[1]))
    for copy in tables:
        copy.start()

    def pair_sent(d, c):
        pair_copy(d).wait_send()
        return c

    lax.fori_loop(0, chips, pair_sent, 0)
    for o in (1, 2, 3):
        a_copy((x + o) % SIDE, x).wait_send()
        for i in range(SIDE):
            b_copy((y + o) % SIDE, i, y).wait_send()
        a2_copy((y + o) % SIDE, y).wait_send()
        b2_copy((x + o) % SIDE, x).wait_send()

    def relay(i):
        s = chip_by(i, -1)
        q_copy(s, s).wait_recv()
        q_relay(s, core).start()

    each(1, chips, relay)

    def q_landed(d, c):
        q_relay(d, 1 - core).wait_recv()
        return c

    lax.fori_loop(0, chips, q_landed, 0)
    for copy in tables:
        copy.wait()

    coef = math.log2(math.e) / math.sqrt(width)
    half = heads // 2
    col = iota((heads, toks // 2), 1)
    upper = iota((heads, width), 0) < half
    none = jnp.zeros((heads, width), BF16)

    def chunk(c):
        base = c * GROUP
        b = tab[0, base]
        qs = [q[tab[2, base + g]] for g in range(GROUP)]
        qs = jnp.concatenate([jnp.concatenate(
            [jnp.where(upper, one, none), jnp.where(upper, none, one)], axis=1) for one in qs], axis=0)
        s = jnp.dot(qs, kbuf[b], preferred_element_type=F32)
        s = jnp.concatenate(
            [jnp.where(col < tab[1, base + g], s[heads * g: heads * (g + 1)], NEG) for g in range(GROUP)], axis=0)
        m = jnp.max(s, axis=1, keepdims=True)
        wt = jnp.exp2((s - m) * coef)
        l = jnp.sum(wt, axis=1, keepdims=True)
        vs = jnp.concatenate([vbuf[b, :toks // 2], vbuf[b, toks // 2:]], axis=1)
        o = jnp.dot(wt.astype(BF16), vs, preferred_element_type=F32).reshape(GROUP, 2, half, 2 * width)
        o = jnp.concatenate([o[:, 0:1, :, :width], o[:, 1:2, :, width:]], axis=1).reshape(GROUP * heads, width) / l
        e = jnp.broadcast_to(m * coef + jnp.log2(l), o.shape)
        return o.reshape(GROUP, 2, half, width), e.reshape(GROUP, 2, half, width)

    def chunks(i, c):
        done = [chunk(i * UNROLL + u) for u in range(UNROLL)]
        for u in range(UNROLL):
            o, e = done[u]
            at = pl.ds((i * UNROLL + u) * GROUP, GROUP)
            o_st[at] = o
            e_st[at] = e
        return c

    lax.fori_loop(0, tab.shape[1] // (GROUP * UNROLL), chunks, 0)

    lane = iota((half, 128), 1)
    same_head = lax.div(lane, 128 // half) == iota((half, 128), 0)
    lane_row = jnp.where(same_head, lane & (128 // half - 1), -2)
    slots = 2 * cap

    def merge(d, hv):
        tops_of, outs = [], []
        for p in range(slots):
            at = slot_s[0, d * slots + p]
            tops_of.append(jnp.where(lane_row == slot_s[1, d * slots + p], e_st[at, hv], NEG))
            outs.append(o_st[at, hv])
        es = jnp.concatenate(tops_of, axis=0)
        top = jnp.max(es, axis=0, keepdims=True)
        f = jnp.exp2(es - top)
        l = jnp.sum(f, axis=0, keepdims=True)
        f = (f * (1.0 / l)).astype(BF16)
        os = jnp.concatenate(outs, axis=0).astype(BF16)
        return lax.dot_general(f, os, TN, preferred_element_type=F32).astype(BF16), top + jnp.log2(l)

    def merges(hv):
        done = [merge(d, hv) for d in range(chips)]
        for d in range(chips):
            partial[hv, d] = done[d][0]
        tops[hv] = jnp.concatenate([one[1] for one in done], axis=0)

    x_copies = (remote(tops.at[1 - core], tops_in, x_send.at[0], x_recv.at[0], partner),
                remote(partial.at[1 - core], partial_in, x_send.at[1], x_recv.at[1], partner))

    merges(1 - core)
    for copy in x_copies:
        copy.start()
    merges(core)

    def columns(fs):
        n = fs.shape[0]
        return jnp.transpose(jnp.concatenate([fs, jnp.zeros((128 - n, 128), F32)], axis=0))

    order = [*range(1, chips), 0]
    x_copies[0].wait_recv()
    t0 = jnp.concatenate([tops[core, pl.ds(chip_by(i, 1), 1), :] for i in order], axis=0)
    t1 = jnp.concatenate([tops_in[pl.ds(chip_by(i, 1), 1), :] for i in order], axis=0)
    top = jnp.maximum(t0, t1)
    f0, f1 = jnp.exp2(t0 - top), jnp.exp2(t1 - top)
    l = f0 + f1
    over = top + jnp.log2(l)
    for k in range(chips):
        tops_out[k] = jnp.broadcast_to(over[k:k + 1], (8, 128))
    f = columns(jnp.concatenate([f0 / l, f1 / l], axis=0))

    def t_copy(k, d, s):
        return remote(tops_out.at[k], tops_all.at[s], t_send.at[k], t_recv.at[s], (row, 2 * d + core))

    part_rows = 128 // 2

    def p_copy(n, k, d, s):
        at = pl.ds(n * part_rows, part_rows)
        return remote(merged.at[k, at], parts.at[s, at], p_send.at[n, k], p_recv.at[n, s], (row, 2 * d + core))

    each(1, chips, lambda i: t_copy(i - 1, chip_by(i, 1), chip).start())
    x_copies[1].wait_recv()
    for n in range(2):
        at = slice(n * part_rows, (n + 1) * part_rows)
        for k, i in enumerate(order):
            d = chip_by(i, 1)
            both = (f[at, k:k + 1] * partial[core, d, at].astype(F32)
                    + f[at, chips + k:chips + k + 1] * partial_in[d, at].astype(F32)).astype(BF16)
            if i:
                merged[k, at] = both
                p_copy(n, k, d, chip).start()
            else:
                parts[chip, at] = both
    tops_all[chip] = tops_out[chips - 1]

    def ent_sent(i, c):
        ent_copy((me + i) % peers, me).wait_send()
        return c

    lax.fori_loop(1, peers, ent_sent, 0)

    def q_sent(i, c):
        q_copy((chip + i) % chips, chip).wait_send()
        return c

    lax.fori_loop(1, chips, q_sent, 0)

    def q_relayed(d, c):
        q_relay(d, core).wait_send()
        return c

    lax.fori_loop(0, chips, q_relayed, 0)
    for copy in x_copies:
        copy.wait_send()
    wo_copy.wait()
    wo_t[0] = jnp.transpose(wo[core])
    wo_t[1] = jnp.transpose(wo_in[...])

    each(0, chips - 1, lambda i: t_copy(0, chip_by(i + 1, -1), chip_by(i + 1, -1)).wait_recv())
    top = tops_all[:, 0, :]
    f = jnp.exp2(top - jnp.max(top, axis=0, keepdims=True))
    f = columns(f / jnp.sum(f, axis=0, keepdims=True))
    pair_rows = 2 * own
    cols = half * width // 2

    def at_copy(n, d, s):
        at = attended.at[pl.ds(s * pair_rows, pair_rows), pl.ds(n * cols, cols)]
        return remote(at, at, ag2_send.at[n, d], ag2_recv.at[n, s], (row, 2 * d + core))

    for n in range(2):
        each(1, chips, lambda i: p_copy(n, 0, chip_by(i, -1), chip_by(i, -1)).wait_recv())
        at = slice(n * part_rows, (n + 1) * part_rows)
        acc = jnp.zeros((part_rows, width), F32)
        for s in range(chips):
            acc += f[at, s:s + 1] * parts[s, at].astype(F32)
        acc = acc.astype(BF16)
        for h in range(half // 2):
            attended[pl.ds(chip * pair_rows, pair_rows), n * cols + h * width:n * cols + (h + 1) * width] = (
                acc[h * pair_rows:(h + 1) * pair_rows])
        each(1, chips, lambda i: at_copy(n, chip_by(i, 1), chip).start())

    def merged_sent(i):
        t_copy(i - 1, chip_by(i, 1), chip).wait_send()
        for n in range(2):
            p_copy(n, i - 1, chip_by(i, 1), chip).wait_send()

    each(1, chips, merged_sent)

    out_rows = out_ref.shape[0]

    def z_copy(c, z, s):
        return remote(terms.at[c, pl.ds(z * out_rows, out_rows)], summed.at[c, s], z_send.at[c, z], z_recv.at[c, s],
                      (z, partner[1] if c else me))

    for n in range(2):
        each(1, chips, lambda i: at_copy(n, chip_by(i, -1), chip_by(i, -1)).wait_recv())
    for c in (1, 0):
        terms[c] = jnp.dot(attended[...], wo_t[c], preferred_element_type=F32).astype(BF16)
        for i in (2, 1, 3, 0)[:3 + c]:
            z_copy(c, (row + i) % planes, row).start()
    for n in range(2):
        each(1, chips, lambda i: at_copy(n, chip_by(i, 1), chip).wait_send())

    result = terms[0, pl.ds(row * out_rows, out_rows), :].astype(F32)
    for c in (1, 0):
        for i in range(c ^ 1, planes):
            z = (row + i) % planes
            z_copy(c, z, z).wait_recv()
            result += summed[c, z].astype(F32)
    out_ref[...] = result.astype(BF16)
    for c in (1, 0):
        for i in range(c ^ 1, planes):
            z_copy(c, (row + i) % planes, row).wait_send()


def run(ht, w, dt, up, gain, freq, holder, index, used, tenant, held, k, v, wo, peers, planes):
    rows, wide, width = ht.shape[1], w.shape[1], gain.shape[1]
    own = rows // peers
    cap = 2 * own * holder.shape[1] // peers
    chips = peers // 2
    heads = wide // width
    blocks, toks, _ = k.shape
    slots = peers * cap
    count = -(-(slots // GROUP + blocks * (GROUP - 1) // GROUP) // UNROLL) * UNROLL
    positions = count * GROUP
    wide_a = (wide + 128) // 256 * 128 + 128
    wide_b = wide + 128 - wide_a
    cols = wo.shape[0]
    vm = pltpu.VMEM
    dma = pltpu.SemaphoreType.DMA
    args = (ht, w, dt, up, gain, freq, holder, index, used, tenant, held, k, v, wo)
    return pl.pallas_call(
        kernel,
        out_shape=jax.ShapeDtypeStruct((rows // planes, cols), BF16),
        in_specs=[pl.BlockSpec(memory_space=pltpu.HBM)] * len(args),
        out_specs=pl.BlockSpec(memory_space=pltpu.VMEM),
        scratch_shapes=[vm(a.shape, a.dtype) for a in args[:11]] + [
            pltpu.SMEM(tenant.shape, I32), pltpu.SMEM(held.shape, I32),
            vm(k.shape, BF16), vm(v.shape, BF16), vm((2, cols, wide // 2), BF16), vm((cols, wide // 2), BF16), vm((2, wide // 2, cols), BF16),
            vm((rows, wide + 128), F32), vm((chips, own, wide + 128), F32),
            vm((SIDE, SIDE, own, wide_a), F32), vm((SIDE, SIDE, own, wide_b), F32),
            vm((SIDE, SIDE, own, wide_a), F32), vm((SIDE, SIDE, own, wide_b), F32),
            vm((SIDE, own, wide_a), F32), vm((SIDE, own, wide_b), F32),
            vm((SIDE, own, wide_a), F32), vm((SIDE, own, wide_b), F32),
            vm((own, wide + 128), F32), vm((128 // up.shape[1], up.shape[1], 128), F32), vm((own, heads, width), F32),
            vm((slots, 128), BF16), vm((slots, 128), BF16), vm((8, positions), I32), vm((8, slots), I32),
            pltpu.SMEM((8, positions), I32), pltpu.SMEM((8, slots), I32),
            vm((rows, heads, width), BF16),
            vm((positions, 2, heads // 2, width), F32), vm((positions, 2, heads // 2, width), F32),
            vm((2, chips, 128, width), BF16), vm((2, chips, 128), F32),
            vm((chips, 128, width), BF16), vm((chips, 128), F32),
            vm((chips, 128, width), BF16), vm((chips, 8, 128), F32),
            vm((chips, 128, width), BF16), vm((chips, 8, 128), F32), vm((rows, wide // 2), BF16),
            vm((2, rows, cols), BF16), vm((2, planes, rows // planes, cols), BF16),
            dma((15,)), dma((2 * PIECES,)), dma((2,)), dma((chips,)), dma((chips,)),
            dma((SIDE,)), dma((SIDE,)), dma((SIDE, SIDE)), dma((SIDE, SIDE)),
            dma((SIDE,)), dma((SIDE,)), dma((SIDE,)), dma((SIDE,)),
            dma((peers,)), dma((peers,)), dma((chips,)), dma((chips,)), dma((chips,)), dma((chips,)),
            dma, dma, dma((2,)), dma((2,)),
            dma((2, chips)), dma((2, chips)), dma((chips,)), dma((chips,)),
            dma((2, chips)), dma((2, chips)), dma((2, planes)), dma((2, planes)),
        ],
        compiler_params=pltpu.CompilerParams(
            vmem_limit_bytes=62 * 2**20, collective_id=0, has_side_effects=True),
        name="decode",
    )(*args)


def local(hidden, query_weight, adapter_down_weight, adapter_up_weight, query_norm_gain, paged_key_cache,
          paged_value_cache, output_weight, holder, holder_block_index, block_used_length, tenant, tenant_adapter):
    peers, planes = lax.axis_size("kv"), lax.axis_size("row")
    count, _, rank = adapter_down_weight.shape
    width = query_norm_gain.shape[0]
    blocks, toks, kv_heads, _ = paged_key_cache.shape
    half = width // 2
    freq = (ROPE_BASE ** (-(np.arange(half) * 2.0) / width)).astype(np.float32)
    freq = jnp.asarray(np.concatenate([freq, freq])[None, :])
    down = jnp.transpose(adapter_down_weight, (0, 2, 1)).reshape(count * rank, -1)
    pool = (blocks, toks * kv_heads, width)
    return run(hidden.T, query_weight, down, adapter_up_weight, query_norm_gain[None, :], freq, holder,
               holder_block_index, block_used_length, tenant[None, :], tenant_adapter[None, :],
               paged_key_cache.reshape(pool), paged_value_cache.reshape(pool), output_weight.T, peers, planes)


def solution(mesh):
    return jax.shard_map(
        local,
        mesh=mesh,
        in_specs=(
            P(None, "kv"),
            P("kv", "row"),
            P(None, "kv", None),
            P(None, None, "row"),
            P(),
            P("kv", None, "row", None),
            P("kv", None, "row", None),
            P("row", "kv"),
            P("kv", None),
            P("kv", None),
            P("kv", None),
            P(),
            P(),
        ),
        out_specs=P("row", "kv"),
        check_vma=False,
    )
```

```python
import functools
import math

import jax
import jax.numpy as jnp
import numpy as np
from jax import lax
from jax.experimental import pallas as pl
from jax.experimental.pallas import tpu as pltpu
from jax.sharding import PartitionSpec as P

NEG = -1e30
F32, BF16, I32 = jnp.float32, jnp.bfloat16, jnp.int32
NT = (((1,), (1,)), ((), ()))
TN = (((0,), (0,)), ((), ()))
TT = (((0,), (1,)), ((), ()))
MESH = pl.DeviceIdType.MESH
PIECES = 4
GROUP = 4
UNROLL = 224
SIDE = 4
ADAPTER_SCALE = 0.5
ROPE_BASE = 1000000.0
EPSILON = 1e-06


def iota(shape, dim):
    return lax.broadcasted_iota(I32, shape, dim)


def flat_row(x):
    rows, n = x.shape
    wide = jnp.concatenate([x.astype(F32)] * rows, axis=1)
    keep = lax.div(iota(wide.shape, 1), n) == iota(wide.shape, 0)
    return jnp.sum(jnp.where(keep, wide, 0.0), axis=0, keepdims=True)


def remote(src, dst, send, recv, device):
    return pltpu.make_async_remote_copy(
        src_ref=src, dst_ref=dst, send_sem=send, recv_sem=recv, device_id=device, device_id_type=MESH)


def entries_by_holder(holder, index, used, me, own, peers, cap):
    dest, index, used = flat_row(holder), flat_row(index), flat_row(used)
    count = dest.shape[1]
    to = dest == iota((peers, count), 0).astype(F32)
    earlier = jnp.where(iota((count, count), 0) < iota((count, count), 1), 1.0, 0.0).astype(BF16)
    before = jnp.dot(jnp.where(to, 1.0, 0.0).astype(BF16), earlier, preferred_element_type=F32)
    place = dest * cap + jnp.sum(jnp.where(to, before, 0.0), axis=0, keepdims=True)
    chosen = jnp.where(place == iota((peers * cap, count), 0).astype(F32), 1.0, 0.0).astype(BF16)
    sub = iota((128, count), 0)
    from_row = (me * own + lax.div(iota((1, count), 1), count // own)).astype(F32)
    fields = jnp.where(sub == 0, index, jnp.where(sub == 1, used, jnp.where(sub == 2, from_row, 0.0)))
    return lax.dot_general(chosen, fields.astype(BF16), NT, preferred_element_type=F32).astype(BF16)


def order_entries(ent, blocks, rows, positions, per_group):
    slots = ent.shape[0]
    entf = ent.astype(F32)
    pick = jnp.where(iota((16, 128), 0) == iota((16, 128), 1), 1.0, 0.0).astype(BF16)
    ent_t = lax.dot_general(pick, ent, NT, preferred_element_type=F32)
    blk_r, len_r, row_r = ent_t[0:1], ent_t[1:2], ent_t[2:3]
    valid_c = entf[:, 1:2] > 0
    key_c = jnp.where(valid_c, entf[:, 0:1], 999.0)
    key_r = jnp.where(len_r > 0, blk_r, 999.0)
    earlier = iota((slots, slots), 1) < iota((slots, slots), 0)
    within = jnp.sum(jnp.where((key_c == key_r) & earlier, 1.0, 0.0), axis=1, keepdims=True)
    block_of = iota((blocks, slots), 0).astype(F32) == key_r
    count = jnp.sum(jnp.where(block_of, 1.0, 0.0), axis=1, keepdims=True)
    chunks = jnp.floor((count + (GROUP - 1)) * (1.0 / GROUP))
    below = jnp.where(iota((blocks, blocks), 1) < iota((blocks, blocks), 0), 1.0, 0.0).astype(BF16)
    first = jnp.dot(below, jnp.broadcast_to(chunks, (blocks, 128)).astype(BF16), preferred_element_type=F32)
    own_block = jnp.where(key_c == iota((slots, blocks), 1).astype(F32), 1.0, 0.0).astype(BF16)
    first_c = jnp.dot(own_block, first.astype(BF16), preferred_element_type=F32)[:, 0:1]
    major = jnp.floor(within * (1.0 / GROUP))
    chunk_c, seat_c = first_c + major, within - major * GROUP
    place = jnp.where(valid_c, chunk_c * GROUP + seat_c, -1.0)
    sub = iota((16, slots), 0)
    fields = jnp.where(sub == 0, blk_r, jnp.where(sub == 1, len_r, jnp.where(sub == 2, row_r, 0.0))).astype(BF16)
    chosen = jnp.where(place == iota((slots, positions), 1).astype(F32), 1.0, 0.0).astype(BF16)
    table = jnp.dot(fields, chosen, preferred_element_type=F32)[0:8]
    sub = iota(table.shape, 0)
    table = table.astype(I32)
    table = jnp.clip(table, 0, jnp.where(sub == 0, blocks - 1, jnp.where(sub == 1, 1 << 16, rows - 1)))
    lane = iota((slots, 128), 1)
    seats = jnp.where(lane == 0, chunk_c, jnp.where(lane == 1, seat_c, 0.0)).astype(BF16)
    seats = lax.dot_general(pick, seats, NT, preferred_element_type=F32)
    where_r = jnp.where(len_r > 0, seats[0:1] * GROUP + seats[1:2], 0.0)
    local_r = row_r - (lax.div(iota((1, slots), 1), per_group) * 16).astype(F32)
    local_r = jnp.where(len_r > 0, local_r, -1.0)
    by_slot = jnp.clip(jnp.where(iota((8, slots), 0) == 0, where_r, local_r).astype(I32), -1, positions - 1)
    by_slot = jnp.where(iota((8, slots), 0) == 0, jnp.maximum(by_slot, 0), by_slot)
    return table, by_slot


def kernel(ht_h, w_h, dt_h, up_h, gain_h, freq_h, holder_h, index_h, used_h, tenant_h, held_h, k_h, v_h, wo_h,
           out_ref,
           ht, w, dt, up, gain, freq, holder, index, used, tenant, held, tenant_s, held_s, kbuf, vbuf, wo, wo_in, wo_t,
           part, pair, mine_a, mine_b, land_a, land_b, sum_a, sum_b, end_a, end_b, total, low_t, turned,
           ent_send, ent, tab_v, slot_v, tab, slot_s, q, o_st, e_st,
           partial, tops, partial_in, tops_in, merged, tops_out, parts, tops_all, attended, terms, summed,
           in_sem, kv_sem, tab_sem, pair_send, pair_recv, a_send, a_recv, b_send, b_recv, a2_send, a2_recv,
           b2_send, b2_recv, en_send, en_recv, ag_send, ag_recv, fw_send, fw_recv,
           wo_send, wo_recv, x_send, x_recv, p_send, p_recv, t_send, t_recv, ag2_send, ag2_recv, z_send, z_recv):
    row, me = lax.axis_index("row"), lax.axis_index("kv")
    peers, planes = lax.axis_size("kv"), lax.axis_size("row")
    chips = peers // 2
    chip, core = me // 2, me % 2
    x, y = chip // SIDE, chip % SIDE
    partner = (row, 2 * chip + 1 - core)
    wide = w.shape[1]
    rows, heads, width = q.shape
    own = rows // peers
    cap = ent.shape[0] // peers
    blocks, toks, _ = kbuf.shape
    wide_a = mine_a.shape[3]
    barrier = pltpu.get_barrier_semaphore()

    def greet(i, c):
        pl.semaphore_signal(barrier, inc=1, device_id=(row, (me + i) % peers), device_id_type=MESH)
        return c

    def greet_plane(i, c):
        pl.semaphore_signal(barrier, inc=1, device_id=((row + i) % planes, me), device_id_type=MESH)
        pl.semaphore_signal(barrier, inc=1, device_id=((row + i) % planes, partner[1]), device_id_type=MESH)
        return c

    loads = [pltpu.make_async_copy(src, dst, in_sem.at[i]) for i, (src, dst) in enumerate((
        (ht_h, ht), (w_h, w), (holder_h, holder), (index_h, index), (used_h, used), (tenant_h, tenant),
        (held_h, held), (dt_h, dt), (tenant_h, tenant_s), (held_h, held_s), (gain_h, gain), (freq_h, freq),
        (up_h, up), (wo_h.at[:, :wide // 2], wo.at[0]), (wo_h.at[:, wide // 2:], wo.at[1])))]
    for copy in loads[:8]:
        copy.start()
    lax.fori_loop(1, peers, greet, 0)
    lax.fori_loop(1, planes, greet_plane, 0)
    step = blocks // PIECES
    pool = []
    for i in range(PIECES):
        at = pl.ds(i * step, step)
        pool += [pltpu.make_async_copy(k_h.at[at], kbuf.at[at], kv_sem.at[2 * i]),
                 pltpu.make_async_copy(v_h.at[at], vbuf.at[at], kv_sem.at[2 * i + 1])]
    for copy in loads[:8]:
        copy.wait()
    for copy in loads[8:] + pool:
        copy.start()

    part[:, :wide] = lax.dot_general(ht[...], w[...], TN, preferred_element_type=F32)
    low = lax.dot_general(ht[...], dt[...], TT, preferred_element_type=F32)
    rank = up.shape[1]
    is_tenant = jnp.where(tenant[...] == iota((held.shape[1], rows), 0), 1.0, 0.0).astype(BF16)
    held_b = jnp.broadcast_to(held[...].astype(F32), (16, held.shape[1])).astype(BF16)
    adapter = jnp.dot(held_b, is_tenant, preferred_element_type=F32)[0:8]
    adapter = jnp.transpose(adapter)[:, 0:1].astype(I32)
    low = jnp.where(lax.div(iota(low.shape, 1), rank) == adapter, low, 0.0)
    part[:, wide:] = sum(low[:, 128 * i: 128 * (i + 1)] for i in range(low.shape[1] // 128))

    pl.semaphore_wait(barrier, peers - 1 + 2 * (planes - 1))

    def pair_copy(d):
        return remote(part.at[pl.ds((2 * d + 1 - core) * own, own)], pair.at[d],
                      pair_send.at[d], pair_recv.at[d], partner)

    def chip_at(ox, oy):
        return (x + ox) % SIDE, (y + oy) % SIDE

    hops = (2, 1, 3, 0)
    for ox in hops:
        for oy in hops:
            dx, dy = chip_at(ox, oy)
            pair_copy(dx * SIDE + dy).start()

    ent_send[...] = entries_by_holder(holder[...], index[...], used[...], me, own, peers, cap)

    def a_copy(t, s):
        return remote(mine_a.at[t], land_a.at[s], a_send.at[t], a_recv.at[s], (row, 2 * (t * SIDE + y) + core))

    def b_copy(t, i, s):
        return remote(mine_b.at[t, i], land_b.at[s, i], b_send.at[t, i], b_recv.at[s, i],
                      (row, 2 * (x * SIDE + t) + core))

    for ox in hops:
        for oy in hops:
            dx, dy = chip_at(ox, oy)
            d = dx * SIDE + dy
            pair_copy(d).wait_recv()
            both = part[pl.ds((2 * d + core) * own, own), :] + pair[d]
            mine_a[dx, dy] = both[:, :wide_a]
            mine_b[dy, dx] = both[:, wide_a:]
            if oy:
                b_copy(dy, dx, y).start()
        if ox:
            a_copy(dx, x).start()

    def ent_copy(t, slot):
        return remote(ent_send.at[pl.ds(t * cap, cap)], ent.at[pl.ds(slot * cap, cap)],
                      en_send.at[t], en_recv.at[slot], (row, t))

    def ent_start(i, c):
        ent_copy((me + i) % peers, me).start()
        return c

    lax.fori_loop(1, peers, ent_start, 0)
    at = pl.ds(me * cap, cap)
    ent[at, :] = ent_send[at, :]
    for copy in loads[8:]:
        copy.wait()
    angles = (jnp.sum(used[...], axis=1, keepdims=True) - 1).astype(F32) * freq[...]
    cosine, sine = jnp.cos(angles), jnp.sin(angles)
    sine = jnp.where(iota(sine.shape, 1) < width // 2, -sine, sine)

    wo_copy = remote(wo.at[1 - core], wo_in, wo_send, wo_recv, partner)
    wo_copy.start()

    for copy in pool:
        copy.wait()

    def turn_keys(b, c):
        kbuf[b] = jnp.transpose(kbuf[b].reshape(toks // 2, 2 * width))
        return c

    lax.fori_loop(0, blocks, turn_keys, 0, unroll=4)

    def a2_copy(t, s):
        return remote(sum_a.at[t], end_a.at[s], a2_send.at[t], a2_recv.at[s], (row, 2 * (x * SIDE + t) + core))

    def b2_copy(t, s):
        return remote(sum_b.at[t], end_b.at[s], b2_send.at[t], b2_recv.at[s], (row, 2 * (t * SIDE + y) + core))

    steps = (1, 3, 2)
    for o in steps:
        a_copy((x + SIDE - o) % SIDE, (x + SIDE - o) % SIDE).wait_recv()
    sum_a[...] = mine_a[x] + land_a[(x + 1) % SIDE] + land_a[(x + 2) % SIDE] + land_a[(x + 3) % SIDE]
    for o in (2, 1, 3):
        a2_copy((y + o) % SIDE, y).start()
    for o in steps:
        for i in range(SIDE):
            b_copy((y + SIDE - o) % SIDE, i, (y + SIDE - o) % SIDE).wait_recv()
    sum_b[...] = mine_b[y] + land_b[(y + 1) % SIDE] + land_b[(y + 2) % SIDE] + land_b[(y + 3) % SIDE]
    for o in (2, 1, 3):
        b2_copy((x + o) % SIDE, x).start()

    for o in steps:
        a2_copy((y + SIDE - o) % SIDE, (y + SIDE - o) % SIDE).wait_recv()
    total[:, :wide_a] = sum_a[y] + end_a[(y + 1) % SIDE] + end_a[(y + 2) % SIDE] + end_a[(y + 3) % SIDE]
    for o in steps:
        b2_copy((x + SIDE - o) % SIDE, (x + SIDE - o) % SIDE).wait_recv()
    total[:, wide_a:] = sum_b[x] + end_b[(x + 1) % SIDE] + end_b[(x + 2) % SIDE] + end_b[(x + 3) % SIDE]

    low_t[...] = jnp.transpose(
        jnp.concatenate([total[:, wide:], jnp.zeros((128 - own, 128), F32)], axis=0)).reshape(low_t.shape)
    for r in range(own):
        adapter = held_s[0, tenant_s[0, me * own + r]]
        column = low_t[lax.rem(adapter, 128 // rank)][:, r:r + 1]
        more = jnp.sum(column * up[adapter], axis=0, keepdims=True)
        total[r:r + 1, :wide] += ADAPTER_SCALE * more
    gain_r = gain[...]
    for h in range(heads):
        t = total[:, h * width:(h + 1) * width]
        t = t * lax.rsqrt(jnp.mean(t * t, axis=1, keepdims=True) + EPSILON) * gain_r
        turned[:, h, :] = t * cosine + pltpu.roll(t, width // 2, 1) * sine
    q[pl.ds(me * own, own)] = turned[...].astype(BF16)

    def chip_by(i, sign):
        dx, dy = i // SIDE, i % SIDE
        return ((x + sign * dx + SIDE) % SIDE) * SIDE + (y + sign * dy + SIDE) % SIDE

    far = sorted(range(1, chips), key=lambda i: -(min(i // SIDE, SIDE - i // SIDE) + min(i % SIDE, SIDE - i % SIDE)))

    def turn(i):
        return lax.rem(chip + i, chips)

    def each(first, last, do):
        def step(i, c):
            do(i)
            return c

        lax.fori_loop(first, last, step, 0)

    def q_copy(d, s):
        at = pl.ds((2 * s + core) * own, own)
        return remote(q.at[at], q.at[at], ag_send.at[d], ag_recv.at[s], (row, 2 * d + core))

    def q_relay(s, c):
        at = pl.ds((2 * s + c) * own, own)
        return remote(q.at[at], q.at[at], fw_send.at[s], fw_recv.at[s], partner)

    for i in far:
        q_copy(chip_by(i, 1), chip).start()
    q_relay(chip, core).start()

    def turn_values(b, c):
        both = vbuf[b].reshape(toks // 2, 2 * width)
        vbuf[b, :toks // 2] = both[:, :width]
        vbuf[b, toks // 2:] = both[:, width:]
        return c

    lax.fori_loop(0, blocks, turn_values, 0, unroll=4)

    def ent_wait(i, c):
        t = (me + peers - i) % peers
        ent_copy(t, t).wait_recv()
        return c

    lax.fori_loop(1, peers, ent_wait, 0)
    table, by_slot = order_entries(ent[...], blocks, rows, tab.shape[1], 2 * cap)
    tab_v[...] = table
    slot_v[...] = by_slot
    tables = (pltpu.make_async_copy(tab_v, tab, tab_sem.at[0]), pltpu.make_async_copy(slot_v, slot_s, tab_sem.at[1]))
    for copy in tables:
        copy.start()

    def pair_sent(d, c):
        pair_copy(d).wait_send()
        return c

    lax.fori_loop(0, chips, pair_sent, 0)
    for o in (1, 2, 3):
        a_copy((x + o) % SIDE, x).wait_send()
        for i in range(SIDE):
            b_copy((y + o) % SIDE, i, y).wait_send()
        a2_copy((y + o) % SIDE, y).wait_send()
        b2_copy((x + o) % SIDE, x).wait_send()

    for i in far:
        s = chip_by(i, -1)
        q_copy(s, s).wait_recv()
        q_relay(s, core).start()


    def q_landed(d, c):
        q_relay(d, 1 - core).wait_recv()
        return c

    lax.fori_loop(0, chips, q_landed, 0)
    for copy in tables:
        copy.wait()

    coef = math.log2(math.e) / math.sqrt(width)
    half = heads // 2
    col = iota((heads, toks // 2), 1)
    upper = iota((heads, width), 0) < half
    none = jnp.zeros((heads, width), BF16)

    def chunk(c):
        base = c * GROUP
        b = tab[0, base]
        qs = [q[tab[2, base + g]] for g in range(GROUP)]
        qs = jnp.concatenate([jnp.concatenate(
            [jnp.where(upper, one, none), jnp.where(upper, none, one)], axis=1) for one in qs], axis=0)
        s = jnp.dot(qs, kbuf[b], preferred_element_type=F32)
        s = jnp.concatenate(
            [jnp.where(col < tab[1, base + g], s[heads * g: heads * (g + 1)], NEG) for g in range(GROUP)], axis=0)
        m = jnp.max(s, axis=1, keepdims=True)
        wt = jnp.exp2((s - m) * coef)
        l = jnp.sum(wt, axis=1, keepdims=True)
        vs = jnp.concatenate([vbuf[b, :toks // 2], vbuf[b, toks // 2:]], axis=1)
        o = jnp.dot(wt.astype(BF16), vs, preferred_element_type=F32).reshape(GROUP, 2, half, 2 * width)
        o = jnp.concatenate([o[:, 0:1, :, :width], o[:, 1:2, :, width:]], axis=1).reshape(GROUP * heads, width) / l
        e = jnp.broadcast_to(m * coef + jnp.log2(l), o.shape)
        return o.reshape(GROUP, 2, half, width), e.reshape(GROUP, 2, half, width)

    def chunks(i, c):
        done = [chunk(i * UNROLL + u) for u in range(UNROLL)]
        for u in range(UNROLL):
            o, e = done[u]
            at = pl.ds((i * UNROLL + u) * GROUP, GROUP)
            o_st[at] = o
            e_st[at] = e
        return c

    lax.fori_loop(0, tab.shape[1] // (GROUP * UNROLL), chunks, 0)

    lane = iota((half, 128), 1)
    same_head = lax.div(lane, 128 // half) == iota((half, 128), 0)
    lane_row = jnp.where(same_head, lane & (128 // half - 1), -2)
    slots = 2 * cap

    def merge(d, hv):
        tops_of, outs = [], []
        for p in range(slots):
            at = slot_s[0, d * slots + p]
            tops_of.append(jnp.where(lane_row == slot_s[1, d * slots + p], e_st[at, hv], NEG))
            outs.append(o_st[at, hv])
        es = jnp.concatenate(tops_of, axis=0)
        top = jnp.max(es, axis=0, keepdims=True)
        f = jnp.exp2(es - top)
        l = jnp.sum(f, axis=0, keepdims=True)
        f = (f * (1.0 / l)).astype(BF16)
        os = jnp.concatenate(outs, axis=0).astype(BF16)
        return lax.dot_general(f, os, TN, preferred_element_type=F32).astype(BF16), top + jnp.log2(l)

    def merges(hv):
        done = [merge(d, hv) for d in range(chips)]
        for d in range(chips):
            partial[hv, d] = done[d][0]
        tops[hv] = jnp.concatenate([one[1] for one in done], axis=0)

    x_copies = (remote(tops.at[1 - core], tops_in, x_send.at[0], x_recv.at[0], partner),
                remote(partial.at[1 - core], partial_in, x_send.at[1], x_recv.at[1], partner))

    merges(1 - core)
    for copy in x_copies:
        copy.start()
    merges(core)

    def columns(fs):
        n = fs.shape[0]
        return jnp.transpose(jnp.concatenate([fs, jnp.zeros((128 - n, 128), F32)], axis=0))

    order = far + [0]
    x_copies[0].wait_recv()
    t0 = jnp.concatenate([tops[core, pl.ds(chip_by(i, 1), 1), :] for i in order], axis=0)
    t1 = jnp.concatenate([tops_in[pl.ds(chip_by(i, 1), 1), :] for i in order], axis=0)
    top = jnp.maximum(t0, t1)
    f0, f1 = jnp.exp2(t0 - top), jnp.exp2(t1 - top)
    l = f0 + f1
    over = top + jnp.log2(l)
    for k in range(chips):
        tops_out[k] = jnp.broadcast_to(over[k:k + 1], (8, 128))
    f = columns(jnp.concatenate([f0 / l, f1 / l], axis=0))

    def t_copy(k, d, s):
        return remote(tops_out.at[k], tops_all.at[s], t_send.at[k], t_recv.at[s], (row, 2 * d + core))

    part_rows = 128 // 2

    def p_copy(n, k, d, s):
        at = pl.ds(n * part_rows, part_rows)
        return remote(merged.at[k, at], parts.at[s, at], p_send.at[n, k], p_recv.at[n, s], (row, 2 * d + core))

    for k, i in enumerate(far):
        t_copy(k, chip_by(i, 1), chip).start()
    x_copies[1].wait_recv()
    for n in range(2):
        at = slice(n * part_rows, (n + 1) * part_rows)
        for k, i in enumerate(order):
            d = chip_by(i, 1)
            both = (f[at, k:k + 1] * partial[core, d, at].astype(F32)
                    + f[at, chips + k:chips + k + 1] * partial_in[d, at].astype(F32)).astype(BF16)
            if i:
                merged[k, at] = both
                p_copy(n, k, d, chip).start()
            else:
                parts[chip, at] = both
    tops_all[chip] = tops_out[chips - 1]

    def ent_sent(i, c):
        ent_copy((me + i) % peers, me).wait_send()
        return c

    lax.fori_loop(1, peers, ent_sent, 0)

    def q_sent(i, c):
        q_copy((chip + i) % chips, chip).wait_send()
        return c

    lax.fori_loop(1, chips, q_sent, 0)

    def q_relayed(d, c):
        q_relay(d, core).wait_send()
        return c

    lax.fori_loop(0, chips, q_relayed, 0)
    for copy in x_copies:
        copy.wait_send()
    wo_copy.wait()
    wo_t[0] = jnp.transpose(wo[core])
    wo_t[1] = jnp.transpose(wo_in[...])

    each(1, chips, lambda i: t_copy(0, turn(i), turn(i)).wait_recv())
    top = tops_all[:, 0, :]
    f = jnp.exp2(top - jnp.max(top, axis=0, keepdims=True))
    f = columns(f / jnp.sum(f, axis=0, keepdims=True))
    pair_rows = 2 * own
    cols = half * width // 2

    def at_copy(n, d, s):
        at = attended.at[pl.ds(s * pair_rows, pair_rows), pl.ds(n * cols, cols)]
        return remote(at, at, ag2_send.at[n, d], ag2_recv.at[n, s], (row, 2 * d + core))

    for n in range(2):
        each(1, chips, lambda i: p_copy(n, 0, turn(i), turn(i)).wait_recv())
        at = slice(n * part_rows, (n + 1) * part_rows)
        acc = jnp.zeros((part_rows, width), F32)
        for s in range(chips):
            acc += f[at, s:s + 1] * parts[s, at].astype(F32)
        acc = acc.astype(BF16)
        for h in range(half // 2):
            attended[pl.ds(chip * pair_rows, pair_rows), n * cols + h * width:n * cols + (h + 1) * width] = (
                acc[h * pair_rows:(h + 1) * pair_rows])
        for i in far:
            at_copy(n, chip_by(i, 1), chip).start()

    def merged_sent(i):
        t_copy(i - 1, turn(i), chip).wait_send()
        for n in range(2):
            p_copy(n, i - 1, turn(i), chip).wait_send()

    each(1, chips, merged_sent)

    out_rows = out_ref.shape[0]

    def z_copy(c, z, s):
        return remote(terms.at[c, pl.ds(z * out_rows, out_rows)], summed.at[c, s], z_send.at[c, z], z_recv.at[c, s],
                      (z, partner[1] if c else me))

    for n in range(2):
        each(1, chips, lambda i: at_copy(n, turn(i), turn(i)).wait_recv())
    for c in (1, 0):
        terms[c] = jnp.dot(attended[...], wo_t[c], preferred_element_type=F32).astype(BF16)
        for i in (2, 1, 3, 0)[:3 + c]:
            z_copy(c, (row + i) % planes, row).start()
    for n in range(2):
        each(1, chips, lambda i: at_copy(n, turn(i), chip).wait_send())

    result = terms[0, pl.ds(row * out_rows, out_rows), :].astype(F32)
    for c in (1, 0):
        for i in range(c ^ 1, planes):
            z = (row + i) % planes
            z_copy(c, z, z).wait_recv()
            result += summed[c, z].astype(F32)
    out_ref[...] = result.astype(BF16)
    for c in (1, 0):
        for i in range(c ^ 1, planes):
            z_copy(c, (row + i) % planes, row).wait_send()


def run(ht, w, dt, up, gain, freq, holder, index, used, tenant, held, k, v, wo, peers, planes):
    rows, wide, width = ht.shape[1], w.shape[1], gain.shape[1]
    own = rows // peers
    cap = 2 * own * holder.shape[1] // peers
    chips = peers // 2
    heads = wide // width
    blocks, toks, _ = k.shape
    slots = peers * cap
    count = -(-(slots // GROUP + blocks * (GROUP - 1) // GROUP) // UNROLL) * UNROLL
    positions = count * GROUP
    wide_a = (wide + 128) // 256 * 128 + 128
    wide_b = wide + 128 - wide_a
    cols = wo.shape[0]
    vm = pltpu.VMEM
    dma = pltpu.SemaphoreType.DMA
    args = (ht, w, dt, up, gain, freq, holder, index, used, tenant, held, k, v, wo)
    return pl.pallas_call(
        kernel,
        out_shape=jax.ShapeDtypeStruct((rows // planes, cols), BF16),
        in_specs=[pl.BlockSpec(memory_space=pltpu.HBM)] * len(args),
        out_specs=pl.BlockSpec(memory_space=pltpu.VMEM),
        scratch_shapes=[vm(a.shape, a.dtype) for a in args[:11]] + [
            pltpu.SMEM(tenant.shape, I32), pltpu.SMEM(held.shape, I32),
            vm(k.shape, BF16), vm(v.shape, BF16), vm((2, cols, wide // 2), BF16), vm((cols, wide // 2), BF16), vm((2, wide // 2, cols), BF16),
            vm((rows, wide + 128), F32), vm((chips, own, wide + 128), F32),
            vm((SIDE, SIDE, own, wide_a), F32), vm((SIDE, SIDE, own, wide_b), F32),
            vm((SIDE, SIDE, own, wide_a), F32), vm((SIDE, SIDE, own, wide_b), F32),
            vm((SIDE, own, wide_a), F32), vm((SIDE, own, wide_b), F32),
            vm((SIDE, own, wide_a), F32), vm((SIDE, own, wide_b), F32),
            vm((own, wide + 128), F32), vm((128 // up.shape[1], up.shape[1], 128), F32), vm((own, heads, width), F32),
            vm((slots, 128), BF16), vm((slots, 128), BF16), vm((8, positions), I32), vm((8, slots), I32),
            pltpu.SMEM((8, positions), I32), pltpu.SMEM((8, slots), I32),
            vm((rows, heads, width), BF16),
            vm((positions, 2, heads // 2, width), F32), vm((positions, 2, heads // 2, width), F32),
            vm((2, chips, 128, width), BF16), vm((2, chips, 128), F32),
            vm((chips, 128, width), BF16), vm((chips, 128), F32),
            vm((chips, 128, width), BF16), vm((chips, 8, 128), F32),
            vm((chips, 128, width), BF16), vm((chips, 8, 128), F32), vm((rows, wide // 2), BF16),
            vm((2, rows, cols), BF16), vm((2, planes, rows // planes, cols), BF16),
            dma((15,)), dma((2 * PIECES,)), dma((2,)), dma((chips,)), dma((chips,)),
            dma((SIDE,)), dma((SIDE,)), dma((SIDE, SIDE)), dma((SIDE, SIDE)),
            dma((SIDE,)), dma((SIDE,)), dma((SIDE,)), dma((SIDE,)),
            dma((peers,)), dma((peers,)), dma((chips,)), dma((chips,)), dma((chips,)), dma((chips,)),
            dma, dma, dma((2,)), dma((2,)),
            dma((2, chips)), dma((2, chips)), dma((chips,)), dma((chips,)),
            dma((2, chips)), dma((2, chips)), dma((2, planes)), dma((2, planes)),
        ],
        compiler_params=pltpu.CompilerParams(
            vmem_limit_bytes=62 * 2**20, collective_id=0, has_side_effects=True),
        name="decode",
    )(*args)


def local(hidden, query_weight, adapter_down_weight, adapter_up_weight, query_norm_gain, paged_key_cache,
          paged_value_cache, output_weight, holder, holder_block_index, block_used_length, tenant, tenant_adapter):
    peers, planes = lax.axis_size("kv"), lax.axis_size("row")
    count, _, rank = adapter_down_weight.shape
    width = query_norm_gain.shape[0]
    blocks, toks, kv_heads, _ = paged_key_cache.shape
    half = width // 2
    freq = (ROPE_BASE ** (-(np.arange(half) * 2.0) / width)).astype(np.float32)
    freq = jnp.asarray(np.concatenate([freq, freq])[None, :])
    down = jnp.transpose(adapter_down_weight, (0, 2, 1)).reshape(count * rank, -1)
    pool = (blocks, toks * kv_heads, width)
    return run(hidden.T, query_weight, down, adapter_up_weight, query_norm_gain[None, :], freq, holder,
               holder_block_index, block_used_length, tenant[None, :], tenant_adapter[None, :],
               paged_key_cache.reshape(pool), paged_value_cache.reshape(pool), output_weight.T, peers, planes)


def solution(mesh):
    return jax.shard_map(
        local,
        mesh=mesh,
        in_specs=(
            P(None, "kv"),
            P("kv", "row"),
            P(None, "kv", None),
            P(None, None, "row"),
            P(),
            P("kv", None, "row", None),
            P("kv", None, "row", None),
            P("row", "kv"),
            P("kv", None),
            P("kv", None),
            P("kv", None),
            P(),
            P(),
        ),
        out_specs=P("row", "kv"),
        check_vma=False,
    )
```
